128 devices in a mesh: seq: 2 (over y_hi), dp: 64 (over y_lo, z, x, core).
Axes of the slice: x: 4, y: 4 (y_hi: 2, y_lo: 2; y = y_hi * 2 + y_lo), z: 4, core: 2. Of those that a mesh axis runs over, the one named last changes fastest.
Arguments:
- tokens: bfloat16 [65536, 768], P(('seq', 'dp')), may hold values from -6 to 6
- input_weight: bfloat16 [768, 2304], replicated, may hold values from -0.21875 to 0.21875
- query_bias: float32 [768], replicated, may hold values from -3 to 3
- value_bias: float32 [768], replicated, may hold values from -1.2 to 1.2
- out_weight: bfloat16 [768, 768], replicated, may hold values from -1.75 to 1.75
- out_bias: float32 [768], replicated, may hold values from -2 to 2
- first_gain: float32 [768], replicated, may hold values from 0.5 to 1.5
- first_shift: float32 [768], replicated, may hold values from -2 to 2
- second_gain: float32 [768], replicated, may hold values from 0.5 to 1.5
- second_shift: float32 [768], replicated, may hold values from -2 to 2
- up_weight: bfloat16 [768, 3072], replicated, may hold values from -0.21875 to 0.21875
- up_bias: float32 [3072], replicated, may hold values from -2 to 2
- down_weight: bfloat16 [3072, 768], replicated, may hold values from -0.109375 to 0.109375
- down_bias: float32 [768], replicated, may hold values from -2 to 2
- cotangent: bfloat16 [65536, 768], P(('seq', 'dp')), may hold values from -6 to 6
- row_counts: int32 [64, 2], P('dp'), may hold values from 128 to 512, as said below
- image_lengths: int32 [64, 4], P('dp'), may hold values from 1 to 1021, as said below
Outputs:
- layer_out: bfloat16 [65536, 768], P(('seq', 'dp'))
- grad_tokens: bfloat16 [65536, 768], P(('seq', 'dp'))
- grad_input_weight: float32 [768, 2304], P('dp')
- grad_query_bias: float32 [768], P('dp')
- grad_value_bias: float32 [768], P('dp')
- grad_out_weight: float32 [768, 768], P('dp')
- grad_out_bias: float32 [768], P('dp')
- grad_first_gain: float32 [768], P('dp')
- grad_first_shift: float32 [768], P('dp')
- grad_second_gain: float32 [768], P('dp')
- grad_second_shift: float32 [768], P('dp')
- grad_up_weight: float32 [768, 3072], P('dp')
- grad_up_bias: float32 [3072], P('dp')
- grad_down_weight: float32 [3072, 768], P('dp')
- grad_down_bias: float32 [768], P('dp')
The draws below stay inside these ranges and needn't reach their ends.
Inputs may be any that keep to these rules, and one draw needn't show every extreme that they name: row_counts[n, s] is the number of used rows of part s of sequence n; in every sequence one of the two counts is exactly 512. `image_lengths`: the 4 lengths of a sequence sum to its two row counts together; the third image holds the last used row of part 0 and the first row of part 1.
All inputs are finite; a program needn't handle non-finite values.
Results may differ from the reference program's by a relative error of at most 0.015.
Values may be sent and summed in bfloat16 or wider, within the bound.
A program may use at most 256 MiB of HBM per device.

```python
import math
import jax
import jax.numpy as jnp
from jax import lax

D = 768
HEADS = 12
HD = 64
FF = 3072
CAP = 512
IMAGES = 4
SEQUENCES = 64
TOKENS = 65536


def packing(key):
    count_key, cut_key = jax.random.split(key)
    pick_key = jax.random.fold_in(key, 17)
    count_keys = jax.random.split(count_key, 2)
    chosen = jax.random.randint(pick_key, (), 0, SEQUENCES)
    seq_index = jnp.arange(SEQUENCES, dtype=jnp.int32)
    is_long = seq_index == chosen
    is_short = seq_index == (chosen + 1) % SEQUENCES
    full_side = jax.random.randint(count_keys[0], (SEQUENCES,), 0, 2)
    other_count = jax.random.randint(count_keys[1], (SEQUENCES,), CAP // 4, CAP + 1)
    other_count = jnp.where(is_short, CAP // 4, other_count)
    other_count = jnp.where(is_long, CAP, other_count)
    first_count = jnp.where(full_side == 0, CAP, other_count)
    second_count = jnp.where(full_side == 0, other_count, CAP)
    counts = jnp.stack([first_count, second_count], axis=1).astype(jnp.int32)
    total_rows = first_count + second_count
    cut_keys = jax.random.split(cut_key, 3)
    half_first = first_count // 2
    cut_one = jax.random.randint(cut_keys[0], (SEQUENCES,), 1, half_first + 1)
    cut_two = jax.random.randint(cut_keys[1], (SEQUENCES,), half_first + 1, first_count)
    cut_three = jax.random.randint(cut_keys[2], (SEQUENCES,), first_count + 1, total_rows)
    lengths = jnp.stack([cut_one, cut_two - cut_one, cut_three - cut_two, total_rows - cut_three], axis=1).astype(jnp.int32)
    widest = jnp.array([1, 1, 2 * CAP - 3, 1], dtype=jnp.int32)
    lengths = jnp.where(is_long[:, None], widest[None, :], lengths)
    return (counts, lengths.astype(jnp.int32))


def draw_row_counts(key, part):
    counts, lengths = packing(key)
    return counts


def draw_image_lengths(key, part):
    counts, lengths = packing(key)
    return lengths


def levels(key, shape, shards, smallest, high):
    loudness, own = 1.0, jax.random.fold_in(key, 6)
    for axis_at, shards_of in shards:
        steps = jnp.exp(jax.random.uniform(jax.random.fold_in(own, axis_at), (shards_of,), jnp.float32, smallest / len(shards), high / len(shards)))
        loudness = loudness * jnp.repeat(steps, shape[axis_at] // shards_of).reshape([-1 if axis == axis_at else 1 for axis in range(len(shape))])
    return loudness


def gaussian(rng, shape, deviation, limit, pieces=(), kind=jnp.bfloat16):
    loudness = levels(rng, shape, pieces, -0.22, 0.18) if pieces else 1.0
    entries = jax.random.normal(rng, shape, jnp.float32) * deviation * loudness
    return jnp.minimum(jnp.maximum(entries, -limit), limit).astype(kind)


def setup_inputs(seed: int = 0) -> dict:
    key_list = jax.random.split(jax.random.key(seed), 18)
    tokens = gaussian(key_list[0], (TOKENS, D), 1.0, 6.0, ((0, 128),))
    input_weight = gaussian(key_list[1], (D, 3 * D), D ** -0.5, 0.21875)
    query_bias = gaussian(key_list[2], (D,), 0.5, 3.0, (), jnp.float32)
    value_bias = gaussian(key_list[3], (D,), 0.2, 1.2, (), jnp.float32)
    out_weight = gaussian(key_list[4], (D, D), (D // 64) ** -0.5, 1.75)
    out_bias = gaussian(key_list[5], (D,), 0.3, 2.0, (), jnp.float32)
    first_gain = jnp.clip(1.0 + 0.1 * jax.random.normal(key_list[6], (D,), jnp.float32), 0.5, 1.5)
    first_shift = gaussian(key_list[7], (D,), 0.3, 2.0, (), jnp.float32)
    second_gain = jnp.clip(1.0 + 0.1 * jax.random.normal(key_list[8], (D,), jnp.float32), 0.5, 1.5)
    second_shift = gaussian(key_list[9], (D,), 0.3, 2.0, (), jnp.float32)
    up_weight = gaussian(key_list[10], (D, FF), D ** -0.5, 0.21875)
    up_bias = gaussian(key_list[11], (FF,), 0.3, 2.0, (), jnp.float32)
    down_weight = gaussian(key_list[12], (FF, D), FF ** -0.5, 0.109375)
    down_bias = gaussian(key_list[13], (D,), 0.3, 2.0, (), jnp.float32)
    cotangent = gaussian(key_list[14], (TOKENS, D), 1.0, 6.0, ((0, 128),))
    row_counts = draw_row_counts(jax.random.fold_in(key_list[17], 71), 0)
    image_lengths = draw_image_lengths(jax.random.fold_in(key_list[17], 71), 0)
    return {"tokens": tokens, "input_weight": input_weight, "query_bias": query_bias, "value_bias": value_bias, "out_weight": out_weight, "out_bias": out_bias, "first_gain": first_gain, "first_shift": first_shift, "second_gain": second_gain, "second_shift": second_shift, "up_weight": up_weight, "up_bias": up_bias, "down_weight": down_weight, "down_bias": down_bias, "cotangent": cotangent, "row_counts": row_counts, "image_lengths": image_lengths}


@jax.custom_vjp
def low(v):
    return lax.optimization_barrier(v.astype(jnp.bfloat16)).astype(jnp.float32)

@jax.custom_vjp
def low_back(v):
    return v

def low_keep(v):
    return (low(v), None)

def low_pass(kept, grad):
    return (grad,)

def back_keep(v):
    return (v, None)

def back_low(kept, grad):
    return (low(grad),)
low.defvjp(low_keep, low_pass)
low_back.defvjp(back_keep, back_low)
EPS = 1e-06
MASKED = -1e+30
HIGHEST = lax.Precision.HIGHEST

def norm_rows(row_block, norm_gain, norm_shift):
    row_mean = lax.optimization_barrier(jnp.mean(row_block, axis=-1, keepdims=True))
    centred = row_block - row_mean
    spread = lax.optimization_barrier(jnp.mean(centred * centred, axis=-1, keepdims=True))
    return centred * lax.rsqrt(spread + EPS) * norm_gain + norm_shift

def sequence_labels(counts, lengths):
    places = jnp.arange(2 * CAP, dtype=jnp.int32)
    part_index = places // CAP
    in_part = places % CAP
    image_ends = jnp.cumsum(lengths)
    shifted = in_part + part_index * counts[0]
    image_index = lax.optimization_barrier(jnp.sum((image_ends[None, :] <= shifted[:, None]).astype(jnp.int32), axis=1))
    owned_rows = jnp.where(part_index == 0, counts[0], counts[1])
    used_rows = in_part < owned_rows
    image_ids = jnp.where(used_rows, image_index, IMAGES + places)
    return (image_ids, used_rows.astype(jnp.float32))

def attend_one(packed):
    queries, key_rows, value_rows, image_ids = packed
    raw_scores = jnp.einsum('qhd,khd->hqk', queries, key_rows, precision=HIGHEST) * (1.0 / math.sqrt(HD))
    scores = low_back(raw_scores)
    same_image = image_ids[:, None] == image_ids[None, :]
    scores = jnp.where(same_image[None], scores, MASKED)
    weights = jax.nn.softmax(scores, axis=-1)
    return jnp.einsum('hqk,khd->qhd', low(weights), value_rows, precision=HIGHEST)

def group_forward(params, group_in):
    input_weight, query_bias, value_bias, out_weight, out_bias, first_gain, first_shift, second_gain, second_shift, up_weight, up_bias, down_weight, down_bias = params
    inputs, image_ids, used_rows = group_in
    count_here = inputs.shape[0]
    normed = low(norm_rows(inputs, first_gain, first_shift))
    projected = jnp.einsum('grd,de->gre', normed, input_weight, precision=HIGHEST)
    queries = low_back(low(projected[..., 0:D] + query_bias))
    key_rows = low_back(low(projected[..., D:2 * D]))
    value_rows = low_back(low(projected[..., 2 * D:3 * D] + value_bias))
    head_shape = (count_here, 2 * CAP, HEADS, HD)
    attended = lax.map(jax.checkpoint(attend_one), (queries.reshape(head_shape), key_rows.reshape(head_shape), value_rows.reshape(head_shape), image_ids))
    attended = low_back(low(attended.reshape(count_here, 2 * CAP, D)))
    branch = low_back(jnp.einsum('grd,de->gre', attended, out_weight, precision=HIGHEST) + out_bias)
    residual = inputs + branch
    second = low(norm_rows(residual, second_gain, second_shift))
    hidden = low_back(jnp.einsum('grd,de->gre', second, up_weight, precision=HIGHEST) + up_bias)
    active = low(jax.nn.gelu(hidden, approximate=False))
    result = residual + jnp.einsum('gre,ed->grd', active, down_weight, precision=HIGHEST) + down_bias
    return result * used_rows[..., None]

def reference(tokens, input_weight, query_bias, value_bias, out_weight, out_bias, first_gain, first_shift, second_gain, second_shift, up_weight, up_bias, down_weight, down_bias, cotangent, row_counts, image_lengths):
    group_size = math.gcd(SEQUENCES, max(1, 4096 // (2 * CAP)))
    group_count = SEQUENCES // group_size

    def arrange(flat):
        return flat.astype(jnp.float32).reshape(2, SEQUENCES, CAP, D).transpose(1, 0, 2, 3).reshape(SEQUENCES, 2 * CAP, D)

    def unarrange(packed):
        return packed.reshape(SEQUENCES, 2, CAP, D).transpose(1, 0, 2, 3).reshape(TOKENS, D)
    image_ids, used_rows = jax.vmap(sequence_labels)(row_counts, image_lengths)
    params = (input_weight.astype(jnp.float32), query_bias.astype(jnp.float32), value_bias.astype(jnp.float32), out_weight.astype(jnp.float32), out_bias.astype(jnp.float32), first_gain.astype(jnp.float32), first_shift.astype(jnp.float32), second_gain.astype(jnp.float32), second_shift.astype(jnp.float32), up_weight.astype(jnp.float32), up_bias.astype(jnp.float32), down_weight.astype(jnp.float32), down_bias.astype(jnp.float32))

    def forward(weights, row_block):
        grouped = (row_block.reshape(group_count, group_size, 2 * CAP, D), image_ids.reshape(group_count, group_size, 2 * CAP), used_rows.reshape(group_count, group_size, 2 * CAP))
        result = lax.map(lambda group_in: jax.checkpoint(group_forward)(weights, group_in), grouped)
        return result.reshape(SEQUENCES, 2 * CAP, D)
    outputs, pull = jax.vjp(forward, params, arrange(tokens))
    param_grads, input_grad = pull(arrange(cotangent))
    return (unarrange(outputs).astype(jnp.bfloat16), unarrange(input_grad).astype(jnp.bfloat16), param_grads[0], param_grads[1], param_grads[2], param_grads[3], param_grads[4], param_grads[5], param_grads[6], param_grads[7], param_grads[8], param_grads[9], param_grads[10], param_grads[11], param_grads[12])
```

```python
import jax
import jax.numpy as jnp
from jax import lax
from jax.experimental import pallas as pl
from jax.experimental.pallas import tpu as pltpu
from jax.sharding import PartitionSpec as P

F32 = jnp.float32
BF = jnp.bfloat16
EPS = 1e-06
ROWS = 512
WIDTH = 768
TILE = 256
CHUNKS = 11
SLOTS = 7
FEATURES = 37
MESH = pl.DeviceIdType.MESH


def dot_nn(left, right):
    return lax.dot_general(left, right, (((1,), (0,)), ((), ())), preferred_element_type=F32)


def dot_nt(left, right):
    return lax.dot_general(left, right, (((1,), (1,)), ((), ())), preferred_element_type=F32)


def dot_tn(left, right):
    return lax.dot_general(left, right, (((0,), (0,)), ((), ())), preferred_element_type=F32)


def norm_parts(block):
    centred = block - jnp.mean(block, axis=-1, keepdims=True)
    spread = jnp.mean(centred * centred, axis=-1, keepdims=True)
    inverse = lax.rsqrt(spread + EPS)
    return centred * inverse, inverse


def kernel(
    counts_ref,
    lengths_ref,
    tokens_hbm,
    cot_hbm,
    wi_hbm,
    wo_hbm,
    wu_hbm,
    wd_hbm,
    qb_ref,
    vb_ref,
    ob_ref,
    fg_ref,
    fs_ref,
    sg_ref,
    ss_ref,
    ub_ref,
    db_ref,
    lo_hbm,
    gt_hbm,
    gi_ref,
    gqb_ref,
    gvb_ref,
    go_ref,
    gob_ref,
    gfg_ref,
    gfs_ref,
    gsg_ref,
    gss_ref,
    gu_ref,
    gub_ref,
    gd_ref,
    gdb_ref,
    W,
    CH,
    R0,
    R1,
    R2,
    R3,
    FT,
    FDO,
    STAT,
    FSTAT,
    QO,
    KO,
    VO,
    QF,
    KF,
    VF,
    TOK,
    COT,
    ATT,
    SEC,
    ACT,
    DH,
    XT,
    RES,
    ACC1,
    ACC2,
    MF,
    PB,
    VS,
    VR,
    wsem,
    iosem,
    xsend,
    xrecv,
    rsend,
    rrecv,
    vsend,
    vrecv,
):
    part = lax.axis_index("seq")
    dp = lax.axis_index("dp")
    y_lo = dp // 32
    z = (dp // 8) % 4
    x = (dp // 2) % 4
    core = dp % 2
    y = 2 * part + y_lo

    def device(yy, zz, xx, cc):
        return (yy // 2, ((yy % 2) * 4 + zz) * 8 + xx * 2 + cc)

    sibling = device(y, z, x, 1 - core)
    z_of = [(z + k) % 4 for k in range(4)]
    x_of = [(x + k) % 4 for k in range(4)]
    y_of = [(y + k) % 4 for k in range(4)]
    z_peer = [device(y, v, x, core) for v in z_of]
    x_peer = [device(y, z, v, core) for v in x_of]
    y_peer = [device(v, z, x, core) for v in y_of]
    partner = y_peer[2]

    def load(src, dst, sem):
        copy = pltpu.make_async_copy(src, dst, sem)
        copy.start()
        return copy

    tok_load = load(tokens_hbm, TOK, iosem.at[0])
    w_load = {}
    for i in range(3):
        w_load[i] = load(wi_hbm.at[:, pl.ds(WIDTH * i, WIDTH)], W.at[i], wsem.at[i])
    cot_load = load(cot_hbm, COT, iosem.at[1])
    w_load[3] = load(wo_hbm, W.at[3], wsem.at[3])

    def load_ffn(f):
        slot = f % 2
        up = load(wu_hbm.at[:, pl.ds(WIDTH * f, WIDTH)], W.at[4 + slot], wsem.at[4 + slot])
        down = load(wd_hbm.at[pl.ds(WIDTH * f, WIDTH)], W.at[6 + slot], wsem.at[6 + slot])
        return up, down

    ffn_load = {0: load_ffn(0), 1: load_ffn(1)}

    barrier = pltpu.get_barrier_semaphore()
    for peer in [sibling] + z_peer[1:] + x_peer[1:] + y_peer[1:]:
        pl.semaphore_signal(barrier, inc=1, device_id=peer, device_id_type=MESH)
    pl.semaphore_wait(barrier, 10)

    def remote(src, dst, send, recv, peer):
        copy = pltpu.make_async_remote_copy(
            src_ref=src,
            dst_ref=dst,
            send_sem=send,
            recv_sem=recv,
            device_id=peer,
            device_id_type=MESH,
        )
        copy.start()
        return copy

    far_tokens = remote(tokens_hbm, FT, xsend.at[0], xrecv.at[0], partner)

    sent = {}

    def rs_core(c):
        sent[c, 0] = [
            remote(
                CH.at[c % SLOTS, :, :, :, 1 - core],
                R0.at[c],
                rsend.at[c, 0],
                rrecv.at[c, 0],
                sibling,
            )
        ]

    def rs_first(c):
        sent[c, 0][0].wait_recv()

        def add(i, carry):
            yl, zz = i // 4, i % 4
            R0[c, yl, zz] = (
                R0[c, yl, zz].astype(F32) + CH[c % SLOTS, yl, zz, :, core].astype(F32)
            ).astype(BF)
            return carry

        lax.fori_loop(0, 8, add, 0)
        sent[c, 1] = []
        for k in (2, 1, 3):
            if c % 2 == 0:
                src, peer = R0.at[c, :, z_of[k]], z_peer[k]
            else:
                src, peer = R0.at[c, :, :, x_of[k]], x_peer[k]
            sent[c, 1].append(
                remote(src, R1.at[c, k - 1], rsend.at[c, k], rrecv.at[c, k], peer)
            )

    def rs_second(c):
        for copy in sent[c, 1]:
            copy.wait_recv()
        for yl in range(2):
            own = R0[c, yl, z] if c % 2 == 0 else R0[c, yl, :, x]
            total = own.astype(F32)
            for k in range(3):
                total = total + R1[c, k, yl].astype(F32)
            R1[c, 0, yl] = total.astype(BF)
        sent[c, 2] = []
        for k in (2, 1, 3):
            if c % 2 == 0:
                src, peer = R1.at[c, 0, :, x_of[k]], x_peer[k]
            else:
                src, peer = R1.at[c, 0, :, z_of[k]], z_peer[k]
            sent[c, 2].append(
                remote(src, R2.at[c, k - 1], rsend.at[c, 3 + k], rrecv.at[c, 3 + k], peer)
            )

    def rs_y(c):
        for copy in sent[c, 2]:
            copy.wait_recv()
        own = R1[c, 0, :, x] if c % 2 == 0 else R1[c, 0, :, z]
        total = own.astype(F32)
        for k in range(3):
            total = total + R2[c, k].astype(F32)
        R2[c, 0] = total.astype(BF)
        sent[c, 3] = []
        for k in (2, 1, 3):
            sent[c, 3].append(
                remote(
                    R2.at[c, 0, y_of[k] % 2],
                    R3.at[c, k - 1],
                    rsend.at[c, 6 + k],
                    rrecv.at[c, 6 + k],
                    y_peer[k],
                )
            )

    def rs_end(c):
        for copy in sent[c, 3]:
            copy.wait_recv()
        total = R2[c, 0, y_lo].astype(F32)
        for k in range(3):
            total = total + R3[c, k].astype(F32)
        if c < 4:
            gu_ref[:, WIDTH * c : WIDTH * (c + 1)] = total[0:12]
        elif c < 7:
            gd_ref[16 * (c - 4) : 16 * (c - 3), :] = total
        elif c == 7:
            go_ref[...] = total[0:12]
        else:
            j = c - 8
            for b in range(3):
                gi_ref[:, WIDTH * b + TILE * j : WIDTH * b + TILE * (j + 1)] = total[
                    0:12, TILE * b : TILE * (b + 1)
                ]

    counts0 = counts_ref[0, 0]
    counts1 = counts_ref[0, 1]
    end0 = lengths_ref[0, 0]
    end1 = end0 + lengths_ref[0, 1]
    end2 = end1 + lengths_ref[0, 2]
    end3 = end2 + lengths_ref[0, 3]

    def used_rows(start, size, width):
        place = lax.broadcasted_iota(jnp.int32, (size, width), 0) + start
        return place < counts0 + part * (counts1 - counts0)

    def features(base, which):
        place = lax.broadcasted_iota(jnp.int32, (ROWS, 128), 0)
        shifted = place + which * counts0
        index = jnp.zeros((ROWS, 128), jnp.int32)
        for end in (end0, end1, end2, end3):
            index = index + jnp.where(end <= shifted, 1, 0)
        owned = counts0 + which * (counts1 - counts0)
        ids = jnp.where(place < owned, index, 4 + which * ROWS + place)
        lane = lax.broadcasted_iota(jnp.int32, (ROWS, 128), 1)
        high = lane >= 64
        spot = jnp.where(high, lane - 64, lane)
        digit = jnp.where(
            spot < 16, ids & 15, jnp.where(spot < 32, ((ids >> 4) & 15) + 16, (ids >> 8) + 32)
        )
        hot = jnp.where(digit == spot, 1.0, 0.0)
        query = jnp.where(spot < FEATURES, 1.0 - hot, 0.0)
        key = hot * -1e30
        MF[base] = jnp.where(high, query, 0.0).astype(BF)
        MF[base + 1] = jnp.where(high, 0.0, query).astype(BF)
        MF[base + 2] = jnp.where(high, key, 0.0).astype(BF)
        MF[base + 3] = jnp.where(high, 0.0, key).astype(BF)

    features(0, part)
    features(4, 1 - part)
    lane_row = lax.broadcasted_iota(jnp.int32, (1, 128), 1)
    select = [
        jnp.where(lane_row < 64, 1.0, 0.0).astype(BF),
        jnp.where(lane_row < 64, 0.0, 1.0).astype(BF),
    ]

    rho = lax.broadcasted_iota(jnp.int32, (ROWS, 384), 0)
    feature = lax.broadcasted_iota(jnp.int32, (ROWS, 384), 1)
    within = rho & 15
    PB[...] = jnp.where(
        (within < 12) & (feature == (rho >> 4) * 12 + within), 1.0, 0.0
    ).astype(BF)

    def padded_transpose(source):
        for b in range(2):
            XT[ROWS * b : ROWS * (b + 1), :] = dot_nt(
                PB[...], source[:, 384 * b : 384 * (b + 1)]
            ).astype(BF)

    def chunk_matmul(c, right):
        def block(m, carry):
            start = pl.multiple_of(m * TILE, TILE)
            out = dot_nn(XT[pl.ds(start, TILE), :], right())
            CH[c % SLOTS, m // 2, pl.ds(2 * (m % 2), 2)] = out.astype(BF).reshape(
                2, 4, 2, 16, WIDTH
            )
            return carry

        lax.fori_loop(0, 4, block, 0)

    ones = jnp.ones((16, ROWS), BF)

    def row_sum(block):
        return dot_nn(ones, block)[0:1]

    def tiles(step):
        def run(t, carry):
            step(pl.ds(pl.multiple_of(t * TILE, TILE), TILE), t * TILE)
            return carry

        lax.fori_loop(0, ROWS // TILE, run, 0)

    qb = qb_ref[...].reshape(1, WIDTH)
    vb = vb_ref[...].reshape(1, WIDTH)
    ob = ob_ref[...].reshape(1, WIDTH)
    fg = fg_ref[...].reshape(1, WIDTH)
    fs = fs_ref[...].reshape(1, WIDTH)
    sg = sg_ref[...].reshape(1, WIDTH)
    ss = ss_ref[...].reshape(1, WIDTH)
    db = db_ref[...].reshape(1, WIDTH)

    def project(source, q_ref, k_ref, v_ref):
        def step(rows, start):
            unit, _ = norm_parts(source[rows, :].astype(F32))
            normed = (unit * fg + fs).astype(BF)
            q = (dot_nn(normed, W[0]) + qb).astype(BF)
            q_ref[rows, :] = q * jnp.asarray(0.125, BF)
            k_ref[rows, :] = dot_nn(normed, W[1]).astype(BF)
            v_ref[rows, :] = (dot_nn(normed, W[2]) + vb).astype(BF)

        tiles(step)

    tok_load.wait()
    for i in range(3):
        w_load[i].wait()
    project(TOK, QO, KO, VO)

    cot_load.wait()

    def mask_cot(rows, start):
        used = used_rows(start, TILE, WIDTH)
        COT[rows, :] = jnp.where(used, COT[rows, :].astype(F32), 0.0).astype(BF)

    tiles(mask_cot)

    far_tokens.wait_recv()
    project(FT, QF, KF, VF)

    def pair_cols(hp):
        return pl.ds(pl.multiple_of(hp * 128, 128), 128)

    def attend(hp, carry):
        cols = pair_cols(hp)
        q = QO[:, cols]
        ko = KO[:, cols]
        kf = KF[:, cols]
        vo_t = VO[:, cols].T
        vf_t = VF[:, cols].T
        outs = []
        for h in range(2):
            qm = q * select[h] + MF[h]
            near = dot_nt(ko * select[h] + MF[2 + h], qm)
            far = dot_nt(kf * select[h] + MF[6 + h], qm)
            top = jnp.maximum(
                jnp.max(near, axis=0, keepdims=True), jnp.max(far, axis=0, keepdims=True)
            )
            near = jnp.exp(near - top)
            far = jnp.exp(far - top)
            total = jnp.sum(near, axis=0, keepdims=True) + jnp.sum(far, axis=0, keepdims=True)
            mixed = dot_nn(vo_t[64 * h : 64 * h + 64], near.astype(BF)) + dot_nn(
                vf_t[64 * h : 64 * h + 64], far.astype(BF)
            )
            outs.append(mixed * (1.0 / total))
            STAT[0, pl.ds(2 * hp + h, 1), :] = top + jnp.log(total)
        ATT[:, cols] = jnp.concatenate(outs, axis=0).T.astype(BF)
        return carry

    lax.fori_loop(0, 6, attend, 0)

    w_load[3].wait()

    def out_step(rows, start):
        res = TOK[rows, :].astype(F32) + dot_nn(ATT[rows, :], W[3]) + ob
        RES[rows, :] = res
        unit, _ = norm_parts(res)
        SEC[rows, :] = (unit * sg + ss).astype(BF)
        ACC1[rows, :] = jnp.zeros((TILE, WIDTH), F32)
        ACC2[rows, :] = jnp.zeros((TILE, WIDTH), F32)

    tiles(out_step)
    padded_transpose(SEC)
    VS[0] = jnp.zeros((16, WIDTH), F32)

    for f in range(4):
        slot = f % 2
        for copy in ffn_load[f]:
            copy.wait()
        ub = ub_ref[WIDTH * f : WIDTH * (f + 1)].reshape(1, WIDTH)

        def ffn_step(rows, start, slot=slot, ub=ub):
            dout = COT[rows, :]
            hidden = dot_nn(SEC[rows, :], W[4 + slot]) + ub
            cdf = 0.5 * (1.0 + lax.erf(hidden * 0.7071067811865476))
            density = jnp.exp(-0.5 * hidden * hidden) * 0.3989422804014327
            active = (hidden * cdf).astype(BF)
            ACT[rows, :] = active
            dhidden = (dot_nt(dout, W[6 + slot]) * (cdf + hidden * density)).astype(BF)
            DH[rows, :] = dhidden
            ACC1[rows, :] += dot_nn(active, W[6 + slot])
            ACC2[rows, :] += dot_nt(dhidden, W[4 + slot])

        tiles(ffn_step)
        if f + 2 < 4:
            ffn_load[f + 2] = load_ffn(f + 2)
        chunk_matmul(f, lambda: DH[...])
        rs_core(f)
        VS[0, 8 + f : 9 + f, :] = row_sum(DH[...])

        def down_step(b, carry, f=f):
            cols = pl.ds(pl.multiple_of(b * 384, 384), 384)
            out = dot_tn(ACT[:, cols], COT[...]).astype(BF).reshape(4, 2, 3, 16, WIDTH)
            for k in range(3):
                CH[4 + k, f // 2, 2 * (f % 2) + b] = out[:, :, k]
            return carry

        lax.fori_loop(0, 2, down_step, 0)
        if f >= 1:
            rs_first(f - 1)
        if f >= 2:
            rs_second(f - 2)

    for k in range(3):
        rs_core(4 + k)
    rs_first(3)
    rs_second(2)
    rs_y(0)

    def second_back(rows, start):
        res = RES[rows, :]
        used = used_rows(start, TILE, WIDTH)
        FT[rows, :] = jnp.where(used, res + ACC1[rows, :] + db, 0.0).astype(BF)
        unit, inverse = norm_parts(res)
        dsecond = ACC2[rows, :]
        VS[0, 5:6, :] += jnp.sum(dsecond * unit, axis=0, keepdims=True)
        VS[0, 6:7, :] += jnp.sum(dsecond, axis=0, keepdims=True)
        g = dsecond * sg
        through = (
            g
            - jnp.mean(g, axis=-1, keepdims=True)
            - unit * jnp.mean(g * unit, axis=-1, keepdims=True)
        ) * inverse
        dres = COT[rows, :].astype(F32) + through
        RES[rows, :] = dres
        SEC[rows, :] = dres.astype(BF)
        DH[rows, :] = dot_nt(dres.astype(BF), W[3]).astype(BF)

    tiles(second_back)
    lo_store = load(FT, lo_hbm, iosem.at[2])
    far_dout = remote(DH, FDO, xsend.at[1], xrecv.at[1], partner)
    VS[0, 7:8, :] = row_sum(COT[...])
    VS[0, 2:3, :] = row_sum(SEC[...])

    head = lax.broadcasted_iota(jnp.int32, (16, WIDTH), 0)
    column = lax.broadcasted_iota(jnp.int32, (16, WIDTH), 1)
    in_head = jnp.where((column >> 6) == head, 1.0, 0.0).astype(BF)
    product = DH[...].astype(F32) * ATT[...].astype(F32)
    rough = product.astype(BF)
    STAT[1] = dot_nt(in_head, rough) + dot_nt(in_head, (product - rough.astype(F32)).astype(BF))
    far_stats = remote(STAT, FSTAT, xsend.at[2], xrecv.at[2], partner)

    padded_transpose(ATT)
    sent[0, 0][0].wait_send()
    chunk_matmul(7, lambda: SEC[...])
    rs_core(7)
    for k in range(3):
        rs_first(4 + k)
    rs_second(3)
    rs_y(1)
    rs_end(0)

    def own_queries(hp, carry):
        cols = pair_cols(hp)
        q = QO[:, cols]
        ko = KO[:, cols]
        kf = KF[:, cols]
        vo = VO[:, cols]
        vf = VF[:, cols]
        do = DH[:, cols]
        ko_t = ko.T
        kf_t = kf.T
        dq = []
        dk = None
        for h in range(2):
            logsum = STAT[0, pl.ds(2 * hp + h, 1), :]
            delta = STAT[1, pl.ds(2 * hp + h, 1), :]
            qm = q * select[h] + MF[h]
            qs = q * select[h]
            dom = do * select[h]
            near = jnp.exp(dot_nt(ko * select[h] + MF[2 + h], qm) - logsum)
            dnear = (near * (dot_nt(vo, dom) - delta)).astype(BF)
            far = jnp.exp(dot_nt(kf * select[h] + MF[6 + h], qm) - logsum)
            dfar = (far * (dot_nt(vf, dom) - delta)).astype(BF)
            dq.append(
                dot_nn(ko_t[64 * h : 64 * h + 64], dnear)
                + dot_nn(kf_t[64 * h : 64 * h + 64], dfar)
            )
            dk_h = dot_nn(dnear, qs)
            dv_h = dot_nn(near.astype(BF), dom)
            dk, dv = (dk_h, dv_h) if dk is None else (dk + dk_h, dv + dv_h)
        ACC1[:, cols] = dk
        ACC2[:, cols] = dv
        QO[:, cols] = (jnp.concatenate(dq, axis=0).T * 0.125).astype(BF)
        return carry

    lax.fori_loop(0, 3, own_queries, 0)
    for k in range(3):
        rs_second(4 + k)
    rs_first(7)
    rs_y(2)
    rs_y(3)
    rs_end(1)
    lax.fori_loop(3, 6, own_queries, 0)
    for k in range(3):
        rs_y(4 + k)
    rs_second(7)
    rs_end(2)
    rs_end(3)

    def again(rows, start):
        unit, _ = norm_parts(TOK[rows, :].astype(F32))
        ATT[rows, :] = (unit * fg + fs).astype(BF)

    tiles(again)
    padded_transpose(ATT)

    far_dout.wait_recv()
    far_stats.wait_recv()

    def far_queries(hp, carry):
        cols = pair_cols(hp)
        q = QF[:, cols]
        ko = KO[:, cols]
        vo = VO[:, cols]
        do = FDO[:, cols]
        dk = ACC1[:, cols]
        dv = ACC2[:, cols]
        for h in range(2):
            logsum = FSTAT[0, pl.ds(2 * hp + h, 1), :]
            delta = FSTAT[1, pl.ds(2 * hp + h, 1), :]
            qs = q * select[h]
            dom = do * select[h]
            probs = jnp.exp(dot_nt(ko * select[h] + MF[2 + h], qs + MF[4 + h]) - logsum)
            dscores = (probs * (dot_nt(vo, dom) - delta)).astype(BF)
            dk = dk + dot_nn(dscores, qs)
            dv = dv + dot_nn(probs.astype(BF), dom)
        KO[:, cols] = dk.astype(BF)
        VO[:, cols] = dv.astype(BF)
        return carry

    for j in range(3):
        c = 8 + j
        lax.fori_loop(2 * j, 2 * j + 2, far_queries, 0)
        sent[c - 7, 0][0].wait_send()
        cols = slice(TILE * j, TILE * (j + 1))

        def joined(cols=cols):
            return jnp.concatenate([QO[:, cols], KO[:, cols], VO[:, cols]], axis=1)

        chunk_matmul(c, joined)
        rs_core(c)
        if j == 0:
            rs_y(7)
            for k in range(3):
                rs_end(4 + k)
        if j == 1:
            rs_first(8)
            rs_end(7)
        if j == 2:
            rs_first(9)
            rs_second(8)

    VS[0, 0:1, :] = row_sum(QO[...])
    VS[0, 1:2, :] = row_sum(VO[...])

    def first_back(rows, start):
        unit, inverse = norm_parts(TOK[rows, :].astype(F32))
        dnormed = (
            dot_nt(QO[rows, :], W[0]) + dot_nt(KO[rows, :], W[1]) + dot_nt(VO[rows, :], W[2])
        )
        VS[0, 3:4, :] += jnp.sum(dnormed * unit, axis=0, keepdims=True)
        VS[0, 4:5, :] += jnp.sum(dnormed, axis=0, keepdims=True)
        g = dnormed * fg
        through = (
            g
            - jnp.mean(g, axis=-1, keepdims=True)
            - unit * jnp.mean(g * unit, axis=-1, keepdims=True)
        ) * inverse
        TOK[rows, :] = (RES[rows, :] + through).astype(BF)

    far_tokens.wait_send()
    tiles(first_back)
    gt_store = load(TOK, gt_hbm, iosem.at[3])

    vsent = []

    def vec_send(step, peers, base):
        vsent.append(
            [
                remote(VS.at[step], VR.at[base + i], vsend.at[base + i], vrecv.at[base + i], peer)
                for i, peer in enumerate(peers)
            ]
        )

    def vec_add(step, base):
        total = VS[step]
        for i, copy in enumerate(vsent[step]):
            copy.wait_recv()
            total = total + VR[base + i]
        VS[step + 1] = total

    vec_send(0, [sibling], 0)
    rs_first(10)
    rs_second(9)
    rs_y(8)
    vec_add(0, 0)
    vec_send(1, z_peer[1:], 1)
    rs_second(10)
    rs_y(9)
    rs_end(8)
    vec_add(1, 1)
    vec_send(2, x_peer[1:], 4)
    rs_y(10)
    rs_end(9)
    vec_add(2, 4)
    vec_send(3, y_peer[1:], 7)
    rs_end(10)
    vec_add(3, 7)

    spot = lax.broadcasted_iota(jnp.int32, (WIDTH, 128), 0)
    lane = lax.broadcasted_iota(jnp.int32, (WIDTH, 128), 1)
    narrow = jnp.where((lane < 12) & (spot == lane + 12 * dp), 1.0, 0.0)
    wide = jnp.where((lane < 48) & (spot == lane + 48 * (dp % 16)), 1.0, 0.0)
    vectors = VS[4]
    exact = dict(precision=lax.Precision.HIGHEST, preferred_element_type=F32)
    small = jnp.dot(vectors, narrow, **exact)
    large = jnp.dot(vectors, wide, **exact)
    row = lax.broadcasted_iota(jnp.int32, (16, 128), 0)
    large = jnp.sum(jnp.where(row == 8 + dp // 16, large, 0.0), axis=0, keepdims=True)
    for i, ref in enumerate(
        (gqb_ref, gvb_ref, gob_ref, gfg_ref, gfs_ref, gsg_ref, gss_ref, gdb_ref)
    ):
        ref[...] = small[i : i + 1, 0:12].reshape(12)
    gub_ref[...] = large[:, 0:48].reshape(48)

    far_dout.wait_send()
    far_stats.wait_send()
    for c in range(CHUNKS):
        if not (c == 0 or 1 <= c <= 3):
            sent[c, 0][0].wait_send()
        for s in (1, 2, 3):
            for copy in sent[c, s]:
                copy.wait_send()
    for copies in vsent:
        for copy in copies:
            copy.wait_send()
    lo_store.wait()
    gt_store.wait()


def body(
    tokens,
    input_weight,
    query_bias,
    value_bias,
    out_weight,
    out_bias,
    first_gain,
    first_shift,
    second_gain,
    second_shift,
    up_weight,
    up_bias,
    down_weight,
    down_bias,
    cotangent,
    row_counts,
    image_lengths,
):
    hbm = pl.BlockSpec(memory_space=pl.ANY)
    vmem = pl.BlockSpec(memory_space=pltpu.VMEM)
    smem = pl.BlockSpec(memory_space=pltpu.SMEM)
    rows = jax.ShapeDtypeStruct((ROWS, WIDTH), BF)

    def f32(*shape):
        return jax.ShapeDtypeStruct(shape, F32)

    def block(kind, *lead):
        return pltpu.VMEM((*lead, ROWS, WIDTH), kind)

    out = pl.pallas_call(
        kernel,
        out_shape=(
            rows,
            rows,
            f32(12, 3 * WIDTH),
            f32(12),
            f32(12),
            f32(12, WIDTH),
            f32(12),
            f32(12),
            f32(12),
            f32(12),
            f32(12),
            f32(12, 4 * WIDTH),
            f32(48),
            f32(48, WIDTH),
            f32(12),
        ),
        in_specs=[smem, smem] + [hbm] * 6 + [vmem] * 9,
        out_specs=(hbm, hbm) + (vmem,) * 13,
        scratch_shapes=[
            pltpu.VMEM((8, WIDTH, WIDTH), BF),
            pltpu.VMEM((SLOTS, 2, 4, 4, 2, 16, WIDTH), BF),
            pltpu.VMEM((CHUNKS, 2, 4, 4, 16, WIDTH), BF),
            pltpu.VMEM((CHUNKS, 3, 2, 4, 16, WIDTH), BF),
            pltpu.VMEM((CHUNKS, 3, 2, 16, WIDTH), BF),
            pltpu.VMEM((CHUNKS, 3, 16, WIDTH), BF),
            block(BF),
            block(BF),
            pltpu.VMEM((2, 16, ROWS), F32),
            pltpu.VMEM((2, 16, ROWS), F32),
        ]
        + [block(BF)] * 12
        + [
            pltpu.VMEM((1024, ROWS), BF),
            block(F32),
            block(F32),
            block(F32),
            pltpu.VMEM((8, ROWS, 128), BF),
            pltpu.VMEM((ROWS, 384), BF),
            pltpu.VMEM((5, 16, WIDTH), F32),
            pltpu.VMEM((10, 16, WIDTH), F32),
            pltpu.SemaphoreType.DMA((8,)),
            pltpu.SemaphoreType.DMA((4,)),
            pltpu.SemaphoreType.DMA((3,)),
            pltpu.SemaphoreType.DMA((3,)),
            pltpu.SemaphoreType.DMA((CHUNKS, 10)),
            pltpu.SemaphoreType.DMA((CHUNKS, 10)),
            pltpu.SemaphoreType.DMA((10,)),
            pltpu.SemaphoreType.DMA((10,)),
        ],
        compiler_params=pltpu.CompilerParams(
            collective_id=0, has_side_effects=True, vmem_limit_bytes=61 * 2**20
        ),
        name="encoder",
    )(
        row_counts,
        image_lengths,
        tokens,
        cotangent,
        input_weight,
        out_weight,
        up_weight,
        down_weight,
        query_bias,
        value_bias,
        out_bias,
        first_gain,
        first_shift,
        second_gain,
        second_shift,
        up_bias,
        down_bias,
    )
    return out


def solution(mesh):
    rows = P(("seq", "dp"), None)
    split = P("dp", None)
    line = P("dp")
    return jax.shard_map(
        body,
        mesh=mesh,
        in_specs=(rows,) + (P(),) * 13 + (rows, split, split),
        out_specs=(
            rows,
            rows,
            split,
            line,
            line,
            split,
            line,
            line,
            line,
            line,
            line,
            split,
            line,
            split,
            line,
        ),
        check_vma=False,
    )
```

```python
import jax
import jax.numpy as jnp
from jax import lax
from jax.experimental import pallas as pl
from jax.experimental.pallas import tpu as pltpu
from jax.sharding import PartitionSpec as P

F32 = jnp.float32
BF = jnp.bfloat16
EPS = 1e-06
ROWS = 512
WIDTH = 768
TILE = 256
CHUNKS = 11
SLOTS = 7
FEATURES = 37
WHOLE = (0, 1, 2, 3, 8, 9, 10)
MESH = pl.DeviceIdType.MESH


def dot_nn(left, right):
    return lax.dot_general(left, right, (((1,), (0,)), ((), ())), preferred_element_type=F32)


def dot_nt(left, right):
    return lax.dot_general(left, right, (((1,), (1,)), ((), ())), preferred_element_type=F32)


def dot_tn(left, right):
    return lax.dot_general(left, right, (((0,), (0,)), ((), ())), preferred_element_type=F32)


def norm_parts(block):
    centred = block - jnp.mean(block, axis=-1, keepdims=True)
    spread = jnp.mean(centred * centred, axis=-1, keepdims=True)
    inverse = lax.rsqrt(spread + EPS)
    return centred * inverse, inverse


def kernel(
    counts_ref,
    lengths_ref,
    tokens_hbm,
    cot_hbm,
    wi_hbm,
    wo_hbm,
    wu_hbm,
    wd_hbm,
    qb_ref,
    vb_ref,
    ob_ref,
    fg_ref,
    fs_ref,
    sg_ref,
    ss_ref,
    ub_ref,
    db_ref,
    lo_hbm,
    gt_hbm,
    gi_ref,
    gqb_ref,
    gvb_ref,
    go_ref,
    gob_ref,
    gfg_ref,
    gfs_ref,
    gsg_ref,
    gss_ref,
    gu_ref,
    gub_ref,
    gd_ref,
    gdb_ref,
    W,
    CH,
    R0,
    R1,
    R2,
    R3,
    S1,
    S2,
    S3,
    S4,
    FT,
    FDO,
    STAT,
    FSTAT,
    QO,
    KO,
    VO,
    QF,
    KF,
    VF,
    TOK,
    COT,
    ATT,
    SEC,
    ACT,
    DH,
    XT,
    RES,
    ACC,
    MF,
    PB,
    TOP,
    SUM,
    VS,
    VR,
    wsem,
    iosem,
    xsend,
    xrecv,
    rsend,
    rrecv,
    vsend,
    vrecv,
):
    ACC1, ACC2 = ACC.at[0], ACC.at[1]
    part = lax.axis_index("seq")
    dp = lax.axis_index("dp")
    y_lo = dp // 32
    z = (dp // 8) % 4
    x = (dp // 2) % 4
    core = dp % 2
    y = 2 * part + y_lo

    def device(yy, zz, xx, cc):
        return (yy // 2, ((yy % 2) * 4 + zz) * 8 + xx * 2 + cc)

    sibling = device(y, z, x, 1 - core)
    z_of = [(z + k) % 4 for k in range(4)]
    x_of = [(x + k) % 4 for k in range(4)]
    y_of = [(y + k) % 4 for k in range(4)]
    z_peer = [device(y, v, x, core) for v in z_of]
    x_peer = [device(y, z, v, core) for v in x_of]
    y_peer = [device(v, z, x, core) for v in y_of]
    partner = y_peer[2]

    def load(src, dst, sem):
        copy = pltpu.make_async_copy(src, dst, sem)
        copy.start()
        return copy

    tok_load = load(tokens_hbm, TOK, iosem.at[0])
    w_load = {}
    for i in range(3):
        w_load[i] = load(wi_hbm.at[:, pl.ds(WIDTH * i, WIDTH)], W.at[i], wsem.at[i])
    cot_load = load(cot_hbm, COT, iosem.at[1])
    w_load[3] = load(wo_hbm, W.at[3], wsem.at[3])

    def load_ffn(f):
        slot = f % 2
        up = load(wu_hbm.at[:, pl.ds(WIDTH * f, WIDTH)], W.at[4 + slot], wsem.at[4 + slot])
        down = load(wd_hbm.at[pl.ds(WIDTH * f, WIDTH)], W.at[6 + slot], wsem.at[6 + slot])
        return up, down

    ffn_load = {0: load_ffn(0), 1: load_ffn(1)}

    barrier = pltpu.get_barrier_semaphore()
    for peer in [sibling] + z_peer[1:] + x_peer[1:] + y_peer[1:]:
        pl.semaphore_signal(barrier, inc=1, device_id=peer, device_id_type=MESH)
    pl.semaphore_wait(barrier, 10)

    def remote(src, dst, send, recv, peer):
        copy = pltpu.make_async_remote_copy(
            src_ref=src,
            dst_ref=dst,
            send_sem=send,
            recv_sem=recv,
            device_id=peer,
            device_id_type=MESH,
        )
        copy.start()
        return copy

    far_tokens = []
    for r in range(2):
        half = pl.ds(TILE * r, TILE)
        far_tokens.append(
            remote(tokens_hbm.at[half], FT.at[half], xsend.at[r], xrecv.at[r], partner)
        )

    sent = {}

    def send_all(key, copies):
        sent[key] = [remote(*copy) for copy in copies]

    def received(key):
        for copy in sent[key]:
            copy.wait_recv()

    def parts(c):
        if c in WHOLE:
            return ((0, 0, 256), (1, 256, 512), (2, 512, 768))
        return ((0, 0, 384), (1, 384, 768))

    def rs_core(c):
        src = CH.at[c % SLOTS, :, :, :, 1 - core]
        send_all((c, 0), [(src, R0.at[c], rsend.at[c, 0], rrecv.at[c, 0], sibling)])

    def rs_first(c):
        received((c, 0))

        def add(i, carry):
            yl, zz = i // 4, i % 4
            R0[c, yl, zz] = (
                R0[c, yl, zz].astype(F32) + CH[c % SLOTS, yl, zz, :, core].astype(F32)
            ).astype(BF)
            return carry

        lax.fori_loop(0, 8, add, 0)
        for p, lo, hi in parts(c):
            copies = []
            for k in (2, 1, 3):
                sem = 10 * p + k
                if p == 0:
                    src = R0.at[c, :, z_of[k], :, :, lo:hi]
                    dst, peer = R1.at[c, k - 1, :, :, :, lo:hi], z_peer[k]
                elif p == 1:
                    src = R0.at[c, :, :, x_of[k], :, lo:hi]
                    dst, peer = R1.at[c, k - 1, :, :, :, lo:hi], x_peer[k]
                else:
                    start = pl.multiple_of(lo + 128 * (y_of[k] // 2), 128)
                    src = R0.at[c, y_of[k] % 2, :, :, :, pl.ds(start, 128)]
                    dst, peer = S1.at[WHOLE.index(c), k - 1], y_peer[k]
                copies.append((src, dst, rsend.at[c, sem], rrecv.at[c, sem], peer))
            send_all((c, 1, p), copies)

    def rs_second(c):
        for p, lo, hi in parts(c):
            received((c, 1, p))
            copies = []
            if p == 2:
                n = WHOLE.index(c)
                start = pl.multiple_of(lo + 128 * part, 128)
                total = R0[c, y_lo, :, :, :, pl.ds(start, 128)].astype(F32)
                for k in range(3):
                    total = total + S1[n, k].astype(F32)
                S1[n, 0] = total.astype(BF)
            else:
                for yl in range(2):
                    if p == 0:
                        total = R0[c, yl, z, :, :, lo:hi].astype(F32)
                    else:
                        total = R0[c, yl, :, x, :, lo:hi].astype(F32)
                    for k in range(3):
                        total = total + R1[c, k, yl, :, :, lo:hi].astype(F32)
                    R1[c, 0, yl, :, :, lo:hi] = total.astype(BF)
            for k in (2, 1, 3):
                sem = 10 * p + 3 + k
                if p == 0:
                    src = R1.at[c, 0, :, x_of[k], :, lo:hi]
                    dst, peer = R2.at[c, k - 1, :, :, lo:hi], x_peer[k]
                elif p == 1:
                    src = R1.at[c, 0, :, z_of[k], :, lo:hi]
                    dst, peer = R2.at[c, k - 1, :, :, lo:hi], z_peer[k]
                else:
                    src = S1.at[n, 0, z_of[k]]
                    dst, peer = S2.at[n, k - 1], z_peer[k]
                copies.append((src, dst, rsend.at[c, sem], rrecv.at[c, sem], peer))
            send_all((c, 2, p), copies)

    def rs_third(c):
        for p, lo, hi in parts(c):
            received((c, 2, p))
            copies = []
            if p == 2:
                n = WHOLE.index(c)
                total = S1[n, 0, z].astype(F32)
                for k in range(3):
                    total = total + S2[n, k].astype(F32)
                S2[n, 0] = total.astype(BF)
            else:
                if p == 0:
                    total = R1[c, 0, :, x, :, lo:hi].astype(F32)
                else:
                    total = R1[c, 0, :, z, :, lo:hi].astype(F32)
                for k in range(3):
                    total = total + R2[c, k, :, :, lo:hi].astype(F32)
                R2[c, 0, :, :, lo:hi] = total.astype(BF)
            for k in (2, 1, 3):
                sem = 10 * p + 6 + k
                if p == 2:
                    src = S2.at[n, 0, x_of[k]]
                    dst, peer = S3.at[n, k - 1], x_peer[k]
                else:
                    src = R2.at[c, 0, y_of[k] % 2, :, lo:hi]
                    dst, peer = R3.at[c, k - 1, :, lo:hi], y_peer[k]
                copies.append((src, dst, rsend.at[c, sem], rrecv.at[c, sem], peer))
            send_all((c, 3, p), copies)

    def store_share(c, lo, hi, total):
        if c < 4:
            gu_ref[:, WIDTH * c + lo : WIDTH * c + hi] = total[0:12]
        elif c < 7:
            gd_ref[16 * (c - 4) : 16 * (c - 3), lo:hi] = total
        elif c == 7:
            go_ref[:, lo:hi] = total[0:12]
        else:
            start = WIDTH * (lo // TILE) + TILE * (c - 8)
            gi_ref[:, start : start + hi - lo] = total[0:12]

    def rs_fourth(c):
        for p, lo, hi in parts(c):
            received((c, 3, p))
            if p == 2:
                n = WHOLE.index(c)
                total = S2[n, 0, x].astype(F32)
                for k in range(3):
                    total = total + S3[n, k].astype(F32)
                S4[n, 0] = total
                copy = (S4.at[n, 0], S4.at[n, 1], rsend.at[c, 30], rrecv.at[c, 30], partner)
                send_all((c, 4), [copy])
            else:
                total = (R2[c, 0, y_lo, :, lo:hi].astype(F32) + R3[c, 1, :, lo:hi].astype(F32)) + (
                    R3[c, 0, :, lo:hi].astype(F32) + R3[c, 2, :, lo:hi].astype(F32)
                )
                store_share(c, lo, hi, total)

    def rs_end(c):
        if c in WHOLE:
            received((c, 4))
            n = WHOLE.index(c)
            mine = S4[n, 0]
            other = S4[n, 1]
            low = jnp.where(part == 0, mine, other)
            high = jnp.where(part == 0, other, mine)
            store_share(c, 512, 768, jnp.concatenate([low, high], axis=1))

    counts0 = counts_ref[0, 0]
    counts1 = counts_ref[0, 1]
    end0 = lengths_ref[0, 0]
    end1 = end0 + lengths_ref[0, 1]
    end2 = end1 + lengths_ref[0, 2]
    end3 = end2 + lengths_ref[0, 3]

    def used_rows(start, size, width):
        place = lax.broadcasted_iota(jnp.int32, (size, width), 0) + start
        return place < counts0 + part * (counts1 - counts0)

    def features(base, which):
        place = lax.broadcasted_iota(jnp.int32, (ROWS, 128), 0)
        shifted = place + which * counts0
        index = jnp.zeros((ROWS, 128), jnp.int32)
        for end in (end0, end1, end2, end3):
            index = index + jnp.where(end <= shifted, 1, 0)
        owned = counts0 + which * (counts1 - counts0)
        ids = jnp.where(place < owned, index, 4 + which * ROWS + place)
        lane = lax.broadcasted_iota(jnp.int32, (ROWS, 128), 1)
        high = lane >= 64
        spot = jnp.where(high, lane - 64, lane)
        digit = jnp.where(
            spot < 16, ids & 15, jnp.where(spot < 32, ((ids >> 4) & 15) + 16, (ids >> 8) + 32)
        )
        hot = jnp.where(digit == spot, 1.0, 0.0)
        query = jnp.where(spot < FEATURES, 1.0 - hot, 0.0)
        key = hot * -1e30
        MF[base] = jnp.where(high, query, 0.0).astype(BF)
        MF[base + 1] = jnp.where(high, 0.0, query).astype(BF)
        MF[base + 2] = jnp.where(high, key, 0.0).astype(BF)
        MF[base + 3] = jnp.where(high, 0.0, key).astype(BF)

    features(0, part)
    features(4, 1 - part)
    lane_row = lax.broadcasted_iota(jnp.int32, (1, 128), 1)
    select = [
        jnp.where(lane_row < 64, 1.0, 0.0).astype(BF),
        jnp.where(lane_row < 64, 0.0, 1.0).astype(BF),
    ]

    rho = lax.broadcasted_iota(jnp.int32, (ROWS, 384), 0)
    feature = lax.broadcasted_iota(jnp.int32, (ROWS, 384), 1)
    within = rho & 15
    PB[...] = jnp.where(
        (within < 12) & (feature == (rho >> 4) * 12 + within), 1.0, 0.0
    ).astype(BF)

    def padded_transpose(source):
        for b in range(2):
            XT[ROWS * b : ROWS * (b + 1), :] = dot_nt(
                PB[...], source[:, 384 * b : 384 * (b + 1)]
            ).astype(BF)

    def chunk_matmul(c, right):
        def block(m, carry):
            start = pl.multiple_of(m * TILE, TILE)
            out = dot_nn(XT[pl.ds(start, TILE), :], right())
            CH[c % SLOTS, m // 2, pl.ds(2 * (m % 2), 2)] = out.astype(BF).reshape(
                2, 4, 2, 16, WIDTH
            )
            return carry

        lax.fori_loop(0, 4, block, 0)

    ones = jnp.ones((16, ROWS), BF)

    def row_sum(block):
        return dot_nn(ones, block)[0:1]

    def tiles(step):
        def run(t, carry):
            step(pl.ds(pl.multiple_of(t * TILE, TILE), TILE), t * TILE)
            return carry

        lax.fori_loop(0, ROWS // TILE, run, 0)

    qb = qb_ref[...].reshape(1, WIDTH)
    vb = vb_ref[...].reshape(1, WIDTH)
    ob = ob_ref[...].reshape(1, WIDTH)
    fg = fg_ref[...].reshape(1, WIDTH)
    fs = fs_ref[...].reshape(1, WIDTH)
    sg = sg_ref[...].reshape(1, WIDTH)
    ss = ss_ref[...].reshape(1, WIDTH)
    db = db_ref[...].reshape(1, WIDTH)

    def projection(source, q_ref, k_ref, v_ref):
        def step(rows, start):
            unit, _ = norm_parts(source[rows, :].astype(F32))
            normed = (unit * fg + fs).astype(BF)
            q = (dot_nn(normed, W[0]) + qb).astype(BF)
            q_ref[rows, :] = q * jnp.asarray(0.125, BF)
            k_ref[rows, :] = dot_nn(normed, W[1]).astype(BF)
            v_ref[rows, :] = (dot_nn(normed, W[2]) + vb).astype(BF)

        return step

    tok_load.wait()
    for i in range(3):
        w_load[i].wait()
    tiles(projection(TOK, QO, KO, VO))

    cot_load.wait()

    def mask_cot(rows, start):
        used = used_rows(start, TILE, WIDTH)
        COT[rows, :] = jnp.where(used, COT[rows, :].astype(F32), 0.0).astype(BF)

    tiles(mask_cot)

    def pair_cols(hp):
        return pl.ds(pl.multiple_of(hp * 128, 128), 128)

    def mix_at(hp, h):
        start = pl.multiple_of(128 * (hp % 4) + 64 * h, 64)
        return hp // 4, pl.ds(start, 64), slice(0, ROWS)

    def attend_own(hp, carry):
        cols = pair_cols(hp)
        q = QO[:, cols]
        keys = KO[:, cols]
        values = VO[:, cols].T
        for h in range(2):
            row = pl.ds(2 * hp + h, 1)
            scores = dot_nt(keys * select[h] + MF[2 + h], q * select[h] + MF[h])
            top = jnp.max(scores, axis=0, keepdims=True)
            probs = jnp.exp(scores - top)
            TOP[row, :] = top
            SUM[row, :] = jnp.sum(probs, axis=0, keepdims=True)
            own = slice(64 * h, 64 * h + 64)
            ACC[mix_at(hp, h)] = dot_nn(values[own], probs.astype(BF))
        return carry

    lax.fori_loop(0, 6, attend_own, 0)

    def attend_far(r):
        rows = slice(TILE * r, TILE * (r + 1))

        def step(hp, carry):
            cols = pair_cols(hp)
            q = QO[:, cols]
            keys = KF[rows, cols]
            values = VF[rows, cols].T
            outs = []
            for h in range(2):
                row = pl.ds(2 * hp + h, 1)
                own = slice(64 * h, 64 * h + 64)
                scores = dot_nt(keys * select[h] + MF[6 + h, rows], q * select[h] + MF[h])
                before = TOP[row, :]
                top = jnp.maximum(before, jnp.max(scores, axis=0, keepdims=True))
                shrink = jnp.exp(before - top)
                probs = jnp.exp(scores - top)
                total = SUM[row, :] * shrink + jnp.sum(probs, axis=0, keepdims=True)
                mixed = ACC[mix_at(hp, h)] * shrink + dot_nn(values[own], probs.astype(BF))
                if r == 0:
                    TOP[row, :] = top
                    SUM[row, :] = total
                    ACC[mix_at(hp, h)] = mixed
                else:
                    STAT[0, row, :] = top + jnp.log(total)
                    outs.append(mixed * (1.0 / total))
            if r == 1:
                ATT[:, cols] = jnp.concatenate(outs, axis=0).T.astype(BF)
            return carry

        return step

    for r in range(2):
        far_tokens[r].wait_recv()
        projection(FT, QF, KF, VF)(pl.ds(TILE * r, TILE), TILE * r)
        lax.fori_loop(0, 6, attend_far(r), 0)

    w_load[3].wait()

    def out_step(rows, start):
        res = TOK[rows, :].astype(F32) + dot_nn(ATT[rows, :], W[3]) + ob
        RES[rows, :] = res
        unit, _ = norm_parts(res)
        SEC[rows, :] = (unit * sg + ss).astype(BF)
        ACC1[rows, :] = jnp.zeros((TILE, WIDTH), F32)
        ACC2[rows, :] = jnp.zeros((TILE, WIDTH), F32)

    tiles(out_step)
    padded_transpose(SEC)
    VS[0] = jnp.zeros((16, WIDTH), F32)

    for f in range(4):
        slot = f % 2
        for copy in ffn_load[f]:
            copy.wait()
        ub = ub_ref[WIDTH * f : WIDTH * (f + 1)].reshape(1, WIDTH)

        def ffn_step(rows, start, slot=slot, ub=ub):
            dout = COT[rows, :]
            hidden = dot_nn(SEC[rows, :], W[4 + slot]) + ub
            cdf = 0.5 * (1.0 + lax.erf(hidden * 0.7071067811865476))
            density = jnp.exp(-0.5 * hidden * hidden) * 0.3989422804014327
            active = (hidden * cdf).astype(BF)
            ACT[rows, :] = active
            dhidden = (dot_nt(dout, W[6 + slot]) * (cdf + hidden * density)).astype(BF)
            DH[rows, :] = dhidden
            ACC1[rows, :] += dot_nn(active, W[6 + slot])
            ACC2[rows, :] += dot_nt(dhidden, W[4 + slot])

        tiles(ffn_step)
        if f + 2 < 4:
            ffn_load[f + 2] = load_ffn(f + 2)
        chunk_matmul(f, lambda: DH[...])
        rs_core(f)
        VS[0, 8 + f : 9 + f, :] = row_sum(DH[...])

        def down_step(b, carry, f=f):
            cols = pl.ds(pl.multiple_of(b * 384, 384), 384)
            out = dot_tn(ACT[:, cols], COT[...]).astype(BF).reshape(4, 2, 3, 16, WIDTH)
            for k in range(3):
                CH[4 + k, f // 2, 2 * (f % 2) + b] = out[:, :, k]
            return carry

        lax.fori_loop(0, 2, down_step, 0)
        if f >= 1:
            rs_first(f - 1)
        if f >= 2:
            rs_second(f - 2)
        if f >= 3:
            rs_third(f - 3)

    for k in range(3):
        rs_core(4 + k)
    rs_first(3)

    def second_back(rows, start):
        res = RES[rows, :]
        used = used_rows(start, TILE, WIDTH)
        FT[rows, :] = jnp.where(used, res + ACC1[rows, :] + db, 0.0).astype(BF)
        unit, inverse = norm_parts(res)
        dsecond = ACC2[rows, :]
        VS[0, 5:6, :] += jnp.sum(dsecond * unit, axis=0, keepdims=True)
        VS[0, 6:7, :] += jnp.sum(dsecond, axis=0, keepdims=True)
        g = dsecond * sg
        through = (
            g
            - jnp.mean(g, axis=-1, keepdims=True)
            - unit * jnp.mean(g * unit, axis=-1, keepdims=True)
        ) * inverse
        dres = COT[rows, :].astype(F32) + through
        RES[rows, :] = dres
        SEC[rows, :] = dres.astype(BF)
        DH[rows, :] = dot_nt(dres.astype(BF), W[3]).astype(BF)

    tiles(second_back)
    lo_store = load(FT, lo_hbm, iosem.at[2])
    far_dout = []
    for r in range(2):
        half = pl.ds(384 * r, 384)
        far_dout.append(
            remote(DH.at[:, half], FDO.at[:, half], xsend.at[2 + r], xrecv.at[2 + r], partner)
        )
    for k in range(3):
        rs_first(4 + k)
    VS[0, 7:8, :] = row_sum(COT[...])
    VS[0, 2:3, :] = row_sum(SEC[...])

    head = lax.broadcasted_iota(jnp.int32, (16, WIDTH), 0)
    column = lax.broadcasted_iota(jnp.int32, (16, WIDTH), 1)
    in_head = jnp.where((column >> 6) == head, 1.0, 0.0).astype(BF)
    product = DH[...].astype(F32) * ATT[...].astype(F32)
    rough = product.astype(BF)
    STAT[1] = dot_nt(in_head, rough) + dot_nt(in_head, (product - rough.astype(F32)).astype(BF))
    far_stats = remote(STAT, FSTAT, xsend.at[4], xrecv.at[4], partner)
    rs_second(2)

    padded_transpose(ATT)
    sent[0, 0][0].wait_send()
    chunk_matmul(7, lambda: SEC[...])
    rs_core(7)
    rs_second(3)
    rs_third(1)
    rs_fourth(0)

    def own_queries(hp, carry):
        cols = pair_cols(hp)
        q = QO[:, cols]
        ko = KO[:, cols]
        kf = KF[:, cols]
        vo = VO[:, cols]
        vf = VF[:, cols]
        do = DH[:, cols]
        ko_t = ko.T
        kf_t = kf.T
        dq = []
        dk = None
        for h in range(2):
            logsum = STAT[0, pl.ds(2 * hp + h, 1), :]
            delta = STAT[1, pl.ds(2 * hp + h, 1), :]
            qm = q * select[h] + MF[h]
            qs = q * select[h]
            dom = do * select[h]
            near = jnp.exp(dot_nt(ko * select[h] + MF[2 + h], qm) - logsum)
            dnear = (near * (dot_nt(vo, dom) - delta)).astype(BF)
            far = jnp.exp(dot_nt(kf * select[h] + MF[6 + h], qm) - logsum)
            dfar = (far * (dot_nt(vf, dom) - delta)).astype(BF)
            dq.append(
                dot_nn(ko_t[64 * h : 64 * h + 64], dnear)
                + dot_nn(kf_t[64 * h : 64 * h + 64], dfar)
            )
            dk_h = dot_nn(dnear, qs)
            dv_h = dot_nn(near.astype(BF), dom)
            dk, dv = (dk_h, dv_h) if dk is None else (dk + dk_h, dv + dv_h)
        ACC1[:, cols] = dk
        ACC2[:, cols] = dv
        QO[:, cols] = (jnp.concatenate(dq, axis=0).T * 0.125).astype(BF)
        return carry

    lax.fori_loop(0, 2, own_queries, 0)
    rs_first(7)
    for k in range(3):
        rs_second(4 + k)
    rs_third(2)
    rs_fourth(1)
    rs_end(0)
    lax.fori_loop(2, 4, own_queries, 0)
    rs_third(3)
    for k in range(3):
        rs_third(4 + k)
    rs_fourth(2)
    rs_end(1)
    lax.fori_loop(4, 6, own_queries, 0)
    rs_second(7)
    for c in (3, 4, 5, 6):
        rs_fourth(c)
    rs_end(2)

    def again(rows, start):
        unit, _ = norm_parts(TOK[rows, :].astype(F32))
        ATT[rows, :] = (unit * fg + fs).astype(BF)

    tiles(again)
    padded_transpose(ATT)

    far_stats.wait_recv()

    def far_queries(hp, carry):
        cols = pair_cols(hp)
        q = QF[:, cols]
        ko = KO[:, cols]
        vo = VO[:, cols]
        do = FDO[:, cols]
        dk = ACC1[:, cols]
        dv = ACC2[:, cols]
        for h in range(2):
            logsum = FSTAT[0, pl.ds(2 * hp + h, 1), :]
            delta = FSTAT[1, pl.ds(2 * hp + h, 1), :]
            qs = q * select[h]
            dom = do * select[h]
            probs = jnp.exp(dot_nt(ko * select[h] + MF[2 + h], qs + MF[4 + h]) - logsum)
            dscores = (probs * (dot_nt(vo, dom) - delta)).astype(BF)
            dk = dk + dot_nn(dscores, qs)
            dv = dv + dot_nn(probs.astype(BF), dom)
        KO[:, cols] = dk.astype(BF)
        VO[:, cols] = dv.astype(BF)
        return carry

    for j in range(3):
        c = 8 + j
        if j < 2:
            far_dout[j].wait_recv()
        lax.fori_loop(2 * j, 2 * j + 2, far_queries, 0)
        sent[c - 7, 0][0].wait_send()
        cols = slice(TILE * j, TILE * (j + 1))

        def joined(cols=cols):
            return jnp.concatenate([QO[:, cols], KO[:, cols], VO[:, cols]], axis=1)

        chunk_matmul(c, joined)
        rs_core(c)
        if j == 0:
            rs_third(7)
            rs_end(3)
        if j == 1:
            rs_first(8)
            rs_fourth(7)
        if j == 2:
            rs_first(9)
            rs_second(8)

    VS[0, 0:1, :] = row_sum(QO[...])
    VS[0, 1:2, :] = row_sum(VO[...])

    def first_back(rows, start):
        unit, inverse = norm_parts(TOK[rows, :].astype(F32))
        dnormed = (
            dot_nt(QO[rows, :], W[0]) + dot_nt(KO[rows, :], W[1]) + dot_nt(VO[rows, :], W[2])
        )
        VS[0, 3:4, :] += jnp.sum(dnormed * unit, axis=0, keepdims=True)
        VS[0, 4:5, :] += jnp.sum(dnormed, axis=0, keepdims=True)
        g = dnormed * fg
        through = (
            g
            - jnp.mean(g, axis=-1, keepdims=True)
            - unit * jnp.mean(g * unit, axis=-1, keepdims=True)
        ) * inverse
        TOK[rows, :] = (RES[rows, :] + through).astype(BF)

    for copy in far_tokens:
        copy.wait_send()
    tiles(first_back)
    gt_store = load(TOK, gt_hbm, iosem.at[3])

    vsent = []

    def vec_send(step, peers, base):
        vsent.append(
            [
                remote(VS.at[step], VR.at[base + i], vsend.at[base + i], vrecv.at[base + i], peer)
                for i, peer in enumerate(peers)
            ]
        )

    def vec_add(step, base):
        for copy in vsent[step]:
            copy.wait_recv()
        if step == 0:
            total = VS[0] + VR[0]
        else:
            total = (VS[step] + VR[base + 1]) + (VR[base] + VR[base + 2])
        VS[step + 1] = total

    vec_send(0, [sibling], 0)
    rs_first(10)
    rs_second(9)
    rs_third(8)
    vec_add(0, 0)
    vec_send(1, z_peer[1:], 1)
    rs_second(10)
    rs_third(9)
    rs_fourth(8)
    vec_add(1, 1)
    vec_send(2, x_peer[1:], 4)
    rs_third(10)
    rs_fourth(9)
    rs_end(8)
    vec_add(2, 4)
    vec_send(3, y_peer[1:], 7)
    rs_fourth(10)
    rs_end(9)
    vec_add(3, 7)
    rs_end(10)

    spot = lax.broadcasted_iota(jnp.int32, (WIDTH, 128), 0)
    lane = lax.broadcasted_iota(jnp.int32, (WIDTH, 128), 1)
    narrow = jnp.where((lane < 12) & (spot == lane + 12 * dp), 1.0, 0.0)
    wide = jnp.where((lane < 48) & (spot == lane + 48 * (dp % 16)), 1.0, 0.0)
    vectors = VS[4]
    exact = dict(precision=lax.Precision.HIGHEST, preferred_element_type=F32)
    small = jnp.dot(vectors, narrow, **exact)
    large = jnp.dot(vectors, wide, **exact)
    row = lax.broadcasted_iota(jnp.int32, (16, 128), 0)
    large = jnp.sum(jnp.where(row == 8 + dp // 16, large, 0.0), axis=0, keepdims=True)
    for i, ref in enumerate(
        (gqb_ref, gvb_ref, gob_ref, gfg_ref, gfs_ref, gsg_ref, gss_ref, gdb_ref)
    ):
        ref[...] = small[i : i + 1, 0:12].reshape(12)
    gub_ref[...] = large[:, 0:48].reshape(48)

    for copy in far_dout:
        copy.wait_send()
    far_stats.wait_send()
    for key in sent:
        if key[1] or key[0] > 3:
            for copy in sent[key]:
                copy.wait_send()
    for copies in vsent:
        for copy in copies:
            copy.wait_send()
    lo_store.wait()
    gt_store.wait()


def finish(*refs):
    count = len(refs) // 2
    for i in range(count):
        refs[count + i][...] = refs[i][...]


def body(
    tokens,
    input_weight,
    query_bias,
    value_bias,
    out_weight,
    out_bias,
    first_gain,
    first_shift,
    second_gain,
    second_shift,
    up_weight,
    up_bias,
    down_weight,
    down_bias,
    cotangent,
    row_counts,
    image_lengths,
):
    hbm = pl.BlockSpec(memory_space=pl.ANY)
    vmem = pl.BlockSpec(memory_space=pltpu.VMEM)
    smem = pl.BlockSpec(memory_space=pltpu.SMEM)
    rows = jax.ShapeDtypeStruct((ROWS, WIDTH), BF)

    def f32(*shape):
        return jax.ShapeDtypeStruct(shape, F32)

    def block(kind, *lead):
        return pltpu.VMEM((*lead, ROWS, WIDTH), kind)

    out = pl.pallas_call(
        kernel,
        out_shape=(
            rows,
            rows,
            f32(12, 3 * WIDTH),
            f32(12),
            f32(12),
            f32(12, WIDTH),
            f32(12),
            f32(12),
            f32(12),
            f32(12),
            f32(12),
            f32(12, 4 * WIDTH),
            f32(48),
            f32(48, WIDTH),
            f32(12),
        ),
        in_specs=[smem, smem] + [hbm] * 6 + [vmem] * 9,
        out_specs=(hbm, hbm) + (vmem,) * 13,
        scratch_shapes=[
            pltpu.VMEM((8, WIDTH, WIDTH), BF),
            pltpu.VMEM((SLOTS, 2, 4, 4, 2, 16, WIDTH), BF),
            pltpu.VMEM((CHUNKS, 2, 4, 4, 16, WIDTH), BF),
            pltpu.VMEM((CHUNKS, 3, 2, 4, 16, WIDTH), BF),
            pltpu.VMEM((CHUNKS, 3, 2, 16, WIDTH), BF),
            pltpu.VMEM((CHUNKS, 3, 16, WIDTH), BF),
            pltpu.VMEM((len(WHOLE), 3, 4, 4, 16, 128), BF),
            pltpu.VMEM((len(WHOLE), 3, 4, 16, 128), BF),
            pltpu.VMEM((len(WHOLE), 3, 16, 128), BF),
            pltpu.VMEM((len(WHOLE), 2, 16, 128), F32),
            block(BF),
            block(BF),
            pltpu.VMEM((2, 16, ROWS), F32),
            pltpu.VMEM((2, 16, ROWS), F32),
        ]
        + [block(BF)] * 12
        + [
            pltpu.VMEM((1024, ROWS), BF),
            block(F32),
            block(F32, 2),
            pltpu.VMEM((8, ROWS, 128), BF),
            pltpu.VMEM((ROWS, 384), BF),
            pltpu.VMEM((16, ROWS), F32),
            pltpu.VMEM((16, ROWS), F32),
            pltpu.VMEM((5, 16, WIDTH), F32),
            pltpu.VMEM((10, 16, WIDTH), F32),
            pltpu.SemaphoreType.DMA((8,)),
            pltpu.SemaphoreType.DMA((4,)),
            pltpu.SemaphoreType.DMA((5,)),
            pltpu.SemaphoreType.DMA((5,)),
            pltpu.SemaphoreType.DMA((CHUNKS, 31)),
            pltpu.SemaphoreType.DMA((CHUNKS, 31)),
            pltpu.SemaphoreType.DMA((10,)),
            pltpu.SemaphoreType.DMA((10,)),
        ],
        compiler_params=pltpu.CompilerParams(
            collective_id=0, has_side_effects=True, vmem_limit_bytes=63 * 2**20
        ),
        name="encoder",
    )(
        row_counts,
        image_lengths,
        tokens,
        cotangent,
        input_weight,
        out_weight,
        up_weight,
        down_weight,
        query_bias,
        value_bias,
        out_bias,
        first_gain,
        first_shift,
        second_gain,
        second_shift,
        up_bias,
        down_bias,
    )
    return pl.pallas_call(
        finish,
        out_shape=tuple(jax.ShapeDtypeStruct(value.shape, value.dtype) for value in out),
        in_specs=[vmem] * len(out),
        out_specs=(vmem,) * len(out),
        name="finish",
    )(*out)


def solution(mesh):
    rows = P(("seq", "dp"), None)
    split = P("dp", None)
    line = P("dp")
    return jax.shard_map(
        body,
        mesh=mesh,
        in_specs=(rows,) + (P(),) * 13 + (rows, split, split),
        out_specs=(
            rows,
            rows,
            split,
            line,
            line,
            split,
            line,
            line,
            line,
            line,
            line,
            split,
            line,
            split,
            line,
        ),
        check_vma=False,
    )
```

```python
import jax
import jax.numpy as jnp
from jax import lax
from jax.experimental import pallas as pl
from jax.experimental.pallas import tpu as pltpu
from jax.sharding import PartitionSpec as P

F32 = jnp.float32
BF = jnp.bfloat16
EPS = 1e-06
ROWS = 512
WIDTH = 768
TILE = 256
CHUNKS = 11
SLOTS = 7
FEATURES = 37
PARTS = (
    ((2, 0, 768),),
    ((0, 0, 768),),
    ((1, 0, 768),),
    ((0, 0, 768),),
    ((1, 0, 768),),
    ((0, 0, 768),),
    ((1, 0, 768),),
    ((0, 0, 768),),
    ((1, 0, 768),),
    ((0, 0, 768),),
    ((0, 0, 256), (1, 256, 512), (2, 512, 768)),
)
Y_FIRST = (0, 10)
STEPS = [(c, 0, 0) for c in range(CHUNKS)]
STEPS += [(c, s, p) for c in range(CHUNKS) for p, _, _ in PARTS[c] for s in (1, 2, 3)]
STEPS += [(c, 4, 2) for c in Y_FIRST]
STEPS += [(c, 5, p) for c in range(CHUNKS) for p, _, _ in PARTS[c] if p < 2]
MESH = pl.DeviceIdType.MESH


def dot_nn(left, right):
    return lax.dot_general(left, right, (((1,), (0,)), ((), ())), preferred_element_type=F32)


def dot_nt(left, right):
    return lax.dot_general(left, right, (((1,), (1,)), ((), ())), preferred_element_type=F32)


def dot_tn(left, right):
    return lax.dot_general(left, right, (((0,), (0,)), ((), ())), preferred_element_type=F32)


def norm_parts(block):
    centred = block - jnp.mean(block, axis=-1, keepdims=True)
    spread = jnp.mean(centred * centred, axis=-1, keepdims=True)
    inverse = lax.rsqrt(spread + EPS)
    return centred * inverse, inverse


def kernel(
    counts_ref,
    lengths_ref,
    tokens_hbm,
    cot_hbm,
    wi_hbm,
    wo_hbm,
    wu_hbm,
    wd_hbm,
    qb_ref,
    vb_ref,
    ob_ref,
    fg_ref,
    fs_ref,
    sg_ref,
    ss_ref,
    ub_ref,
    db_ref,
    lo_hbm,
    gt_hbm,
    gi_ref,
    gqb_ref,
    gvb_ref,
    go_ref,
    gob_ref,
    gfg_ref,
    gfs_ref,
    gsg_ref,
    gss_ref,
    gu_ref,
    gub_ref,
    gd_ref,
    gdb_ref,
    W,
    CH,
    R0,
    R1,
    R2,
    R3,
    S1,
    S2,
    S3,
    S4,
    FT,
    FDO,
    STAT,
    FSTAT,
    QO,
    KO,
    VO,
    QF,
    KF,
    VF,
    TOK,
    COT,
    ATT,
    SEC,
    ACT,
    DH,
    XT,
    RES,
    ACC,
    MF,
    PB,
    TOP,
    SUM,
    VS,
    VR,
    wsem,
    iosem,
    xsend,
    xrecv,
    rsend,
    rrecv,
    vsend,
    vrecv,
):
    ACC1, ACC2 = ACC.at[0], ACC.at[1]
    part = lax.axis_index("seq")
    dp = lax.axis_index("dp")
    y_lo = dp // 32
    z = (dp // 8) % 4
    x = (dp // 2) % 4
    core = dp % 2
    y = 2 * part + y_lo

    def device(yy, zz, xx, cc):
        return (yy // 2, ((yy % 2) * 4 + zz) * 8 + xx * 2 + cc)

    sibling = device(y, z, x, 1 - core)
    z_of = [(z + k) % 4 for k in range(4)]
    x_of = [(x + k) % 4 for k in range(4)]
    y_of = [(y + k) % 4 for k in range(4)]
    z_a, z_b = z + 1 - 2 * (z % 2), 3 - z
    x_a, x_b = x + 1 - 2 * (x % 2), 3 - x
    near_z = [device(y, v, x, core) for v in (z_a, z_b)]
    near_x = [device(y, z, v, core) for v in (x_a, x_b)]
    z_peer = [device(y, v, x, core) for v in z_of]
    x_peer = [device(y, z, v, core) for v in x_of]
    y_peer = [device(v, z, x, core) for v in y_of]
    partner = y_peer[2]

    def load(src, dst, sem):
        copy = pltpu.make_async_copy(src, dst, sem)
        copy.start()
        return copy

    tok_load = load(tokens_hbm, TOK, iosem.at[0])
    w_load = {}
    for i in range(3):
        w_load[i] = load(wi_hbm.at[:, pl.ds(WIDTH * i, WIDTH)], W.at[i], wsem.at[i])
    cot_load = load(cot_hbm, COT, iosem.at[1])
    w_load[3] = load(wo_hbm, W.at[3], wsem.at[3])

    def load_ffn(f):
        slot = f % 2
        up = load(wu_hbm.at[:, pl.ds(WIDTH * f, WIDTH)], W.at[4 + slot], wsem.at[4 + slot])
        down = load(wd_hbm.at[pl.ds(WIDTH * f, WIDTH)], W.at[6 + slot], wsem.at[6 + slot])
        return up, down

    ffn_load = {0: load_ffn(0), 1: load_ffn(1)}

    barrier = pltpu.get_barrier_semaphore()
    for peer in [sibling] + z_peer[1:] + x_peer[1:] + y_peer[1:]:
        pl.semaphore_signal(barrier, inc=1, device_id=peer, device_id_type=MESH)
    pl.semaphore_wait(barrier, 10)

    def remote(src, dst, send, recv, peer):
        copy = pltpu.make_async_remote_copy(
            src_ref=src,
            dst_ref=dst,
            send_sem=send,
            recv_sem=recv,
            device_id=peer,
            device_id_type=MESH,
        )
        copy.start()
        return copy

    far_tokens = []
    for r in range(2):
        half = pl.ds(TILE * r, TILE)
        far_tokens.append(
            remote(tokens_hbm.at[half], FT.at[half], xsend.at[r], xrecv.at[r], partner)
        )

    def all_bytes(ref, sem):
        pltpu.make_async_copy(ref, ref, sem).wait()

    landing = {}

    def send_all(key, dst, copies):
        i = STEPS.index(key)
        landing[key] = dst
        for src, into, peer in copies:
            remote(src, into, rsend.at[i], rrecv.at[i], peer)

    def received(key):
        all_bytes(landing[key], rrecv.at[STEPS.index(key)])

    def gone(key):
        all_bytes(landing.pop(key), rsend.at[STEPS.index(key)])

    def rs_core(c):
        src = CH.at[c % SLOTS, :, :, :, 1 - core]
        send_all((c, 0, 0), R0.at[c], [(src, R0.at[c], sibling)])

    def y_slot(c):
        n = Y_FIRST.index(c)
        return n, 384 if n == 0 else 128

    def rs_first(c):
        received((c, 0, 0))

        def add(i, carry):
            yl, zz = i // 4, i % 4
            R0[c, yl, zz] = (
                R0[c, yl, zz].astype(F32) + CH[c % SLOTS, yl, zz, :, core].astype(F32)
            ).astype(BF)
            return carry

        lax.fori_loop(0, 8, add, 0)
        for p, lo, hi in PARTS[c]:
            copies = []
            if p == 2:
                n, width = y_slot(c)
                whole = S1.at[n, :, :, :, :, 0:width]
                for k in (2, 1, 3):
                    start = pl.multiple_of(lo + width * (y_of[k] // 2), 128)
                    src = R0.at[c, y_of[k] % 2, :, :, :, pl.ds(start, width)]
                    copies.append((src, S1.at[n, k - 1, :, :, :, 0:width], y_peer[k]))
            else:
                whole = R1.at[c, 0:2, :, :, :, lo:hi]
                a, b = (z_a, z_b) if p == 0 else (x_a, x_b)
                across = 3 - a
                peers = near_z if p == 0 else near_x
                for half, nearest in ((0, a), (1, b)):
                    for spot, wanted in ((1, across), (0, nearest)):
                        dst = R1.at[c, half, spot, :, :, lo:hi]
                        copies.append((shares(c, p, half, wanted, lo, hi), dst, peers[half]))
            send_all((c, 1, p), whole, copies)

    def shares(c, p, yl, v, lo, hi):
        if p == 0:
            return R0.at[c, yl, v, :, :, lo:hi]
        return R0.at[c, yl, :, v, :, lo:hi]

    def rs_mid(c):
        for p, lo, hi in PARTS[c]:
            if p == 2:
                continue
            received((c, 1, p))
            v, a, b = (z, z_a, z_b) if p == 0 else (x, x_a, x_b)
            for half, other in ((0, b), (1, a)):
                for spot, kept in ((0, v), (1, other)):
                    at = (c, half, spot, slice(None), slice(None), slice(lo, hi))
                    own = shares(c, p, half, kept, lo, hi)[...]
                    R1[at] = (own.astype(F32) + R1[at].astype(F32)).astype(BF)
            peers = near_z if p == 0 else near_x
            copies = []
            for half in range(2):
                src = R1.at[c, half, 1, :, :, lo:hi]
                copies.append((src, R1.at[c, 2, half, :, :, lo:hi], peers[1 - half]))
            send_all((c, 5, p), R1.at[c, 2, :, :, :, lo:hi], copies)

    def rs_second(c):
        for p, lo, hi in PARTS[c]:
            received((c, 1 if p == 2 else 5, p))
            copies = []
            if p == 2:
                n, width = y_slot(c)
                start = pl.multiple_of(lo + width * part, 128)
                for zz in range(4):
                    total = R0[c, y_lo, zz, :, :, pl.ds(start, width)].astype(F32)
                    for k in range(3):
                        total = total + S1[n, k, zz, :, :, 0:width].astype(F32)
                    S1[n, 0, zz, :, :, 0:width] = total.astype(BF)
                whole = S2.at[n, :, :, :, 0:width]
            else:
                for half in range(2):
                    at = (c, half, 0, slice(None), slice(None), slice(lo, hi))
                    total = R1[at].astype(F32) + R1[c, 2, half, :, :, lo:hi].astype(F32)
                    R1[at] = total.astype(BF)
                whole = R2.at[c, :, :, :, lo:hi]
            for k in (2, 1, 3):
                if p == 0:
                    src = R1.at[c, 0:2, 0, x_of[k], :, lo:hi]
                    dst, peer = R2.at[c, k - 1, :, :, lo:hi], x_peer[k]
                elif p == 1:
                    src = R1.at[c, 0:2, 0, z_of[k], :, lo:hi]
                    dst, peer = R2.at[c, k - 1, :, :, lo:hi], z_peer[k]
                else:
                    src = S1.at[n, 0, z_of[k], :, :, 0:width]
                    dst, peer = S2.at[n, k - 1, :, :, 0:width], z_peer[k]
                copies.append((src, dst, peer))
            send_all((c, 2, p), whole, copies)

    def rs_third(c):
        for p, lo, hi in PARTS[c]:
            received((c, 2, p))
            copies = []
            if p == 2:
                n, width = y_slot(c)
                total = S1[n, 0, z, :, :, 0:width].astype(F32)
                for k in range(3):
                    total = total + S2[n, k, :, :, 0:width].astype(F32)
                S2[n, 0, :, :, 0:width] = total.astype(BF)
                whole = S3.at[n, :, :, 0:width]
            else:
                if p == 0:
                    total = R1[c, 0:2, 0, x, :, lo:hi].astype(F32)
                else:
                    total = R1[c, 0:2, 0, z, :, lo:hi].astype(F32)
                for k in range(3):
                    total = total + R2[c, k, :, :, lo:hi].astype(F32)
                R2[c, 0, :, :, lo:hi] = total.astype(BF)
                whole = R3.at[c, :, :, lo:hi]
            for k in (2, 1, 3):
                if p == 2:
                    src = S2.at[n, 0, x_of[k], :, 0:width]
                    dst, peer = S3.at[n, k - 1, :, 0:width], x_peer[k]
                else:
                    src = R2.at[c, 0, y_of[k] % 2, :, lo:hi]
                    dst, peer = R3.at[c, k - 1, :, lo:hi], y_peer[k]
                copies.append((src, dst, peer))
            send_all((c, 3, p), whole, copies)

    def store_share(c, lo, hi, total):
        if c < 4:
            gu_ref[:, WIDTH * c + lo : WIDTH * c + hi] = total[0:12]
        elif c < 7:
            gd_ref[16 * (c - 4) : 16 * (c - 3), lo:hi] = total
        elif c == 7:
            go_ref[:, lo:hi] = total[0:12]
        else:
            for b in range(lo // TILE, hi // TILE):
                start = WIDTH * b + TILE * (c - 8)
                gi_ref[:, start : start + TILE] = total[0:12, TILE * b - lo : TILE * (b + 1) - lo]

    def rs_fourth(c):
        for p, lo, hi in PARTS[c]:
            received((c, 3, p))
            if p == 2:
                n, width = y_slot(c)
                total = S2[n, 0, x, :, 0:width].astype(F32)
                for k in range(3):
                    total = total + S3[n, k, :, 0:width].astype(F32)
                S4[n, 0, :, 0:width] = total
                dst = S4.at[n, 1, :, 0:width]
                send_all((c, 4, p), dst, [(S4.at[n, 0, :, 0:width], dst, partner)])
            else:
                total = (R2[c, 0, y_lo, :, lo:hi].astype(F32) + R3[c, 1, :, lo:hi].astype(F32)) + (
                    R3[c, 0, :, lo:hi].astype(F32) + R3[c, 2, :, lo:hi].astype(F32)
                )
                store_share(c, lo, hi, total)

    def rs_end(c):
        n, width = y_slot(c)
        received((c, 4, 2))
        mine = S4[n, 0, :, 0:width]
        other = S4[n, 1, :, 0:width]
        low = jnp.where(part == 0, mine, other)
        high = jnp.where(part == 0, other, mine)
        lo = PARTS[c][-1][1]
        store_share(c, lo, lo + 2 * width, jnp.concatenate([low, high], axis=1))

    counts0 = counts_ref[0, 0]
    counts1 = counts_ref[0, 1]
    end0 = lengths_ref[0, 0]
    end1 = end0 + lengths_ref[0, 1]
    end2 = end1 + lengths_ref[0, 2]
    end3 = end2 + lengths_ref[0, 3]

    def used_rows(start, size, width):
        place = lax.broadcasted_iota(jnp.int32, (size, width), 0) + start
        return place < counts0 + part * (counts1 - counts0)

    def features(base, which):
        place = lax.broadcasted_iota(jnp.int32, (ROWS, 128), 0)
        shifted = place + which * counts0
        index = jnp.zeros((ROWS, 128), jnp.int32)
        for end in (end0, end1, end2, end3):
            index = index + jnp.where(end <= shifted, 1, 0)
        owned = counts0 + which * (counts1 - counts0)
        ids = jnp.where(place < owned, index, 4 + which * ROWS + place)
        lane = lax.broadcasted_iota(jnp.int32, (ROWS, 128), 1)
        high = lane >= 64
        spot = jnp.where(high, lane - 64, lane)
        digit = jnp.where(
            spot < 16, ids & 15, jnp.where(spot < 32, ((ids >> 4) & 15) + 16, (ids >> 8) + 32)
        )
        hot = jnp.where(digit == spot, 1.0, 0.0)
        query = jnp.where(spot < FEATURES, 1.0 - hot, 0.0)
        key = hot * -1e30
        MF[base] = jnp.where(high, query, 0.0).astype(BF)
        MF[base + 1] = jnp.where(high, 0.0, query).astype(BF)
        MF[base + 2] = jnp.where(high, key, 0.0).astype(BF)
        MF[base + 3] = jnp.where(high, 0.0, key).astype(BF)

    features(0, part)
    features(4, 1 - part)
    lane_row = lax.broadcasted_iota(jnp.int32, (1, 128), 1)
    select = [
        jnp.where(lane_row < 64, 1.0, 0.0).astype(BF),
        jnp.where(lane_row < 64, 0.0, 1.0).astype(BF),
    ]

    rho = lax.broadcasted_iota(jnp.int32, (ROWS, 384), 0)
    feature = lax.broadcasted_iota(jnp.int32, (ROWS, 384), 1)
    within = rho & 15
    PB[...] = jnp.where(
        (within < 12) & (feature == (rho >> 4) * 12 + within), 1.0, 0.0
    ).astype(BF)

    def padded_transpose(source):
        for b in range(2):
            XT[ROWS * b : ROWS * (b + 1), :] = dot_nt(
                PB[...], source[:, 384 * b : 384 * (b + 1)]
            ).astype(BF)

    def chunk_matmul(c, right):
        def block(m, carry):
            start = pl.multiple_of(m * TILE, TILE)
            out = dot_nn(XT[pl.ds(start, TILE), :], right())
            CH[c % SLOTS, m // 2, pl.ds(2 * (m % 2), 2)] = out.astype(BF).reshape(
                2, 4, 2, 16, WIDTH
            )
            return carry

        lax.fori_loop(0, 4, block, 0)

    ones = jnp.ones((16, ROWS), BF)

    def row_sum(block):
        return dot_nn(ones, block)[0:1]

    def tiles(step):
        def run(t, carry):
            step(pl.ds(pl.multiple_of(t * TILE, TILE), TILE), t * TILE)
            return carry

        lax.fori_loop(0, ROWS // TILE, run, 0)

    qb = qb_ref[...].reshape(1, WIDTH)
    vb = vb_ref[...].reshape(1, WIDTH)
    ob = ob_ref[...].reshape(1, WIDTH)
    fg = fg_ref[...].reshape(1, WIDTH)
    fs = fs_ref[...].reshape(1, WIDTH)
    sg = sg_ref[...].reshape(1, WIDTH)
    ss = ss_ref[...].reshape(1, WIDTH)
    db = db_ref[...].reshape(1, WIDTH)

    def projection(source, q_ref, k_ref, v_ref):
        def step(rows, start):
            unit, _ = norm_parts(source[rows, :].astype(F32))
            normed = (unit * fg + fs).astype(BF)
            q = (dot_nn(normed, W[0]) + qb).astype(BF)
            q_ref[rows, :] = q * jnp.asarray(0.125, BF)
            k_ref[rows, :] = dot_nn(normed, W[1]).astype(BF)
            v_ref[rows, :] = (dot_nn(normed, W[2]) + vb).astype(BF)

        return step

    tok_load.wait()
    for i in range(3):
        w_load[i].wait()
    tiles(projection(TOK, QO, KO, VO))

    cot_load.wait()

    def mask_cot(rows, start):
        used = used_rows(start, TILE, WIDTH)
        COT[rows, :] = jnp.where(used, COT[rows, :].astype(F32), 0.0).astype(BF)

    tiles(mask_cot)

    def pair_cols(hp):
        return pl.ds(pl.multiple_of(hp * 128, 128), 128)

    def mix_at(hp, h):
        start = pl.multiple_of(128 * (hp % 4) + 64 * h, 64)
        return hp // 4, pl.ds(start, 64), slice(0, ROWS)

    def attend_own(hp, carry):
        cols = pair_cols(hp)
        q = QO[:, cols]
        keys = KO[:, cols]
        values = VO[:, cols].T
        for h in range(2):
            row = pl.ds(2 * hp + h, 1)
            scores = dot_nt(keys * select[h] + MF[2 + h], q * select[h] + MF[h])
            top = jnp.max(scores, axis=0, keepdims=True)
            probs = jnp.exp(scores - top)
            TOP[row, :] = top
            SUM[row, :] = jnp.sum(probs, axis=0, keepdims=True)
            own = slice(64 * h, 64 * h + 64)
            ACC[mix_at(hp, h)] = dot_nn(values[own], probs.astype(BF))
        return carry

    lax.fori_loop(0, 6, attend_own, 0)

    def attend_far(r):
        rows = slice(TILE * r, TILE * (r + 1))

        def step(hp, carry):
            cols = pair_cols(hp)
            q = QO[:, cols]
            keys = KF[rows, cols]
            values = VF[rows, cols].T
            outs = []
            for h in range(2):
                row = pl.ds(2 * hp + h, 1)
                own = slice(64 * h, 64 * h + 64)
                scores = dot_nt(keys * select[h] + MF[6 + h, rows], q * select[h] + MF[h])
                before = TOP[row, :]
                top = jnp.maximum(before, jnp.max(scores, axis=0, keepdims=True))
                shrink = jnp.exp(before - top)
                probs = jnp.exp(scores - top)
                total = SUM[row, :] * shrink + jnp.sum(probs, axis=0, keepdims=True)
                mixed = ACC[mix_at(hp, h)] * shrink + dot_nn(values[own], probs.astype(BF))
                if r == 0:
                    TOP[row, :] = top
                    SUM[row, :] = total
                    ACC[mix_at(hp, h)] = mixed
                else:
                    STAT[0, row, :] = top + jnp.log(total)
                    outs.append(mixed * (1.0 / total))
            if r == 1:
                ATT[:, cols] = jnp.concatenate(outs, axis=0).T.astype(BF)
            return carry

        return step

    for r in range(2):
        far_tokens[r].wait_recv()
        projection(FT, QF, KF, VF)(pl.ds(TILE * r, TILE), TILE * r)
        lax.fori_loop(0, 6, attend_far(r), 0)

    w_load[3].wait()

    def out_step(rows, start):
        res = TOK[rows, :].astype(F32) + dot_nn(ATT[rows, :], W[3]) + ob
        RES[rows, :] = res
        unit, _ = norm_parts(res)
        SEC[rows, :] = (unit * sg + ss).astype(BF)
        ACC1[rows, :] = jnp.zeros((TILE, WIDTH), F32)
        ACC2[rows, :] = jnp.zeros((TILE, WIDTH), F32)

    tiles(out_step)
    padded_transpose(SEC)
    VS[0] = jnp.zeros((16, WIDTH), F32)

    for f in range(4):
        slot = f % 2
        for copy in ffn_load[f]:
            copy.wait()
        ub = ub_ref[WIDTH * f : WIDTH * (f + 1)].reshape(1, WIDTH)

        def ffn_step(rows, start, slot=slot, ub=ub):
            dout = COT[rows, :]
            hidden = dot_nn(SEC[rows, :], W[4 + slot]) + ub
            cdf = 0.5 * (1.0 + lax.erf(hidden * 0.7071067811865476))
            density = jnp.exp(-0.5 * hidden * hidden) * 0.3989422804014327
            active = (hidden * cdf).astype(BF)
            ACT[rows, :] = active
            dhidden = (dot_nt(dout, W[6 + slot]) * (cdf + hidden * density)).astype(BF)
            DH[rows, :] = dhidden
            ACC1[rows, :] += dot_nn(active, W[6 + slot])
            ACC2[rows, :] += dot_nt(dhidden, W[4 + slot])

        tiles(ffn_step)
        if f + 2 < 4:
            ffn_load[f + 2] = load_ffn(f + 2)
        chunk_matmul(f, lambda: DH[...])
        rs_core(f)
        VS[0, 8 + f : 9 + f, :] = row_sum(DH[...])

        def down_step(b, carry, f=f):
            cols = pl.ds(pl.multiple_of(b * 384, 384), 384)
            out = dot_tn(ACT[:, cols], COT[...]).astype(BF).reshape(4, 2, 3, 16, WIDTH)
            for k in range(3):
                CH[4 + k, f // 2, 2 * (f % 2) + b] = out[:, :, k]
            return carry

        lax.fori_loop(0, 2, down_step, 0)
        if f >= 1:
            rs_first(f - 1)

    rs_mid(1)
    for k in range(3):
        rs_core(4 + k)

    def second_back(rows, start):
        res = RES[rows, :]
        used = used_rows(start, TILE, WIDTH)
        FT[rows, :] = jnp.where(used, res + ACC1[rows, :] + db, 0.0).astype(BF)
        unit, inverse = norm_parts(res)
        dsecond = ACC2[rows, :]
        VS[0, 5:6, :] += jnp.sum(dsecond * unit, axis=0, keepdims=True)
        VS[0, 6:7, :] += jnp.sum(dsecond, axis=0, keepdims=True)
        g = dsecond * sg
        through = (
            g
            - jnp.mean(g, axis=-1, keepdims=True)
            - unit * jnp.mean(g * unit, axis=-1, keepdims=True)
        ) * inverse
        dres = COT[rows, :].astype(F32) + through
        RES[rows, :] = dres
        SEC[rows, :] = dres.astype(BF)
        DH[rows, :] = dot_nt(dres.astype(BF), W[3]).astype(BF)

    tiles(second_back)
    lo_store = load(FT, lo_hbm, iosem.at[2])
    far_dout = []
    for r in range(2):
        half = pl.ds(384 * r, 384)
        far_dout.append(
            remote(DH.at[:, half], FDO.at[:, half], xsend.at[2 + r], xrecv.at[2 + r], partner)
        )
    rs_first(3)
    rs_second(0)
    VS[0, 7:8, :] = row_sum(COT[...])
    VS[0, 2:3, :] = row_sum(SEC[...])

    head = lax.broadcasted_iota(jnp.int32, (16, WIDTH), 0)
    column = lax.broadcasted_iota(jnp.int32, (16, WIDTH), 1)
    in_head = jnp.where((column >> 6) == head, 1.0, 0.0).astype(BF)
    product = DH[...].astype(F32) * ATT[...].astype(F32)
    rough = product.astype(BF)
    STAT[1] = dot_nt(in_head, rough) + dot_nt(in_head, (product - rough.astype(F32)).astype(BF))
    far_stats = remote(STAT, FSTAT, xsend.at[4], xrecv.at[4], partner)

    padded_transpose(ATT)
    gone((0, 0, 0))
    chunk_matmul(7, lambda: SEC[...])
    rs_core(7)
    rs_first(4)
    rs_mid(2)
    rs_second(1)
    rs_first(5)

    def own_queries(hp, carry):
        cols = pair_cols(hp)
        q = QO[:, cols]
        ko = KO[:, cols]
        kf = KF[:, cols]
        vo = VO[:, cols]
        vf = VF[:, cols]
        do = DH[:, cols]
        ko_t = ko.T
        kf_t = kf.T
        dq = []
        dk = None
        for h in range(2):
            logsum = STAT[0, pl.ds(2 * hp + h, 1), :]
            delta = STAT[1, pl.ds(2 * hp + h, 1), :]
            qm = q * select[h] + MF[h]
            qs = q * select[h]
            dom = do * select[h]
            near = jnp.exp(dot_nt(ko * select[h] + MF[2 + h], qm) - logsum)
            dnear = (near * (dot_nt(vo, dom) - delta)).astype(BF)
            far = jnp.exp(dot_nt(kf * select[h] + MF[6 + h], qm) - logsum)
            dfar = (far * (dot_nt(vf, dom) - delta)).astype(BF)
            dq.append(
                dot_nn(ko_t[64 * h : 64 * h + 64], dnear)
                + dot_nn(kf_t[64 * h : 64 * h + 64], dfar)
            )
            dk_h = dot_nn(dnear, qs)
            dv_h = dot_nn(near.astype(BF), dom)
            dk, dv = (dk_h, dv_h) if dk is None else (dk + dk_h, dv + dv_h)
        ACC1[:, cols] = dk
        ACC2[:, cols] = dv
        QO[:, cols] = (jnp.concatenate(dq, axis=0).T * 0.125).astype(BF)
        return carry

    lax.fori_loop(0, 2, own_queries, 0)
    rs_mid(3)
    rs_first(6)
    lax.fori_loop(2, 4, own_queries, 0)
    rs_first(7)
    rs_mid(4)
    rs_mid(5)
    rs_second(2)
    rs_third(0)
    rs_third(1)
    lax.fori_loop(4, 6, own_queries, 0)
    rs_mid(6)
    rs_second(3)
    rs_second(4)
    rs_third(2)

    def again(rows, start):
        unit, _ = norm_parts(TOK[rows, :].astype(F32))
        ATT[rows, :] = (unit * fg + fs).astype(BF)

    tiles(again)
    padded_transpose(ATT)

    far_stats.wait_recv()

    def far_queries(hp, carry):
        cols = pair_cols(hp)
        q = QF[:, cols]
        ko = KO[:, cols]
        vo = VO[:, cols]
        do = FDO[:, cols]
        dk = ACC1[:, cols]
        dv = ACC2[:, cols]
        for h in range(2):
            logsum = FSTAT[0, pl.ds(2 * hp + h, 1), :]
            delta = FSTAT[1, pl.ds(2 * hp + h, 1), :]
            qs = q * select[h]
            dom = do * select[h]
            probs = jnp.exp(dot_nt(ko * select[h] + MF[2 + h], qs + MF[4 + h]) - logsum)
            dscores = (probs * (dot_nt(vo, dom) - delta)).astype(BF)
            dk = dk + dot_nn(dscores, qs)
            dv = dv + dot_nn(probs.astype(BF), dom)
        KO[:, cols] = dk.astype(BF)
        VO[:, cols] = dv.astype(BF)
        return carry

    for j in range(3):
        c = 8 + j
        if j < 2:
            far_dout[j].wait_recv()
        lax.fori_loop(2 * j, 2 * j + 2, far_queries, 0)
        gone((c - 7, 0, 0))
        cols = slice(TILE * j, TILE * (j + 1))

        def joined(cols=cols):
            return jnp.concatenate([QO[:, cols], KO[:, cols], VO[:, cols]], axis=1)

        chunk_matmul(c, joined)
        rs_core(c)
        if j == 0:
            rs_mid(7)
            rs_second(5)
            rs_second(6)
            rs_third(3)
            rs_third(4)
            rs_fourth(0)
            rs_fourth(1)
        if j == 1:
            rs_first(8)
            rs_second(7)
            rs_third(5)
            rs_third(6)
            rs_fourth(2)
            rs_fourth(3)
            rs_end(0)
        if j == 2:
            rs_first(9)
            rs_mid(8)
            rs_third(7)
            rs_fourth(4)
            rs_fourth(5)

    VS[0, 0:1, :] = row_sum(QO[...])
    VS[0, 1:2, :] = row_sum(VO[...])

    def first_back(rows, start):
        unit, inverse = norm_parts(TOK[rows, :].astype(F32))
        dnormed = (
            dot_nt(QO[rows, :], W[0]) + dot_nt(KO[rows, :], W[1]) + dot_nt(VO[rows, :], W[2])
        )
        VS[0, 3:4, :] += jnp.sum(dnormed * unit, axis=0, keepdims=True)
        VS[0, 4:5, :] += jnp.sum(dnormed, axis=0, keepdims=True)
        g = dnormed * fg
        through = (
            g
            - jnp.mean(g, axis=-1, keepdims=True)
            - unit * jnp.mean(g * unit, axis=-1, keepdims=True)
        ) * inverse
        TOK[rows, :] = (RES[rows, :] + through).astype(BF)

    for copy in far_tokens:
        copy.wait_send()
    tiles(first_back)
    gt_store = load(TOK, gt_hbm, iosem.at[3])

    def vec_send(step, peers):
        base = (0, 1, 4, 7)[step]
        for i, peer in enumerate(peers):
            remote(VS.at[step], VR.at[base + i], vsend.at[step], vrecv.at[step], peer)

    def vec_add(step):
        base = (0, 1, 4, 7)[step]
        if step == 0:
            all_bytes(VR.at[0:1], vrecv.at[0])
            total = VS[0] + VR[0]
        else:
            all_bytes(VR.at[base : base + 3], vrecv.at[step])
            total = (VS[step] + VR[base + 1]) + (VR[base] + VR[base + 2])
        VS[step + 1] = total

    vec_send(0, [sibling])
    rs_first(10)
    rs_mid(9)
    rs_second(8)
    rs_fourth(6)
    rs_fourth(7)
    vec_add(0)
    vec_send(1, z_peer[1:])
    rs_mid(10)
    rs_second(9)
    rs_third(8)
    vec_add(1)
    vec_send(2, x_peer[1:])
    rs_second(10)
    rs_third(9)
    rs_fourth(8)
    vec_add(2)
    vec_send(3, y_peer[1:])
    rs_third(10)
    rs_fourth(9)
    rs_fourth(10)
    vec_add(3)
    rs_end(10)

    spot = lax.broadcasted_iota(jnp.int32, (WIDTH, 128), 0)
    lane = lax.broadcasted_iota(jnp.int32, (WIDTH, 128), 1)
    narrow = jnp.where((lane < 12) & (spot == lane + 12 * dp), 1.0, 0.0)
    wide = jnp.where((lane < 48) & (spot == lane + 48 * (dp % 16)), 1.0, 0.0)
    vectors = VS[4]
    exact = dict(precision=lax.Precision.HIGHEST, preferred_element_type=F32)
    small = jnp.dot(vectors, narrow, **exact)
    large = jnp.dot(vectors, wide, **exact)
    row = lax.broadcasted_iota(jnp.int32, (16, 128), 0)
    large = jnp.sum(jnp.where(row == 8 + dp // 16, large, 0.0), axis=0, keepdims=True)
    for i, ref in enumerate(
        (gqb_ref, gvb_ref, gob_ref, gfg_ref, gfs_ref, gsg_ref, gss_ref, gdb_ref)
    ):
        ref[...] = small[i : i + 1, 0:12].reshape(12)
    gub_ref[...] = large[:, 0:48].reshape(48)

    for copy in far_dout:
        copy.wait_send()
    far_stats.wait_send()
    for key in list(landing):
        gone(key)
    all_bytes(VR.at[0:1], vsend.at[0])
    for step in range(1, 4):
        all_bytes(VR.at[3 * step - 2 : 3 * step + 1], vsend.at[step])
    lo_store.wait()
    gt_store.wait()


def finish(*refs):
    count = len(refs) // 2
    for i in range(count):
        refs[count + i][...] = refs[i][...]


def body(
    tokens,
    input_weight,
    query_bias,
    value_bias,
    out_weight,
    out_bias,
    first_gain,
    first_shift,
    second_gain,
    second_shift,
    up_weight,
    up_bias,
    down_weight,
    down_bias,
    cotangent,
    row_counts,
    image_lengths,
):
    hbm = pl.BlockSpec(memory_space=pl.ANY)
    vmem = pl.BlockSpec(memory_space=pltpu.VMEM)
    smem = pl.BlockSpec(memory_space=pltpu.SMEM)
    rows = jax.ShapeDtypeStruct((ROWS, WIDTH), BF)

    def f32(*shape):
        return jax.ShapeDtypeStruct(shape, F32)

    def block(kind, *lead):
        return pltpu.VMEM((*lead, ROWS, WIDTH), kind)

    out = pl.pallas_call(
        kernel,
        out_shape=(
            rows,
            rows,
            f32(12, 3 * WIDTH),
            f32(12),
            f32(12),
            f32(12, WIDTH),
            f32(12),
            f32(12),
            f32(12),
            f32(12),
            f32(12),
            f32(12, 4 * WIDTH),
            f32(48),
            f32(48, WIDTH),
            f32(12),
        ),
        in_specs=[smem, smem] + [hbm] * 6 + [vmem] * 9,
        out_specs=(hbm, hbm) + (vmem,) * 13,
        scratch_shapes=[
            pltpu.VMEM((8, WIDTH, WIDTH), BF),
            pltpu.VMEM((SLOTS, 2, 4, 4, 2, 16, WIDTH), BF),
            pltpu.VMEM((CHUNKS, 2, 4, 4, 16, WIDTH), BF),
            pltpu.VMEM((CHUNKS, 3, 2, 4, 16, WIDTH), BF),
            pltpu.VMEM((CHUNKS, 3, 2, 16, WIDTH), BF),
            pltpu.VMEM((CHUNKS, 3, 16, WIDTH), BF),
            pltpu.VMEM((2, 3, 4, 4, 16, 384), BF),
            pltpu.VMEM((2, 3, 4, 16, 384), BF),
            pltpu.VMEM((2, 3, 16, 384), BF),
            pltpu.VMEM((2, 2, 16, 384), F32),
            block(BF),
            block(BF),
            pltpu.VMEM((2, 16, ROWS), F32),
            pltpu.VMEM((2, 16, ROWS), F32),
        ]
        + [block(BF)] * 12
        + [
            pltpu.VMEM((1024, ROWS), BF),
            block(F32),
            block(F32, 2),
            pltpu.VMEM((8, ROWS, 128), BF),
            pltpu.VMEM((ROWS, 384), BF),
            pltpu.VMEM((16, ROWS), F32),
            pltpu.VMEM((16, ROWS), F32),
            pltpu.VMEM((5, 16, WIDTH), F32),
            pltpu.VMEM((10, 16, WIDTH), F32),
            pltpu.SemaphoreType.DMA((8,)),
            pltpu.SemaphoreType.DMA((4,)),
            pltpu.SemaphoreType.DMA((5,)),
            pltpu.SemaphoreType.DMA((5,)),
            pltpu.SemaphoreType.DMA((len(STEPS),)),
            pltpu.SemaphoreType.DMA((len(STEPS),)),
            pltpu.SemaphoreType.DMA((4,)),
            pltpu.SemaphoreType.DMA((4,)),
        ],
        compiler_params=pltpu.CompilerParams(
            collective_id=0, has_side_effects=True, vmem_limit_bytes=63 * 2**20
        ),
        name="encoder",
    )(
        row_counts,
        image_lengths,
        tokens,
        cotangent,
        input_weight,
        out_weight,
        up_weight,
        down_weight,
        query_bias,
        value_bias,
        out_bias,
        first_gain,
        first_shift,
        second_gain,
        second_shift,
        up_bias,
        down_bias,
    )
    return pl.pallas_call(
        finish,
        out_shape=tuple(jax.ShapeDtypeStruct(value.shape, value.dtype) for value in out),
        in_specs=[vmem] * len(out),
        out_specs=(vmem,) * len(out),
        name="finish",
    )(*out)


def solution(mesh):
    rows = P(("seq", "dp"), None)
    split = P("dp", None)
    line = P("dp")
    return jax.shard_map(
        body,
        mesh=mesh,
        in_specs=(rows,) + (P(),) * 13 + (rows, split, split),
        out_specs=(
            rows,
            rows,
            split,
            line,
            line,
            split,
            line,
            line,
            line,
            line,
            line,
            split,
            line,
            split,
            line,
        ),
        check_vma=False,
    )
```

```python
import jax
import jax.numpy as jnp
from jax import lax
from jax.experimental import pallas as pl
from jax.experimental.pallas import tpu as pltpu
from jax.sharding import PartitionSpec as P

F32 = jnp.float32
BF = jnp.bfloat16
EPS = 1e-06
ROWS = 512
WIDTH = 768
TILE = 256
CHUNKS = 11
SLOTS = 7
FEATURES = 37
PARTS = (
    ((2, 0, 768),),
    ((0, 0, 768),),
    ((1, 0, 768),),
    ((0, 0, 768),),
    ((1, 0, 768),),
    ((0, 0, 768),),
    ((1, 0, 768),),
    ((0, 0, 768),),
    ((1, 0, 768),),
    ((0, 0, 384), (1, 384, 768)),
    ((3, 0, 384), (4, 384, 768)),
)
Y_FIRST = (0,)
STEPS = [(c, 0, 0) for c in range(CHUNKS)]
STEPS += [(c, s, p) for c in range(CHUNKS) for p, _, _ in PARTS[c] for s in (1, 2, 3)]
STEPS += [(c, 4, 2) for c in Y_FIRST]
STEPS += [(c, 5, p) for c in range(CHUNKS) for p, _, _ in PARTS[c] if p < 2]
MESH = pl.DeviceIdType.MESH


def dot_nn(left, right):
    return lax.dot_general(left, right, (((1,), (0,)), ((), ())), preferred_element_type=F32)


def dot_nt(left, right):
    return lax.dot_general(left, right, (((1,), (1,)), ((), ())), preferred_element_type=F32)


def dot_tn(left, right):
    return lax.dot_general(left, right, (((0,), (0,)), ((), ())), preferred_element_type=F32)


def norm_parts(block):
    centred = block - jnp.mean(block, axis=-1, keepdims=True)
    spread = jnp.mean(centred * centred, axis=-1, keepdims=True)
    inverse = lax.rsqrt(spread + EPS)
    return centred * inverse, inverse


def kernel(
    counts_ref,
    lengths_ref,
    tokens_hbm,
    cot_hbm,
    wi_hbm,
    wo_hbm,
    wu_hbm,
    wd_hbm,
    qb_ref,
    vb_ref,
    ob_ref,
    fg_ref,
    fs_ref,
    sg_ref,
    ss_ref,
    ub_ref,
    db_ref,
    lo_hbm,
    gt_hbm,
    gi_ref,
    gqb_ref,
    gvb_ref,
    go_ref,
    gob_ref,
    gfg_ref,
    gfs_ref,
    gsg_ref,
    gss_ref,
    gu_ref,
    gub_ref,
    gd_ref,
    gdb_ref,
    W,
    CH,
    R0,
    R1,
    R2,
    R3,
    S1,
    S2,
    S3,
    S4,
    FT,
    FDO,
    STAT,
    FSTAT,
    QO,
    KO,
    VO,
    QF,
    KF,
    VF,
    TOK,
    COT,
    ATT,
    SEC,
    ACT,
    DH,
    XT,
    XN,
    RES,
    ACC,
    MF,
    PB,
    TOP,
    SUM,
    VS,
    VR,
    wsem,
    dsem,
    iosem,
    xsend,
    xrecv,
    rsend,
    rrecv,
    vsend,
    vrecv,
):
    ACC1, ACC2 = ACC.at[0], ACC.at[1]
    part = lax.axis_index("seq")
    dp = lax.axis_index("dp")
    y_lo = dp // 32
    z = (dp // 8) % 4
    x = (dp // 2) % 4
    core = dp % 2
    y = 2 * part + y_lo

    def device(yy, zz, xx, cc):
        return (yy // 2, ((yy % 2) * 4 + zz) * 8 + xx * 2 + cc)

    sibling = device(y, z, x, 1 - core)
    z_of = [(z + k) % 4 for k in range(4)]
    x_of = [(x + k) % 4 for k in range(4)]
    y_of = [(y + k) % 4 for k in range(4)]
    z_a, z_b = z + 1 - 2 * (z % 2), 3 - z
    x_a, x_b = x + 1 - 2 * (x % 2), 3 - x
    near_z = [device(y, v, x, core) for v in (z_a, z_b)]
    near_x = [device(y, z, v, core) for v in (x_a, x_b)]
    z_peer = [device(y, v, x, core) for v in z_of]
    x_peer = [device(y, z, v, core) for v in x_of]
    y_peer = [device(v, z, x, core) for v in y_of]
    partner = y_peer[2]

    def load(src, dst, sem):
        copy = pltpu.make_async_copy(src, dst, sem)
        copy.start()
        return copy

    tok_load = load(tokens_hbm, TOK, iosem.at[0])
    w_load = {}
    for i in range(3):
        w_load[i] = load(wi_hbm.at[:, pl.ds(WIDTH * i, WIDTH)], W.at[i], wsem.at[i])
    cot_load = load(cot_hbm, COT, iosem.at[1])
    w_load[3] = load(wo_hbm, W.at[3], wsem.at[3])

    def load_ffn(f):
        slot = f % 2
        up = load(wu_hbm.at[:, pl.ds(WIDTH * f, WIDTH)], W.at[4 + slot], wsem.at[4 + slot])
        down = load(wd_hbm.at[pl.ds(WIDTH * f, WIDTH)], W.at[6 + slot], wsem.at[6 + slot])
        return up, down

    ffn_load = {0: load_ffn(0), 1: load_ffn(1)}
    down_load = [
        load(wd_hbm.at[pl.ds(2 * WIDTH + ROWS * i, ROWS)], ref, dsem.at[i])
        for i, ref in enumerate((SEC, ACT, DH))
    ]

    barrier = pltpu.get_barrier_semaphore()
    for peer in [sibling] + z_peer[1:] + x_peer[1:] + y_peer[1:]:
        pl.semaphore_signal(barrier, inc=1, device_id=peer, device_id_type=MESH)
    pl.semaphore_wait(barrier, 10)

    def remote(src, dst, send, recv, peer):
        copy = pltpu.make_async_remote_copy(
            src_ref=src,
            dst_ref=dst,
            send_sem=send,
            recv_sem=recv,
            device_id=peer,
            device_id_type=MESH,
        )
        copy.start()
        return copy

    far_tokens = remote(tokens_hbm, FT, xsend.at[0], xrecv.at[0], partner)

    def all_bytes(ref, sem):
        pltpu.make_async_copy(ref, ref, sem).wait()

    landing = {}

    def send_all(key, dst, copies):
        i = STEPS.index(key)
        landing[key] = dst
        for src, into, peer in copies:
            remote(src, into, rsend.at[i], rrecv.at[i], peer)

    def received(key):
        all_bytes(landing[key], rrecv.at[STEPS.index(key)])

    def gone(key):
        all_bytes(landing.pop(key), rsend.at[STEPS.index(key)])

    def rs_core(c):
        src = CH.at[c % SLOTS, :, :, :, 1 - core]
        send_all((c, 0, 0), R0.at[c], [(src, R0.at[c], sibling)])

    def row_of(c):
        return c - sum(first < c for first in Y_FIRST)

    def y_slot(c):
        n = Y_FIRST.index(c)
        return n, 384

    def rs_first(c):
        received((c, 0, 0))

        def add(i, carry):
            yl, zz = i // 4, i % 4
            R0[c, yl, zz] = (
                R0[c, yl, zz].astype(F32) + CH[c % SLOTS, yl, zz, :, core].astype(F32)
            ).astype(BF)
            return carry

        lax.fori_loop(0, 8, add, 0)
        for p, lo, hi in PARTS[c]:
            copies = []
            if p == 2:
                n, width = y_slot(c)
                whole = S1.at[n, :, :, :, :, 0:width]
                for k in (2, 1, 3):
                    start = pl.multiple_of(lo + width * (y_of[k] // 2), 128)
                    src = R0.at[c, y_of[k] % 2, :, :, :, pl.ds(start, width)]
                    copies.append((src, S1.at[n, k - 1, :, :, :, 0:width], y_peer[k]))
            elif p > 2:
                whole = R1.at[row_of(c), :, :, :, :, lo:hi]
                for k in (2, 1, 3):
                    if p == 3:
                        src, peer = R0.at[c, :, z_of[k], :, :, lo:hi], z_peer[k]
                    else:
                        src, peer = R0.at[c, :, :, x_of[k], :, lo:hi], x_peer[k]
                    copies.append((src, R1.at[row_of(c), k - 1, :, :, :, lo:hi], peer))
            else:
                whole = R1.at[row_of(c), 0:2, :, :, :, lo:hi]
                a, b = (z_a, z_b) if p == 0 else (x_a, x_b)
                across = 3 - a
                peers = near_z if p == 0 else near_x
                for half, nearest in ((0, a), (1, b)):
                    for spot, wanted in ((1, across), (0, nearest)):
                        dst = R1.at[row_of(c), half, spot, :, :, lo:hi]
                        copies.append((shares(c, p, half, wanted, lo, hi), dst, peers[half]))
            send_all((c, 1, p), whole, copies)

    def shares(c, p, yl, v, lo, hi):
        if p == 0:
            return R0.at[c, yl, v, :, :, lo:hi]
        return R0.at[c, yl, :, v, :, lo:hi]

    def rs_mid(c):
        for p, lo, hi in PARTS[c]:
            if p > 1:
                continue
            received((c, 1, p))
            v, a, b = (z, z_a, z_b) if p == 0 else (x, x_a, x_b)
            for half, other in ((0, b), (1, a)):
                for spot, kept in ((0, v), (1, other)):
                    at = (row_of(c), half, spot, slice(None), slice(None), slice(lo, hi))
                    own = shares(c, p, half, kept, lo, hi)[...]
                    R1[at] = (own.astype(F32) + R1[at].astype(F32)).astype(BF)
            peers = near_z if p == 0 else near_x
            copies = []
            for half in range(2):
                src = R1.at[row_of(c), half, 1, :, :, lo:hi]
                copies.append((src, R1.at[row_of(c), 2, half, :, :, lo:hi], peers[1 - half]))
            send_all((c, 5, p), R1.at[row_of(c), 2, :, :, :, lo:hi], copies)

    def rs_second(c):
        for p, lo, hi in PARTS[c]:
            received((c, 5 if p < 2 else 1, p))
            copies = []
            if p == 2:
                n, width = y_slot(c)
                start = pl.multiple_of(lo + width * part, 128)
                for zz in range(4):
                    total = R0[c, y_lo, zz, :, :, pl.ds(start, width)].astype(F32)
                    for k in range(3):
                        total = total + S1[n, k, zz, :, :, 0:width].astype(F32)
                    S1[n, 0, zz, :, :, 0:width] = total.astype(BF)
                whole = S2.at[n, :, :, :, 0:width]
            elif p > 2:
                for yl in range(2):
                    if p == 3:
                        total = R0[c, yl, z, :, :, lo:hi].astype(F32)
                    else:
                        total = R0[c, yl, :, x, :, lo:hi].astype(F32)
                    for k in range(3):
                        total = total + R1[row_of(c), k, yl, :, :, lo:hi].astype(F32)
                    R1[row_of(c), 0, yl, :, :, lo:hi] = total.astype(BF)
                whole = R2.at[row_of(c), :, :, :, lo:hi]
            else:
                for half in range(2):
                    at = (row_of(c), half, 0, slice(None), slice(None), slice(lo, hi))
                    total = R1[at].astype(F32) + R1[row_of(c), 2, half, :, :, lo:hi].astype(F32)
                    R1[at] = total.astype(BF)
                whole = R2.at[row_of(c), :, :, :, lo:hi]
            for k in (2, 1, 3):
                if p == 3:
                    src = R1.at[row_of(c), 0, :, x_of[k], :, lo:hi]
                    dst, peer = R2.at[row_of(c), k - 1, :, :, lo:hi], x_peer[k]
                elif p == 4:
                    src = R1.at[row_of(c), 0, :, z_of[k], :, lo:hi]
                    dst, peer = R2.at[row_of(c), k - 1, :, :, lo:hi], z_peer[k]
                elif p == 0:
                    src = R1.at[row_of(c), 0:2, 0, x_of[k], :, lo:hi]
                    dst, peer = R2.at[row_of(c), k - 1, :, :, lo:hi], x_peer[k]
                elif p == 1:
                    src = R1.at[row_of(c), 0:2, 0, z_of[k], :, lo:hi]
                    dst, peer = R2.at[row_of(c), k - 1, :, :, lo:hi], z_peer[k]
                else:
                    src = S1.at[n, 0, z_of[k], :, :, 0:width]
                    dst, peer = S2.at[n, k - 1, :, :, 0:width], z_peer[k]
                copies.append((src, dst, peer))
            send_all((c, 2, p), whole, copies)

    def rs_third(c):
        for p, lo, hi in PARTS[c]:
            received((c, 2, p))
            copies = []
            if p == 2:
                n, width = y_slot(c)
                total = S1[n, 0, z, :, :, 0:width].astype(F32)
                for k in range(3):
                    total = total + S2[n, k, :, :, 0:width].astype(F32)
                S2[n, 0, :, :, 0:width] = total.astype(BF)
                whole = S3.at[n, :, :, 0:width]
            else:
                if p == 3:
                    total = R1[row_of(c), 0, :, x, :, lo:hi].astype(F32)
                elif p == 4:
                    total = R1[row_of(c), 0, :, z, :, lo:hi].astype(F32)
                elif p == 0:
                    total = R1[row_of(c), 0:2, 0, x, :, lo:hi].astype(F32)
                else:
                    total = R1[row_of(c), 0:2, 0, z, :, lo:hi].astype(F32)
                for k in range(3):
                    total = total + R2[row_of(c), k, :, :, lo:hi].astype(F32)
                R2[row_of(c), 0, :, :, lo:hi] = total.astype(BF)
                whole = R3.at[row_of(c), :, :, lo:hi]
            for k in (2, 1, 3):
                if p == 2:
                    src = S2.at[n, 0, x_of[k], :, 0:width]
                    dst, peer = S3.at[n, k - 1, :, 0:width], x_peer[k]
                else:
                    src = R2.at[row_of(c), 0, y_of[k] % 2, :, lo:hi]
                    dst, peer = R3.at[row_of(c), k - 1, :, lo:hi], y_peer[k]
                copies.append((src, dst, peer))
            send_all((c, 3, p), whole, copies)

    def store_share(c, lo, hi, total):
        if c < 4:
            gu_ref[:, WIDTH * c + lo : WIDTH * c + hi] = total[0:12]
        elif c < 7:
            gd_ref[16 * (c - 4) : 16 * (c - 3), lo:hi] = total
        elif c == 7:
            go_ref[:, lo:hi] = total[0:12]
        else:
            for b in range(lo // 384, hi // 384):
                start = 384 * b if c == 8 else WIDTH * (b + 1) + 384 * (c - 9)
                gi_ref[:, start : start + 384] = total[0:12, 384 * b - lo : 384 * (b + 1) - lo]

    def rs_fourth(c):
        for p, lo, hi in PARTS[c]:
            received((c, 3, p))
            if p == 2:
                n, width = y_slot(c)
                total = S2[n, 0, x, :, 0:width].astype(F32)
                for k in range(3):
                    total = total + S3[n, k, :, 0:width].astype(F32)
                S4[n, 0, :, 0:width] = total
                dst = S4.at[n, 1, :, 0:width]
                send_all((c, 4, p), dst, [(S4.at[n, 0, :, 0:width], dst, partner)])
            else:
                total = (R2[row_of(c), 0, y_lo, :, lo:hi].astype(F32) + R3[row_of(c), 1, :, lo:hi].astype(F32)) + (
                    R3[row_of(c), 0, :, lo:hi].astype(F32) + R3[row_of(c), 2, :, lo:hi].astype(F32)
                )
                store_share(c, lo, hi, total)

    def rs_end(c):
        n, width = y_slot(c)
        received((c, 4, 2))
        mine = S4[n, 0, :, 0:width]
        other = S4[n, 1, :, 0:width]
        low = jnp.where(part == 0, mine, other)
        high = jnp.where(part == 0, other, mine)
        lo = PARTS[c][-1][1]
        store_share(c, lo, lo + 2 * width, jnp.concatenate([low, high], axis=1))

    counts0 = counts_ref[0, 0]
    counts1 = counts_ref[0, 1]
    end0 = lengths_ref[0, 0]
    end1 = end0 + lengths_ref[0, 1]
    end2 = end1 + lengths_ref[0, 2]
    end3 = end2 + lengths_ref[0, 3]

    def used_rows(start, size, width):
        place = lax.broadcasted_iota(jnp.int32, (size, width), 0) + start
        return place < counts0 + part * (counts1 - counts0)

    def features(base, which):
        place = lax.broadcasted_iota(jnp.int32, (ROWS, 128), 0)
        shifted = place + which * counts0
        index = jnp.zeros((ROWS, 128), jnp.int32)
        for end in (end0, end1, end2, end3):
            index = index + jnp.where(end <= shifted, 1, 0)
        owned = counts0 + which * (counts1 - counts0)
        ids = jnp.where(place < owned, index, 4 + which * ROWS + place)
        lane = lax.broadcasted_iota(jnp.int32, (ROWS, 128), 1)
        high = lane >= 64
        spot = jnp.where(high, lane - 64, lane)
        digit = jnp.where(
            spot < 16, ids & 15, jnp.where(spot < 32, ((ids >> 4) & 15) + 16, (ids >> 8) + 32)
        )
        hot = jnp.where(digit == spot, 1.0, 0.0)
        query = jnp.where(spot < FEATURES, 1.0 - hot, 0.0)
        key = hot * -1e30
        MF[base] = jnp.where(high, query, 0.0).astype(BF)
        MF[base + 1] = jnp.where(high, 0.0, query).astype(BF)
        MF[base + 2] = jnp.where(high, key, 0.0).astype(BF)
        MF[base + 3] = jnp.where(high, 0.0, key).astype(BF)

    features(0, part)
    features(4, 1 - part)
    lane_row = lax.broadcasted_iota(jnp.int32, (1, 128), 1)
    select = [
        jnp.where(lane_row < 64, 1.0, 0.0).astype(BF),
        jnp.where(lane_row < 64, 0.0, 1.0).astype(BF),
    ]

    rho = lax.broadcasted_iota(jnp.int32, (ROWS, 384), 0)
    feature = lax.broadcasted_iota(jnp.int32, (ROWS, 384), 1)
    within = rho & 15
    PB[...] = jnp.where(
        (within < 12) & (feature == (rho >> 4) * 12 + within), 1.0, 0.0
    ).astype(BF)

    def padded_transpose(source, into):
        for b in range(2):
            into[ROWS * b : ROWS * (b + 1), :] = dot_nt(
                PB[...], source[:, 384 * b : 384 * (b + 1)]
            ).astype(BF)

    def chunk_matmul(c, right):
        def block(m, carry):
            start = pl.multiple_of(m * TILE, TILE)
            out = dot_nn((XT if c < 8 else XN)[pl.ds(start, TILE), :], right())
            CH[c % SLOTS, m // 2, pl.ds(2 * (m % 2), 2)] = out.astype(BF).reshape(
                2, 4, 2, 16, WIDTH
            )
            return carry

        lax.fori_loop(0, 4, block, 0)

    ones = jnp.ones((16, ROWS), BF)

    def row_sum(block):
        return dot_nn(ones, block)[0:1]

    def tiles(step):
        def run(t, carry):
            step(pl.ds(pl.multiple_of(t * TILE, TILE), TILE), t * TILE)
            return carry

        lax.fori_loop(0, ROWS // TILE, run, 0)

    qb = qb_ref[...].reshape(1, WIDTH)
    vb = vb_ref[...].reshape(1, WIDTH)
    ob = ob_ref[...].reshape(1, WIDTH)
    fg = fg_ref[...].reshape(1, WIDTH)
    fs = fs_ref[...].reshape(1, WIDTH)
    sg = sg_ref[...].reshape(1, WIDTH)
    ss = ss_ref[...].reshape(1, WIDTH)
    db = db_ref[...].reshape(1, WIDTH)

    def projection(source, q_ref, k_ref, v_ref):
        def step(rows, start):
            unit, _ = norm_parts(source[rows, :].astype(F32))
            normed = (unit * fg + fs).astype(BF)
            q = (dot_nn(normed, W[0]) + qb).astype(BF)
            q_ref[rows, :] = q * jnp.asarray(0.125, BF)
            k_ref[rows, :] = dot_nn(normed, W[1]).astype(BF)
            v_ref[rows, :] = (dot_nn(normed, W[2]) + vb).astype(BF)

        return step

    tok_load.wait()
    for i in range(3):
        w_load[i].wait()
    tiles(projection(TOK, QO, KO, VO))

    cot_load.wait()

    def mask_cot(rows, start):
        used = used_rows(start, TILE, WIDTH)
        COT[rows, :] = jnp.where(used, COT[rows, :].astype(F32), 0.0).astype(BF)

    tiles(mask_cot)

    def pair_cols(hp):
        return pl.ds(pl.multiple_of(hp * 128, 128), 128)

    def mix_at(hp, h):
        start = pl.multiple_of(128 * (hp % 4) + 64 * h, 64)
        return hp // 4, pl.ds(start, 64), slice(0, ROWS)

    def attend_own(hp, carry):
        cols = pair_cols(hp)
        q = QO[:, cols]
        keys = KO[:, cols]
        values = VO[:, cols].T
        for h in range(2):
            row = pl.ds(2 * hp + h, 1)
            scores = dot_nt(keys * select[h] + MF[2 + h], q * select[h] + MF[h])
            top = jnp.max(scores, axis=0, keepdims=True)
            probs = jnp.exp(scores - top)
            TOP[row, :] = top
            SUM[row, :] = jnp.sum(probs, axis=0, keepdims=True)
            own = slice(64 * h, 64 * h + 64)
            ACC[mix_at(hp, h)] = dot_nn(values[own], probs.astype(BF))
        return carry

    lax.fori_loop(0, 6, attend_own, 0)

    def attend_far(hp, carry):
        cols = pair_cols(hp)
        q = QO[:, cols]
        keys = KF[:, cols]
        values = VF[:, cols].T
        outs = []
        for h in range(2):
            row = pl.ds(2 * hp + h, 1)
            own = slice(64 * h, 64 * h + 64)
            scores = dot_nt(keys * select[h] + MF[6 + h], q * select[h] + MF[h])
            before = TOP[row, :]
            top = jnp.maximum(before, jnp.max(scores, axis=0, keepdims=True))
            shrink = jnp.exp(before - top)
            probs = jnp.exp(scores - top)
            total = SUM[row, :] * shrink + jnp.sum(probs, axis=0, keepdims=True)
            mixed = ACC[mix_at(hp, h)] * shrink + dot_nn(values[own], probs.astype(BF))
            STAT[0, row, :] = top + jnp.log(total)
            outs.append(mixed * (1.0 / total))
        ATT[:, cols] = jnp.concatenate(outs, axis=0).T.astype(BF)
        return carry

    def again(rows, start):
        unit, _ = norm_parts(TOK[rows, :].astype(F32))
        ATT[rows, :] = (unit * fg + fs).astype(BF)

    tiles(again)
    padded_transpose(ATT, XN)

    for copy in down_load:
        copy.wait()
    for f in range(2):
        ffn_load[f][1].wait()

    def early_step(rows, start):
        dout = COT[rows, :]
        block = start // TILE * 2

        def keep(f, lo, value):
            CH[f, 0, pl.ds(block, 2), :, :, :, lo : lo + value.shape[1]] = value.astype(BF).reshape(
                2, 4, 2, 16, value.shape[1]
            )

        for f in range(2):
            keep(f, 0, dot_nt(dout, W[6 + f]))
        keep(2, 0, dot_nt(dout, SEC[...]))
        middle = dot_nt(dout, ACT[...])
        keep(2, 512, middle[:, 0:256])
        keep(3, 0, middle[:, 256:512])
        keep(3, 256, dot_nt(dout, DH[...]))

    tiles(early_step)

    far_tokens.wait_recv()
    tiles(projection(FT, QF, KF, VF))
    lax.fori_loop(0, 6, attend_far, 0)

    w_load[3].wait()

    def out_step(rows, start):
        res = TOK[rows, :].astype(F32) + dot_nn(ATT[rows, :], W[3]) + ob
        RES[rows, :] = res
        unit, _ = norm_parts(res)
        SEC[rows, :] = (unit * sg + ss).astype(BF)
        ACC1[rows, :] = jnp.zeros((TILE, WIDTH), F32)
        ACC2[rows, :] = jnp.zeros((TILE, WIDTH), F32)

    tiles(out_step)
    padded_transpose(SEC, XT)
    VS[0] = jnp.zeros((16, WIDTH), F32)

    for f in range(4):
        slot = f % 2
        ffn_load[f][0].wait()
        if f > 1:
            ffn_load[f][1].wait()
        ub = ub_ref[WIDTH * f : WIDTH * (f + 1)].reshape(1, WIDTH)

        def ffn_step(rows, start, f=f, slot=slot, ub=ub):
            early = CH[f, 0, pl.ds(start // TILE * 2, 2)].reshape(TILE, WIDTH).astype(F32)
            hidden = dot_nn(SEC[rows, :], W[4 + slot]) + ub
            cdf = 0.5 * (1.0 + lax.erf(hidden * 0.7071067811865476))
            density = jnp.exp(-0.5 * hidden * hidden) * 0.3989422804014327
            active = (hidden * cdf).astype(BF)
            ACT[rows, :] = active
            dhidden = (early * (cdf + hidden * density)).astype(BF)
            DH[rows, :] = dhidden
            ACC1[rows, :] += dot_nn(active, W[6 + slot])
            ACC2[rows, :] += dot_nt(dhidden, W[4 + slot])

        tiles(ffn_step)
        if f + 2 < 4:
            ffn_load[f + 2] = load_ffn(f + 2)
        chunk_matmul(f, lambda: DH[...])
        rs_core(f)
        VS[0, 8 + f : 9 + f, :] = row_sum(DH[...])

        def down_step(b, carry, f=f):
            cols = pl.ds(pl.multiple_of(b * 384, 384), 384)
            out = dot_tn(ACT[:, cols], COT[...]).astype(BF).reshape(4, 2, 3, 16, WIDTH)
            for k in range(3):
                CH[4 + k, f // 2, 2 * (f % 2) + b] = out[:, :, k]
            return carry

        lax.fori_loop(0, 2, down_step, 0)
        if f >= 1:
            rs_first(f - 1)

    for k in range(3):
        rs_core(4 + k)

    def second_back(rows, start):
        res = RES[rows, :]
        used = used_rows(start, TILE, WIDTH)
        FT[rows, :] = jnp.where(used, res + ACC1[rows, :] + db, 0.0).astype(BF)
        unit, inverse = norm_parts(res)
        dsecond = ACC2[rows, :]
        VS[0, 5:6, :] += jnp.sum(dsecond * unit, axis=0, keepdims=True)
        VS[0, 6:7, :] += jnp.sum(dsecond, axis=0, keepdims=True)
        g = dsecond * sg
        through = (
            g
            - jnp.mean(g, axis=-1, keepdims=True)
            - unit * jnp.mean(g * unit, axis=-1, keepdims=True)
        ) * inverse
        dres = COT[rows, :].astype(F32) + through
        RES[rows, :] = dres
        SEC[rows, :] = dres.astype(BF)
        DH[rows, :] = dot_nt(dres.astype(BF), W[3]).astype(BF)

    tiles(second_back)
    lo_store = load(FT, lo_hbm, iosem.at[2])
    far_dout = []
    for r in range(2):
        half = pl.ds(384 * r, 384)
        far_dout.append(
            remote(DH.at[:, half], FDO.at[:, half], xsend.at[2 + r], xrecv.at[2 + r], partner)
        )
    rs_first(3)
    VS[0, 7:8, :] = row_sum(COT[...])
    VS[0, 2:3, :] = row_sum(SEC[...])

    head = lax.broadcasted_iota(jnp.int32, (16, WIDTH), 0)
    column = lax.broadcasted_iota(jnp.int32, (16, WIDTH), 1)
    in_head = jnp.where((column >> 6) == head, 1.0, 0.0).astype(BF)
    product = DH[...].astype(F32) * ATT[...].astype(F32)
    rough = product.astype(BF)
    STAT[1] = dot_nt(in_head, rough) + dot_nt(in_head, (product - rough.astype(F32)).astype(BF))
    far_stats = remote(STAT, FSTAT, xsend.at[4], xrecv.at[4], partner)

    padded_transpose(ATT, XT)
    gone((0, 0, 0))
    chunk_matmul(7, lambda: SEC[...])
    rs_core(7)
    rs_first(4)
    rs_first(5)
    rs_mid(1)

    def own_queries(hp, carry):
        cols = pair_cols(hp)
        q = QO[:, cols]
        ko = KO[:, cols]
        kf = KF[:, cols]
        vo = VO[:, cols]
        vf = VF[:, cols]
        do = DH[:, cols]
        ko_t = ko.T
        kf_t = kf.T
        dq = []
        dk = None
        for h in range(2):
            logsum = STAT[0, pl.ds(2 * hp + h, 1), :]
            delta = STAT[1, pl.ds(2 * hp + h, 1), :]
            qm = q * select[h] + MF[h]
            qs = q * select[h]
            dom = do * select[h]
            near = jnp.exp(dot_nt(ko * select[h] + MF[2 + h], qm) - logsum)
            dnear = (near * (dot_nt(vo, dom) - delta)).astype(BF)
            far = jnp.exp(dot_nt(kf * select[h] + MF[6 + h], qm) - logsum)
            dfar = (far * (dot_nt(vf, dom) - delta)).astype(BF)
            dq.append(
                dot_nn(ko_t[64 * h : 64 * h + 64], dnear)
                + dot_nn(kf_t[64 * h : 64 * h + 64], dfar)
            )
            dk_h = dot_nn(dnear, qs)
            dv_h = dot_nn(near.astype(BF), dom)
            dk, dv = (dk_h, dv_h) if dk is None else (dk + dk_h, dv + dv_h)
        ACC1[:, cols] = dk
        ACC2[:, cols] = dv
        QO[:, cols] = (jnp.concatenate(dq, axis=0).T * 0.125).astype(BF)
        return carry

    lax.fori_loop(0, 2, own_queries, 0)
    rs_first(6)
    rs_mid(2)
    rs_second(0)
    lax.fori_loop(2, 4, own_queries, 0)
    rs_first(7)
    rs_mid(3)
    rs_second(1)
    rs_mid(4)
    lax.fori_loop(4, 6, own_queries, 0)
    rs_mid(5)
    rs_second(2)
    rs_third(0)

    def again(rows, start):
        unit, _ = norm_parts(TOK[rows, :].astype(F32))
        ATT[rows, :] = (unit * fg + fs).astype(BF)


    gone((1, 0, 0))
    chunk_matmul(8, lambda: QO[...])
    rs_core(8)
    rs_mid(6)
    rs_second(3)
    rs_third(1)

    far_stats.wait_recv()

    def far_queries(hp, carry):
        cols = pair_cols(hp)
        q = QF[:, cols]
        ko = KO[:, cols]
        vo = VO[:, cols]
        do = FDO[:, cols]
        dk = ACC1[:, cols]
        dv = ACC2[:, cols]
        for h in range(2):
            logsum = FSTAT[0, pl.ds(2 * hp + h, 1), :]
            delta = FSTAT[1, pl.ds(2 * hp + h, 1), :]
            qs = q * select[h]
            dom = do * select[h]
            probs = jnp.exp(dot_nt(ko * select[h] + MF[2 + h], qs + MF[4 + h]) - logsum)
            dscores = (probs * (dot_nt(vo, dom) - delta)).astype(BF)
            dk = dk + dot_nn(dscores, qs)
            dv = dv + dot_nn(probs.astype(BF), dom)
        KO[:, cols] = dk.astype(BF)
        VO[:, cols] = dv.astype(BF)
        return carry

    def chunk_in(c, joined):
        gone((c - 7, 0, 0))
        chunk_matmul(c, joined)
        rs_core(c)

    def keys_values(j):
        cols = slice(384 * j, 384 * (j + 1))
        return jnp.concatenate([KO[:, cols], VO[:, cols]], axis=1)

    far_dout[0].wait_recv()
    lax.fori_loop(0, 3, far_queries, 0)
    chunk_in(9, lambda: keys_values(0))
    rs_first(8)
    rs_mid(7)
    rs_second(4)
    rs_second(5)
    rs_third(2)
    rs_third(3)
    rs_fourth(0)
    far_dout[1].wait_recv()
    lax.fori_loop(3, 4, far_queries, 0)
    rs_first(9)
    lax.fori_loop(4, 6, far_queries, 0)
    chunk_in(10, lambda: keys_values(1))
    rs_mid(8)
    rs_second(6)
    rs_second(7)
    rs_third(4)
    rs_third(5)
    rs_fourth(1)
    rs_fourth(2)
    rs_fourth(3)

    VS[0, 0:1, :] = row_sum(QO[...])
    VS[0, 1:2, :] = row_sum(VO[...])

    def first_back(rows, start):
        unit, inverse = norm_parts(TOK[rows, :].astype(F32))
        dnormed = (
            dot_nt(QO[rows, :], W[0]) + dot_nt(KO[rows, :], W[1]) + dot_nt(VO[rows, :], W[2])
        )
        VS[0, 3:4, :] += jnp.sum(dnormed * unit, axis=0, keepdims=True)
        VS[0, 4:5, :] += jnp.sum(dnormed, axis=0, keepdims=True)
        g = dnormed * fg
        through = (
            g
            - jnp.mean(g, axis=-1, keepdims=True)
            - unit * jnp.mean(g * unit, axis=-1, keepdims=True)
        ) * inverse
        TOK[rows, :] = (RES[rows, :] + through).astype(BF)

    far_tokens.wait_send()
    tiles(first_back)
    gt_store = load(TOK, gt_hbm, iosem.at[3])

    def vec_send(step, peers):
        base = (0, 1, 4, 7)[step]
        for i, peer in enumerate(peers):
            remote(VS.at[step], VR.at[base + i], vsend.at[step], vrecv.at[step], peer)

    def vec_add(step):
        base = (0, 1, 4, 7)[step]
        if step == 0:
            all_bytes(VR.at[0:1], vrecv.at[0])
            total = VS[0] + VR[0]
        else:
            all_bytes(VR.at[base : base + 3], vrecv.at[step])
            total = (VS[step] + VR[base + 1]) + (VR[base] + VR[base + 2])
        VS[step + 1] = total

    vec_send(0, [sibling])
    rs_first(10)
    rs_mid(9)
    rs_second(8)
    rs_third(6)
    rs_third(7)
    rs_fourth(4)
    rs_fourth(5)
    vec_add(0)
    vec_send(1, z_peer[1:])
    rs_mid(10)
    rs_second(9)
    rs_third(8)
    rs_fourth(6)
    rs_second(10)
    vec_add(1)
    vec_send(2, x_peer[1:])
    rs_third(9)
    rs_fourth(7)
    rs_fourth(8)
    rs_third(10)
    vec_add(2)
    vec_send(3, y_peer[1:])
    rs_end(0)
    rs_fourth(9)
    rs_fourth(10)
    vec_add(3)

    vectors = VS[4]
    small = pltpu.roll(vectors, (WIDTH - 12 * dp) % WIDTH, 1)
    large = pltpu.roll(vectors, (WIDTH - 48 * (dp % 16)) % WIDTH, 1)[:, 0:128]
    row = lax.broadcasted_iota(jnp.int32, (16, 128), 0)
    large = jnp.sum(jnp.where(row == 8 + dp // 16, large, 0.0), axis=0, keepdims=True)
    for i, ref in enumerate(
        (gqb_ref, gvb_ref, gob_ref, gfg_ref, gfs_ref, gsg_ref, gss_ref, gdb_ref)
    ):
        ref[...] = small[i : i + 1, 0:12].reshape(12)
    gub_ref[...] = large[:, 0:48].reshape(48)

    for copy in far_dout:
        copy.wait_send()
    far_stats.wait_send()
    for key in list(landing):
        gone(key)
    all_bytes(VR.at[0:1], vsend.at[0])
    for step in range(1, 4):
        all_bytes(VR.at[3 * step - 2 : 3 * step + 1], vsend.at[step])
    lo_store.wait()
    gt_store.wait()


def finish(*refs):
    count = (len(refs) - 2) // 3
    sems = refs[3 * count :]
    hops = []
    for i in range(count):
        src, dst, held = refs[i], refs[count + i], refs[2 * count + i]
        hops.append(
            (
                pltpu.make_async_copy(src, held, sems[0].at[i]),
                pltpu.make_async_copy(held, dst, sems[1].at[i]),
            )
        )
    for first, _ in hops:
        first.start()
    for first, second in hops:
        first.wait()
        second.start()
    for _, second in hops:
        second.wait()


def body(
    tokens,
    input_weight,
    query_bias,
    value_bias,
    out_weight,
    out_bias,
    first_gain,
    first_shift,
    second_gain,
    second_shift,
    up_weight,
    up_bias,
    down_weight,
    down_bias,
    cotangent,
    row_counts,
    image_lengths,
):
    hbm = pl.BlockSpec(memory_space=pl.ANY)
    vmem = pl.BlockSpec(memory_space=pltpu.VMEM)
    smem = pl.BlockSpec(memory_space=pltpu.SMEM)
    rows = jax.ShapeDtypeStruct((ROWS, WIDTH), BF)

    def f32(*shape):
        return jax.ShapeDtypeStruct(shape, F32)

    def block(kind, *lead):
        return pltpu.VMEM((*lead, ROWS, WIDTH), kind)

    out = pl.pallas_call(
        kernel,
        out_shape=(
            rows,
            rows,
            f32(12, 3 * WIDTH),
            f32(12),
            f32(12),
            f32(12, WIDTH),
            f32(12),
            f32(12),
            f32(12),
            f32(12),
            f32(12),
            f32(12, 4 * WIDTH),
            f32(48),
            f32(48, WIDTH),
            f32(12),
        ),
        in_specs=[smem, smem] + [hbm] * 6 + [vmem] * 9,
        out_specs=(hbm, hbm) + (vmem,) * 13,
        scratch_shapes=[
            pltpu.VMEM((8, WIDTH, WIDTH), BF),
            pltpu.VMEM((SLOTS, 2, 4, 4, 2, 16, WIDTH), BF),
            pltpu.VMEM((CHUNKS, 2, 4, 4, 16, WIDTH), BF),
            pltpu.VMEM((CHUNKS - len(Y_FIRST), 3, 2, 4, 16, WIDTH), BF),
            pltpu.VMEM((CHUNKS - len(Y_FIRST), 3, 2, 16, WIDTH), BF),
            pltpu.VMEM((CHUNKS - len(Y_FIRST), 3, 16, WIDTH), BF),
            pltpu.VMEM((1, 3, 4, 4, 16, 384), BF),
            pltpu.VMEM((1, 3, 4, 16, 384), BF),
            pltpu.VMEM((1, 3, 16, 384), BF),
            pltpu.VMEM((1, 2, 16, 384), F32),
            block(BF),
            block(BF),
            pltpu.VMEM((2, 16, ROWS), F32),
            pltpu.VMEM((2, 16, ROWS), F32),
        ]
        + [block(BF)] * 12
        + [
            pltpu.VMEM((1024, ROWS), BF),
            pltpu.VMEM((1024, ROWS), BF),
            block(F32),
            block(F32, 2),
            pltpu.VMEM((8, ROWS, 128), BF),
            pltpu.VMEM((ROWS, 384), BF),
            pltpu.VMEM((16, ROWS), F32),
            pltpu.VMEM((16, ROWS), F32),
            pltpu.VMEM((5, 16, WIDTH), F32),
            pltpu.VMEM((10, 16, WIDTH), F32),
            pltpu.SemaphoreType.DMA((8,)),
            pltpu.SemaphoreType.DMA((3,)),
            pltpu.SemaphoreType.DMA((4,)),
            pltpu.SemaphoreType.DMA((5,)),
            pltpu.SemaphoreType.DMA((5,)),
            pltpu.SemaphoreType.DMA((len(STEPS),)),
            pltpu.SemaphoreType.DMA((len(STEPS),)),
            pltpu.SemaphoreType.DMA((4,)),
            pltpu.SemaphoreType.DMA((4,)),
        ],
        compiler_params=pltpu.CompilerParams(
            collective_id=0, has_side_effects=True, vmem_limit_bytes=63 * 2**20
        ),
        name="encoder",
    )(
        row_counts,
        image_lengths,
        tokens,
        cotangent,
        input_weight,
        out_weight,
        up_weight,
        down_weight,
        query_bias,
        value_bias,
        out_bias,
        first_gain,
        first_shift,
        second_gain,
        second_shift,
        up_bias,
        down_bias,
    )
    return pl.pallas_call(
        finish,
        out_shape=tuple(jax.ShapeDtypeStruct(value.shape, value.dtype) for value in out),
        in_specs=[hbm] * len(out),
        out_specs=(hbm,) * len(out),
        scratch_shapes=[pltpu.VMEM(value.shape, value.dtype) for value in out]
        + [pltpu.SemaphoreType.DMA((len(out),))] * 2,
        name="finish",
    )(*out)


def solution(mesh):
    rows = P(("seq", "dp"), None)
    split = P("dp", None)
    line = P("dp")
    return jax.shard_map(
        body,
        mesh=mesh,
        in_specs=(rows,) + (P(),) * 13 + (rows, split, split),
        out_specs=(
            rows,
            rows,
            split,
            line,
            line,
            split,
            line,
            line,
            line,
            line,
            line,
            split,
            line,
            split,
            line,
        ),
        check_vma=False,
    )
```

```python
import jax
import jax.numpy as jnp
from jax import lax
from jax.experimental import pallas as pl
from jax.experimental.pallas import tpu as pltpu
from jax.sharding import PartitionSpec as P

F32 = jnp.float32
BF = jnp.bfloat16
EPS = 1e-06
ROWS = 512
WIDTH = 768
TILE = 256
CHUNKS = 11
SLOTS = 7
FEATURES = 37
PARTS = (
    ((2, 0, 768),),
    ((0, 0, 768),),
    ((1, 0, 768),),
    ((0, 0, 768),),
    ((1, 0, 768),),
    ((0, 0, 768),),
    ((1, 0, 768),),
    ((0, 0, 768),),
    ((0, 0, 384), (1, 384, 768)),
    ((0, 0, 384), (1, 384, 768)),
    ((3, 0, 384), (4, 384, 768)),
)
Y_FIRST = (0,)
STEPS = [(c, 0, 0) for c in range(CHUNKS)]
STEPS += [(c, s, p) for c in range(CHUNKS) for p, _, _ in PARTS[c] for s in (1, 2, 3)]
STEPS += [(c, 4, 2) for c in Y_FIRST]
STEPS += [(c, 5, p) for c in range(CHUNKS) for p, _, _ in PARTS[c] if p < 2]
MESH = pl.DeviceIdType.MESH


def dot_nn(left, right):
    return lax.dot_general(left, right, (((1,), (0,)), ((), ())), preferred_element_type=F32)


def dot_nt(left, right):
    return lax.dot_general(left, right, (((1,), (1,)), ((), ())), preferred_element_type=F32)


def dot_tn(left, right):
    return lax.dot_general(left, right, (((0,), (0,)), ((), ())), preferred_element_type=F32)


def norm_parts(block):
    centred = block - jnp.mean(block, axis=-1, keepdims=True)
    spread = jnp.mean(centred * centred, axis=-1, keepdims=True)
    inverse = lax.rsqrt(spread + EPS)
    return centred * inverse, inverse


def kernel(
    counts_ref,
    lengths_ref,
    tokens_hbm,
    cot_hbm,
    wi_hbm,
    wo_hbm,
    wu_hbm,
    wd_hbm,
    qb_ref,
    vb_ref,
    ob_ref,
    fg_ref,
    fs_ref,
    sg_ref,
    ss_ref,
    ub_ref,
    db_ref,
    lo_hbm,
    gt_hbm,
    gi_ref,
    gqb_ref,
    gvb_ref,
    go_ref,
    gob_ref,
    gfg_ref,
    gfs_ref,
    gsg_ref,
    gss_ref,
    gu_ref,
    gub_ref,
    gd_ref,
    gdb_ref,
    W,
    CH,
    R0,
    R1,
    R2,
    R3,
    S1,
    S2,
    S3,
    S4,
    FT,
    FDO,
    STAT,
    FSTAT,
    QO,
    KO,
    VO,
    QF,
    KF,
    VF,
    TOK,
    COT,
    ATT,
    SEC,
    ACT,
    DH,
    XT,
    XN,
    RES,
    ACC,
    MF,
    PB,
    TOP,
    SUM,
    VS,
    VR,
    wsem,
    dsem,
    iosem,
    xsend,
    xrecv,
    rsend,
    rrecv,
    vsend,
    vrecv,
):
    ACC1, ACC2 = ACC.at[0], ACC.at[1]
    part = lax.axis_index("seq")
    dp = lax.axis_index("dp")
    y_lo = dp // 32
    z = (dp // 8) % 4
    x = (dp // 2) % 4
    core = dp % 2
    y = 2 * part + y_lo

    def device(yy, zz, xx, cc):
        return (yy // 2, ((yy % 2) * 4 + zz) * 8 + xx * 2 + cc)

    sibling = device(y, z, x, 1 - core)
    z_of = [(z + k) % 4 for k in range(4)]
    x_of = [(x + k) % 4 for k in range(4)]
    y_of = [(y + k) % 4 for k in range(4)]
    z_a, z_b = z + 1 - 2 * (z % 2), 3 - z
    x_a, x_b = x + 1 - 2 * (x % 2), 3 - x
    near_z = [device(y, v, x, core) for v in (z_a, z_b)]
    near_x = [device(y, z, v, core) for v in (x_a, x_b)]
    z_peer = [device(y, v, x, core) for v in z_of]
    x_peer = [device(y, z, v, core) for v in x_of]
    y_peer = [device(v, z, x, core) for v in y_of]
    partner = y_peer[2]

    def load(src, dst, sem):
        copy = pltpu.make_async_copy(src, dst, sem)
        copy.start()
        return copy

    tok_load = load(tokens_hbm, TOK, iosem.at[0])
    w_load = {}
    for i in range(3):
        w_load[i] = load(wi_hbm.at[:, pl.ds(WIDTH * i, WIDTH)], W.at[i], wsem.at[i])
    cot_load = load(cot_hbm, COT, iosem.at[1])
    w_load[3] = load(wo_hbm, W.at[3], wsem.at[3])

    def load_ffn(f):
        slot = f % 2
        up = load(wu_hbm.at[:, pl.ds(WIDTH * f, WIDTH)], W.at[4 + slot], wsem.at[4 + slot])
        down = load(wd_hbm.at[pl.ds(WIDTH * f, WIDTH)], W.at[6 + slot], wsem.at[6 + slot])
        return up, down

    ffn_load = {0: load_ffn(0), 1: load_ffn(1)}
    down_load = [
        load(wd_hbm.at[pl.ds(2 * WIDTH + ROWS * i, ROWS)], ref, dsem.at[i])
        for i, ref in enumerate((SEC, ACT, DH))
    ]

    barrier = pltpu.get_barrier_semaphore()
    for peer in [sibling] + z_peer[1:] + x_peer[1:] + y_peer[1:]:
        pl.semaphore_signal(barrier, inc=1, device_id=peer, device_id_type=MESH)
    pl.semaphore_wait(barrier, 10)

    def remote(src, dst, send, recv, peer):
        copy = pltpu.make_async_remote_copy(
            src_ref=src,
            dst_ref=dst,
            send_sem=send,
            recv_sem=recv,
            device_id=peer,
            device_id_type=MESH,
        )
        copy.start()
        return copy

    far_tokens = remote(tokens_hbm, FT, xsend.at[0], xrecv.at[0], partner)

    def all_bytes(ref, sem):
        pltpu.make_async_copy(ref, ref, sem).wait()

    landing = {}

    def send_all(key, dst, copies):
        i = STEPS.index(key)
        landing[key] = dst
        for src, into, peer in copies:
            remote(src, into, rsend.at[i], rrecv.at[i], peer)

    def received(key):
        all_bytes(landing[key], rrecv.at[STEPS.index(key)])

    def gone(key):
        all_bytes(landing.pop(key), rsend.at[STEPS.index(key)])

    def rs_core(c):
        src = CH.at[c % SLOTS, :, :, :, 1 - core]
        send_all((c, 0, 0), R0.at[c], [(src, R0.at[c], sibling)])

    def row_of(c):
        return c - sum(first < c for first in Y_FIRST)

    def y_slot(c):
        n = Y_FIRST.index(c)
        return n, 384

    def rs_first(c):
        received((c, 0, 0))

        def add(i, carry):
            yl, zz = i // 4, i % 4
            R0[c, yl, zz] = (
                R0[c, yl, zz].astype(F32) + CH[c % SLOTS, yl, zz, :, core].astype(F32)
            ).astype(BF)
            return carry

        lax.fori_loop(0, 8, add, 0)
        for p, lo, hi in PARTS[c]:
            copies = []
            if p == 2:
                n, width = y_slot(c)
                whole = S1.at[n, :, :, :, :, 0:width]
                for k in (2, 1, 3):
                    start = pl.multiple_of(lo + width * (y_of[k] // 2), 128)
                    src = R0.at[c, y_of[k] % 2, :, :, :, pl.ds(start, width)]
                    copies.append((src, S1.at[n, k - 1, :, :, :, 0:width], y_peer[k]))
            elif p > 2:
                whole = R1.at[row_of(c), :, :, :, :, lo:hi]
                for k in (2, 1, 3):
                    if p == 3:
                        src, peer = R0.at[c, :, z_of[k], :, :, lo:hi], z_peer[k]
                    else:
                        src, peer = R0.at[c, :, :, x_of[k], :, lo:hi], x_peer[k]
                    copies.append((src, R1.at[row_of(c), k - 1, :, :, :, lo:hi], peer))
            else:
                whole = R1.at[row_of(c), 0:2, :, :, :, lo:hi]
                a, b = (z_a, z_b) if p == 0 else (x_a, x_b)
                across = 3 - a
                peers = near_z if p == 0 else near_x
                for half, nearest in ((0, a), (1, b)):
                    for spot, wanted in ((1, across), (0, nearest)):
                        dst = R1.at[row_of(c), half, spot, :, :, lo:hi]
                        copies.append((shares(c, p, half, wanted, lo, hi), dst, peers[half]))
            send_all((c, 1, p), whole, copies)

    def shares(c, p, yl, v, lo, hi):
        if p == 0:
            return R0.at[c, yl, v, :, :, lo:hi]
        return R0.at[c, yl, :, v, :, lo:hi]

    def rs_mid(c):
        for p, lo, hi in PARTS[c]:
            if p > 1:
                continue
            received((c, 1, p))
            v, a, b = (z, z_a, z_b) if p == 0 else (x, x_a, x_b)
            for half, other in ((0, b), (1, a)):
                for spot, kept in ((0, v), (1, other)):
                    at = (row_of(c), half, spot, slice(None), slice(None), slice(lo, hi))
                    own = shares(c, p, half, kept, lo, hi)[...]
                    R1[at] = (own.astype(F32) + R1[at].astype(F32)).astype(BF)
            peers = near_z if p == 0 else near_x
            copies = []
            for half in range(2):
                src = R1.at[row_of(c), half, 1, :, :, lo:hi]
                copies.append((src, R1.at[row_of(c), 2, half, :, :, lo:hi], peers[1 - half]))
            send_all((c, 5, p), R1.at[row_of(c), 2, :, :, :, lo:hi], copies)

    def rs_second(c):
        for p, lo, hi in PARTS[c]:
            received((c, 5 if p < 2 else 1, p))
            copies = []
            if p == 2:
                n, width = y_slot(c)
                start = pl.multiple_of(lo + width * part, 128)
                for zz in range(4):
                    total = R0[c, y_lo, zz, :, :, pl.ds(start, width)].astype(F32)
                    for k in range(3):
                        total = total + S1[n, k, zz, :, :, 0:width].astype(F32)
                    S1[n, 0, zz, :, :, 0:width] = total.astype(BF)
                whole = S2.at[n, :, :, :, 0:width]
            elif p > 2:
                for yl in range(2):
                    if p == 3:
                        total = R0[c, yl, z, :, :, lo:hi].astype(F32)
                    else:
                        total = R0[c, yl, :, x, :, lo:hi].astype(F32)
                    for k in range(3):
                        total = total + R1[row_of(c), k, yl, :, :, lo:hi].astype(F32)
                    R1[row_of(c), 0, yl, :, :, lo:hi] = total.astype(BF)
                whole = R2.at[row_of(c), :, :, :, lo:hi]
            else:
                for half in range(2):
                    at = (row_of(c), half, 0, slice(None), slice(None), slice(lo, hi))
                    total = R1[at].astype(F32) + R1[row_of(c), 2, half, :, :, lo:hi].astype(F32)
                    R1[at] = total.astype(BF)
                whole = R2.at[row_of(c), :, :, :, lo:hi]
            for k in (2, 1, 3):
                if p == 3:
                    src = R1.at[row_of(c), 0, :, x_of[k], :, lo:hi]
                    dst, peer = R2.at[row_of(c), k - 1, :, :, lo:hi], x_peer[k]
                elif p == 4:
                    src = R1.at[row_of(c), 0, :, z_of[k], :, lo:hi]
                    dst, peer = R2.at[row_of(c), k - 1, :, :, lo:hi], z_peer[k]
                elif p == 0:
                    src = R1.at[row_of(c), 0:2, 0, x_of[k], :, lo:hi]
                    dst, peer = R2.at[row_of(c), k - 1, :, :, lo:hi], x_peer[k]
                elif p == 1:
                    src = R1.at[row_of(c), 0:2, 0, z_of[k], :, lo:hi]
                    dst, peer = R2.at[row_of(c), k - 1, :, :, lo:hi], z_peer[k]
                else:
                    src = S1.at[n, 0, z_of[k], :, :, 0:width]
                    dst, peer = S2.at[n, k - 1, :, :, 0:width], z_peer[k]
                copies.append((src, dst, peer))
            send_all((c, 2, p), whole, copies)

    def rs_third(c):
        for p, lo, hi in PARTS[c]:
            received((c, 2, p))
            copies = []
            if p == 2:
                n, width = y_slot(c)
                total = S1[n, 0, z, :, :, 0:width].astype(F32)
                for k in range(3):
                    total = total + S2[n, k, :, :, 0:width].astype(F32)
                S2[n, 0, :, :, 0:width] = total.astype(BF)
                whole = S3.at[n, :, :, 0:width]
            else:
                if p == 3:
                    total = R1[row_of(c), 0, :, x, :, lo:hi].astype(F32)
                elif p == 4:
                    total = R1[row_of(c), 0, :, z, :, lo:hi].astype(F32)
                elif p == 0:
                    total = R1[row_of(c), 0:2, 0, x, :, lo:hi].astype(F32)
                else:
                    total = R1[row_of(c), 0:2, 0, z, :, lo:hi].astype(F32)
                for k in range(3):
                    total = total + R2[row_of(c), k, :, :, lo:hi].astype(F32)
                R2[row_of(c), 0, :, :, lo:hi] = total.astype(BF)
                whole = R3.at[row_of(c), :, :, lo:hi]
            for k in (2, 1, 3):
                if p == 2:
                    src = S2.at[n, 0, x_of[k], :, 0:width]
                    dst, peer = S3.at[n, k - 1, :, 0:width], x_peer[k]
                else:
                    src = R2.at[row_of(c), 0, y_of[k] % 2, :, lo:hi]
                    dst, peer = R3.at[row_of(c), k - 1, :, lo:hi], y_peer[k]
                copies.append((src, dst, peer))
            send_all((c, 3, p), whole, copies)

    def store_share(c, lo, hi, total):
        if c < 4:
            gu_ref[:, WIDTH * c + lo : WIDTH * c + hi] = total[0:12]
        elif c < 7:
            gd_ref[16 * (c - 4) : 16 * (c - 3), lo:hi] = total
        elif c == 7:
            go_ref[:, lo:hi] = total[0:12]
        else:
            for b in range(lo // 384, hi // 384):
                start = 384 * b if c == 8 else WIDTH * (b + 1) + 384 * (c - 9)
                gi_ref[:, start : start + 384] = total[0:12, 384 * b - lo : 384 * (b + 1) - lo]

    def rs_fourth(c):
        for p, lo, hi in PARTS[c]:
            received((c, 3, p))
            if p == 2:
                n, width = y_slot(c)
                total = S2[n, 0, x, :, 0:width].astype(F32)
                for k in range(3):
                    total = total + S3[n, k, :, 0:width].astype(F32)
                S4[n, 0, :, 0:width] = total
                dst = S4.at[n, 1, :, 0:width]
                send_all((c, 4, p), dst, [(S4.at[n, 0, :, 0:width], dst, partner)])
            else:
                total = (R2[row_of(c), 0, y_lo, :, lo:hi].astype(F32) + R3[row_of(c), 1, :, lo:hi].astype(F32)) + (
                    R3[row_of(c), 0, :, lo:hi].astype(F32) + R3[row_of(c), 2, :, lo:hi].astype(F32)
                )
                store_share(c, lo, hi, total)

    def rs_end(c):
        n, width = y_slot(c)
        received((c, 4, 2))
        mine = S4[n, 0, :, 0:width]
        other = S4[n, 1, :, 0:width]
        low = jnp.where(part == 0, mine, other)
        high = jnp.where(part == 0, other, mine)
        lo = PARTS[c][-1][1]
        store_share(c, lo, lo + 2 * width, jnp.concatenate([low, high], axis=1))

    counts0 = counts_ref[0, 0]
    counts1 = counts_ref[0, 1]
    end0 = lengths_ref[0, 0]
    end1 = end0 + lengths_ref[0, 1]
    end2 = end1 + lengths_ref[0, 2]
    end3 = end2 + lengths_ref[0, 3]

    def used_rows(start, size, width):
        place = lax.broadcasted_iota(jnp.int32, (size, width), 0) + start
        return place < counts0 + part * (counts1 - counts0)

    def features(base, which):
        place = lax.broadcasted_iota(jnp.int32, (ROWS, 128), 0)
        shifted = place + which * counts0
        index = jnp.zeros((ROWS, 128), jnp.int32)
        for end in (end0, end1, end2, end3):
            index = index + jnp.where(end <= shifted, 1, 0)
        owned = counts0 + which * (counts1 - counts0)
        ids = jnp.where(place < owned, index, 4 + which * ROWS + place)
        lane = lax.broadcasted_iota(jnp.int32, (ROWS, 128), 1)
        high = lane >= 64
        spot = jnp.where(high, lane - 64, lane)
        digit = jnp.where(
            spot < 16, ids & 15, jnp.where(spot < 32, ((ids >> 4) & 15) + 16, (ids >> 8) + 32)
        )
        hot = jnp.where(digit == spot, 1.0, 0.0)
        query = jnp.where(spot < FEATURES, 1.0 - hot, 0.0)
        key = hot * -1e30
        MF[base] = jnp.where(high, query, 0.0).astype(BF)
        MF[base + 1] = jnp.where(high, 0.0, query).astype(BF)
        MF[base + 2] = jnp.where(high, key, 0.0).astype(BF)
        MF[base + 3] = jnp.where(high, 0.0, key).astype(BF)

    features(0, part)
    features(4, 1 - part)
    lane_row = lax.broadcasted_iota(jnp.int32, (1, 128), 1)
    select = [
        jnp.where(lane_row < 64, 1.0, 0.0).astype(BF),
        jnp.where(lane_row < 64, 0.0, 1.0).astype(BF),
    ]

    rho = lax.broadcasted_iota(jnp.int32, (ROWS, 384), 0)
    feature = lax.broadcasted_iota(jnp.int32, (ROWS, 384), 1)
    within = rho & 15
    PB[...] = jnp.where(
        (within < 12) & (feature == (rho >> 4) * 12 + within), 1.0, 0.0
    ).astype(BF)

    def padded_transpose(source, into):
        for b in range(2):
            into[ROWS * b : ROWS * (b + 1), :] = dot_nt(
                PB[...], source[:, 384 * b : 384 * (b + 1)]
            ).astype(BF)

    def chunk_matmul(c, right):
        left = XT if c < 8 else XN

        def block(m, carry):
            cols = pl.ds(pl.multiple_of(m * TILE, TILE), TILE)
            out = dot_nn(left[...], right[:, cols]).astype(BF)
            CH[c % SLOTS, :, :, :, :, :, cols] = out.reshape(2, 4, 4, 2, 16, TILE)
            return carry

        lax.fori_loop(0, 3, block, 0)

    ones = jnp.ones((16, ROWS), BF)

    def row_sum(block):
        return dot_nn(ones, block)[0:1]

    def tiles(step):
        def run(t, carry):
            step(pl.ds(pl.multiple_of(t * TILE, TILE), TILE), t * TILE)
            return carry

        lax.fori_loop(0, ROWS // TILE, run, 0)

    qb = qb_ref[...].reshape(1, WIDTH)
    vb = vb_ref[...].reshape(1, WIDTH)
    ob = ob_ref[...].reshape(1, WIDTH)
    fg = fg_ref[...].reshape(1, WIDTH)
    fs = fs_ref[...].reshape(1, WIDTH)
    sg = sg_ref[...].reshape(1, WIDTH)
    ss = ss_ref[...].reshape(1, WIDTH)
    db = db_ref[...].reshape(1, WIDTH)

    def projection(source, q_ref, k_ref, v_ref):
        def step(rows, start):
            unit, _ = norm_parts(source[rows, :].astype(F32))
            normed = (unit * fg + fs).astype(BF)
            q = (dot_nn(normed, W[0]) + qb).astype(BF)
            q_ref[rows, :] = q * jnp.asarray(0.125, BF)
            k_ref[rows, :] = dot_nn(normed, W[1]).astype(BF)
            v_ref[rows, :] = (dot_nn(normed, W[2]) + vb).astype(BF)

        return step

    tok_load.wait()
    for i in range(3):
        w_load[i].wait()
    tiles(projection(TOK, QO, KO, VO))

    cot_load.wait()

    def mask_cot(rows, start):
        used = used_rows(start, TILE, WIDTH)
        COT[rows, :] = jnp.where(used, COT[rows, :].astype(F32), 0.0).astype(BF)

    tiles(mask_cot)

    def pair_cols(hp):
        return pl.ds(pl.multiple_of(hp * 128, 128), 128)

    def mix_at(hp, h):
        start = pl.multiple_of(128 * (hp % 4) + 64 * h, 64)
        return hp // 4, pl.ds(start, 64), slice(0, ROWS)

    def attend_own(hp, carry):
        cols = pair_cols(hp)
        q = QO[:, cols]
        keys = KO[:, cols]
        values = VO[:, cols].T
        for h in range(2):
            row = pl.ds(2 * hp + h, 1)
            scores = dot_nt(keys * select[h] + MF[2 + h], q * select[h] + MF[h])
            top = jnp.max(scores, axis=0, keepdims=True)
            probs = jnp.exp(scores - top)
            TOP[row, :] = top
            SUM[row, :] = jnp.sum(probs, axis=0, keepdims=True)
            own = slice(64 * h, 64 * h + 64)
            ACC[mix_at(hp, h)] = dot_nn(values[own], probs.astype(BF))
        return carry

    lax.fori_loop(0, 6, attend_own, 0)

    def attend_far(hp, carry):
        cols = pair_cols(hp)
        q = QO[:, cols]
        keys = KF[:, cols]
        values = VF[:, cols].T
        outs = []
        for h in range(2):
            row = pl.ds(2 * hp + h, 1)
            own = slice(64 * h, 64 * h + 64)
            scores = dot_nt(keys * select[h] + MF[6 + h], q * select[h] + MF[h])
            before = TOP[row, :]
            top = jnp.maximum(before, jnp.max(scores, axis=0, keepdims=True))
            shrink = jnp.exp(before - top)
            probs = jnp.exp(scores - top)
            total = SUM[row, :] * shrink + jnp.sum(probs, axis=0, keepdims=True)
            mixed = ACC[mix_at(hp, h)] * shrink + dot_nn(values[own], probs.astype(BF))
            STAT[0, row, :] = top + jnp.log(total)
            outs.append(mixed * (1.0 / total))
        ATT[:, cols] = jnp.concatenate(outs, axis=0).T.astype(BF)
        return carry

    def again(rows, start):
        unit, _ = norm_parts(TOK[rows, :].astype(F32))
        ATT[rows, :] = (unit * fg + fs).astype(BF)

    tiles(again)
    padded_transpose(ATT, XN)

    for copy in down_load:
        copy.wait()
    for f in range(2):
        ffn_load[f][1].wait()

    def early_step(rows, start):
        dout = COT[rows, :]
        block = start // TILE * 2

        def keep(f, lo, value):
            CH[f, 0, pl.ds(block, 2), :, :, :, lo : lo + value.shape[1]] = value.astype(BF).reshape(
                2, 4, 2, 16, value.shape[1]
            )

        for f in range(2):
            keep(f, 0, dot_nt(dout, W[6 + f]))
        keep(2, 0, dot_nt(dout, SEC[...]))
        middle = dot_nt(dout, ACT[...])
        keep(2, 512, middle[:, 0:256])
        keep(3, 0, middle[:, 256:512])
        keep(3, 256, dot_nt(dout, DH[...]))

    tiles(early_step)

    far_tokens.wait_recv()
    tiles(projection(FT, QF, KF, VF))
    lax.fori_loop(0, 6, attend_far, 0)

    w_load[3].wait()

    def out_step(rows, start):
        res = TOK[rows, :].astype(F32) + dot_nn(ATT[rows, :], W[3]) + ob
        RES[rows, :] = res
        unit, _ = norm_parts(res)
        SEC[rows, :] = (unit * sg + ss).astype(BF)
        ACC1[rows, :] = jnp.zeros((TILE, WIDTH), F32)
        ACC2[rows, :] = jnp.zeros((TILE, WIDTH), F32)

    tiles(out_step)
    padded_transpose(SEC, XT)
    VS[0] = jnp.zeros((16, WIDTH), F32)

    for f in range(4):
        slot = f % 2
        ffn_load[f][0].wait()
        if f > 1:
            ffn_load[f][1].wait()
        ub = ub_ref[WIDTH * f : WIDTH * (f + 1)].reshape(1, WIDTH)

        def ffn_step(rows, start, f=f, slot=slot, ub=ub):
            early = CH[f, 0, pl.ds(start // TILE * 2, 2)].reshape(TILE, WIDTH).astype(F32)
            hidden = dot_nn(SEC[rows, :], W[4 + slot]) + ub
            cdf = 0.5 * (1.0 + lax.erf(hidden * 0.7071067811865476))
            density = jnp.exp(-0.5 * hidden * hidden) * 0.3989422804014327
            active = (hidden * cdf).astype(BF)
            ACT[rows, :] = active
            dhidden = (early * (cdf + hidden * density)).astype(BF)
            DH[rows, :] = dhidden
            ACC1[rows, :] += dot_nn(active, W[6 + slot])
            ACC2[rows, :] += dot_nt(dhidden, W[4 + slot])

        tiles(ffn_step)
        if f + 2 < 4:
            ffn_load[f + 2] = load_ffn(f + 2)
        if f >= 1:
            rs_first(f - 1)
        chunk_matmul(f, DH)
        rs_core(f)
        VS[0, 8 + f : 9 + f, :] = row_sum(DH[...])

        def down_step(b, carry, f=f):
            cols = pl.ds(pl.multiple_of(b * 384, 384), 384)
            out = dot_tn(ACT[:, cols], COT[...]).astype(BF).reshape(4, 2, 3, 16, WIDTH)
            for k in range(3):
                CH[4 + k, f // 2, 2 * (f % 2) + b] = out[:, :, k]
            return carry

        lax.fori_loop(0, 2, down_step, 0)
    for k in range(3):
        rs_core(4 + k)

    def second_back(rows, start):
        res = RES[rows, :]
        used = used_rows(start, TILE, WIDTH)
        FT[rows, :] = jnp.where(used, res + ACC1[rows, :] + db, 0.0).astype(BF)
        unit, inverse = norm_parts(res)
        dsecond = ACC2[rows, :]
        VS[0, 5:6, :] += jnp.sum(dsecond * unit, axis=0, keepdims=True)
        VS[0, 6:7, :] += jnp.sum(dsecond, axis=0, keepdims=True)
        g = dsecond * sg
        through = (
            g
            - jnp.mean(g, axis=-1, keepdims=True)
            - unit * jnp.mean(g * unit, axis=-1, keepdims=True)
        ) * inverse
        dres = COT[rows, :].astype(F32) + through
        RES[rows, :] = dres
        SEC[rows, :] = dres.astype(BF)
        DH[rows, :] = dot_nt(dres.astype(BF), W[3]).astype(BF)

    tiles(second_back)
    lo_store = load(FT, lo_hbm, iosem.at[2])
    far_dout = []
    for r in range(2):
        half = pl.ds(384 * r, 384)
        far_dout.append(
            remote(DH.at[:, half], FDO.at[:, half], xsend.at[2 + r], xrecv.at[2 + r], partner)
        )
    rs_first(3)
    VS[0, 7:8, :] = row_sum(COT[...])
    VS[0, 2:3, :] = row_sum(SEC[...])

    head = lax.broadcasted_iota(jnp.int32, (16, WIDTH), 0)
    column = lax.broadcasted_iota(jnp.int32, (16, WIDTH), 1)
    in_head = jnp.where((column >> 6) == head, 1.0, 0.0).astype(BF)
    product = DH[...].astype(F32) * ATT[...].astype(F32)
    rough = product.astype(BF)
    STAT[1] = dot_nt(in_head, rough) + dot_nt(in_head, (product - rough.astype(F32)).astype(BF))
    far_stats = remote(STAT, FSTAT, xsend.at[4], xrecv.at[4], partner)

    padded_transpose(ATT, XT)
    gone((0, 0, 0))
    chunk_matmul(7, SEC)
    rs_core(7)
    rs_first(4)
    rs_first(5)
    rs_mid(1)

    def own_queries(hp, carry):
        cols = pair_cols(hp)
        q = QO[:, cols]
        ko = KO[:, cols]
        kf = KF[:, cols]
        vo = VO[:, cols]
        vf = VF[:, cols]
        do = DH[:, cols]
        ko_t = ko.T
        kf_t = kf.T
        dq = []
        dk = None
        for h in range(2):
            logsum = STAT[0, pl.ds(2 * hp + h, 1), :]
            delta = STAT[1, pl.ds(2 * hp + h, 1), :]
            qm = q * select[h] + MF[h]
            qs = q * select[h]
            dom = do * select[h]
            near = jnp.exp(dot_nt(ko * select[h] + MF[2 + h], qm) - logsum)
            dnear = (near * (dot_nt(vo, dom) - delta)).astype(BF)
            far = jnp.exp(dot_nt(kf * select[h] + MF[6 + h], qm) - logsum)
            dfar = (far * (dot_nt(vf, dom) - delta)).astype(BF)
            dq.append(
                dot_nn(ko_t[64 * h : 64 * h + 64], dnear)
                + dot_nn(kf_t[64 * h : 64 * h + 64], dfar)
            )
            dk_h = dot_nn(dnear, qs)
            dv_h = dot_nn(near.astype(BF), dom)
            dk, dv = (dk_h, dv_h) if dk is None else (dk + dk_h, dv + dv_h)
        ACC1[:, cols] = dk
        ACC2[:, cols] = dv
        QO[:, cols] = (jnp.concatenate(dq, axis=0).T * 0.125).astype(BF)
        return carry

    lax.fori_loop(0, 2, own_queries, 0)
    rs_first(6)
    rs_mid(2)
    rs_second(0)
    lax.fori_loop(2, 4, own_queries, 0)
    rs_first(7)
    rs_mid(3)
    rs_second(1)
    rs_mid(4)
    lax.fori_loop(4, 6, own_queries, 0)
    rs_mid(5)
    rs_second(2)
    rs_third(0)

    def again(rows, start):
        unit, _ = norm_parts(TOK[rows, :].astype(F32))
        ATT[rows, :] = (unit * fg + fs).astype(BF)


    gone((1, 0, 0))
    chunk_matmul(8, QO)
    rs_core(8)
    rs_mid(6)
    rs_second(3)
    rs_third(1)

    far_stats.wait_recv()

    def far_queries(hp, carry):
        cols = pair_cols(hp)
        q = QF[:, cols]
        ko = KO[:, cols]
        vo = VO[:, cols]
        do = FDO[:, cols]
        dk = ACC1[:, cols]
        dv = ACC2[:, cols]
        for h in range(2):
            logsum = FSTAT[0, pl.ds(2 * hp + h, 1), :]
            delta = FSTAT[1, pl.ds(2 * hp + h, 1), :]
            qs = q * select[h]
            dom = do * select[h]
            probs = jnp.exp(dot_nt(ko * select[h] + MF[2 + h], qs + MF[4 + h]) - logsum)
            dscores = (probs * (dot_nt(vo, dom) - delta)).astype(BF)
            dk = dk + dot_nn(dscores, qs)
            dv = dv + dot_nn(probs.astype(BF), dom)
        KO[:, cols] = dk.astype(BF)
        VO[:, cols] = dv.astype(BF)
        return carry

    def chunk_in(c):
        cols = slice(384 * (c - 9), 384 * (c - 8))
        ACT[:, 0:384] = KO[:, cols]
        ACT[:, 384:768] = VO[:, cols]
        gone((c - 7, 0, 0))
        chunk_matmul(c, ACT)
        rs_core(c)

    far_dout[0].wait_recv()
    lax.fori_loop(0, 3, far_queries, 0)
    chunk_in(9)
    rs_first(8)
    rs_mid(7)
    rs_second(4)
    rs_second(5)
    rs_third(2)
    rs_third(3)
    rs_fourth(0)
    far_dout[1].wait_recv()
    lax.fori_loop(3, 4, far_queries, 0)
    rs_first(9)
    lax.fori_loop(4, 6, far_queries, 0)
    chunk_in(10)
    rs_mid(8)
    rs_second(6)
    rs_second(7)
    rs_third(4)
    rs_third(5)
    rs_fourth(1)
    rs_fourth(2)
    rs_fourth(3)

    VS[0, 0:1, :] = row_sum(QO[...])
    VS[0, 1:2, :] = row_sum(VO[...])

    def first_back(rows, start):
        unit, inverse = norm_parts(TOK[rows, :].astype(F32))
        dnormed = (
            dot_nt(QO[rows, :], W[0]) + dot_nt(KO[rows, :], W[1]) + dot_nt(VO[rows, :], W[2])
        )
        VS[0, 3:4, :] += jnp.sum(dnormed * unit, axis=0, keepdims=True)
        VS[0, 4:5, :] += jnp.sum(dnormed, axis=0, keepdims=True)
        g = dnormed * fg
        through = (
            g
            - jnp.mean(g, axis=-1, keepdims=True)
            - unit * jnp.mean(g * unit, axis=-1, keepdims=True)
        ) * inverse
        TOK[rows, :] = (RES[rows, :] + through).astype(BF)

    far_tokens.wait_send()
    tiles(first_back)
    gt_store = load(TOK, gt_hbm, iosem.at[3])

    def vec_send(step, peers):
        base = (0, 1, 4, 7)[step]
        for i, peer in enumerate(peers):
            remote(VS.at[step], VR.at[base + i], vsend.at[step], vrecv.at[step], peer)

    def vec_add(step):
        base = (0, 1, 4, 7)[step]
        if step == 0:
            all_bytes(VR.at[0:1], vrecv.at[0])
            total = VS[0] + VR[0]
        else:
            all_bytes(VR.at[base : base + 3], vrecv.at[step])
            total = (VS[step] + VR[base + 1]) + (VR[base] + VR[base + 2])
        VS[step + 1] = total

    vec_send(0, [sibling])
    rs_first(10)
    rs_mid(9)
    rs_second(8)
    rs_third(6)
    rs_third(7)
    rs_fourth(4)
    rs_fourth(5)
    vec_add(0)
    vec_send(1, z_peer[1:])
    rs_mid(10)
    rs_second(9)
    rs_third(8)
    rs_fourth(6)
    rs_second(10)
    vec_add(1)
    vec_send(2, x_peer[1:])
    rs_third(9)
    rs_fourth(7)
    rs_fourth(8)
    rs_third(10)
    vec_add(2)
    vec_send(3, y_peer[1:])
    rs_end(0)
    rs_fourth(9)
    rs_fourth(10)
    vec_add(3)

    vectors = VS[4]
    small = pltpu.roll(vectors, (WIDTH - 12 * dp) % WIDTH, 1)
    large = pltpu.roll(vectors, (WIDTH - 48 * (dp % 16)) % WIDTH, 1)[:, 0:128]
    row = lax.broadcasted_iota(jnp.int32, (16, 128), 0)
    large = jnp.sum(jnp.where(row == 8 + dp // 16, large, 0.0), axis=0, keepdims=True)
    for i, ref in enumerate(
        (gqb_ref, gvb_ref, gob_ref, gfg_ref, gfs_ref, gsg_ref, gss_ref, gdb_ref)
    ):
        ref[...] = small[i : i + 1, 0:12].reshape(12)
    gub_ref[...] = large[:, 0:48].reshape(48)

    for copy in far_dout:
        copy.wait_send()
    far_stats.wait_send()
    for key in list(landing):
        gone(key)
    all_bytes(VR.at[0:1], vsend.at[0])
    for step in range(1, 4):
        all_bytes(VR.at[3 * step - 2 : 3 * step + 1], vsend.at[step])
    lo_store.wait()
    gt_store.wait()


def finish(*refs):
    count = (len(refs) - 2) // 3
    sems = refs[3 * count :]
    hops = []
    for i in range(count):
        src, dst, held = refs[i], refs[count + i], refs[2 * count + i]
        hops.append(
            (
                pltpu.make_async_copy(src, held, sems[0].at[i]),
                pltpu.make_async_copy(held, dst, sems[1].at[i]),
            )
        )
    for first, _ in hops:
        first.start()
    for first, second in hops:
        first.wait()
        second.start()
    for _, second in hops:
        second.wait()


def body(
    tokens,
    input_weight,
    query_bias,
    value_bias,
    out_weight,
    out_bias,
    first_gain,
    first_shift,
    second_gain,
    second_shift,
    up_weight,
    up_bias,
    down_weight,
    down_bias,
    cotangent,
    row_counts,
    image_lengths,
):
    hbm = pl.BlockSpec(memory_space=pl.ANY)
    vmem = pl.BlockSpec(memory_space=pltpu.VMEM)
    smem = pl.BlockSpec(memory_space=pltpu.SMEM)
    rows = jax.ShapeDtypeStruct((ROWS, WIDTH), BF)

    def f32(*shape):
        return jax.ShapeDtypeStruct(shape, F32)

    def block(kind, *lead):
        return pltpu.VMEM((*lead, ROWS, WIDTH), kind)

    out = pl.pallas_call(
        kernel,
        out_shape=(
            rows,
            rows,
            f32(12, 3 * WIDTH),
            f32(12),
            f32(12),
            f32(12, WIDTH),
            f32(12),
            f32(12),
            f32(12),
            f32(12),
            f32(12),
            f32(12, 4 * WIDTH),
            f32(48),
            f32(48, WIDTH),
            f32(12),
        ),
        in_specs=[smem, smem] + [hbm] * 6 + [vmem] * 9,
        out_specs=(hbm, hbm) + (vmem,) * 13,
        scratch_shapes=[
            pltpu.VMEM((8, WIDTH, WIDTH), BF),
            pltpu.VMEM((SLOTS, 2, 4, 4, 2, 16, WIDTH), BF),
            pltpu.VMEM((CHUNKS, 2, 4, 4, 16, WIDTH), BF),
            pltpu.VMEM((CHUNKS - len(Y_FIRST), 3, 2, 4, 16, WIDTH), BF),
            pltpu.VMEM((CHUNKS - len(Y_FIRST), 3, 2, 16, WIDTH), BF),
            pltpu.VMEM((CHUNKS - len(Y_FIRST), 3, 16, WIDTH), BF),
            pltpu.VMEM((1, 3, 4, 4, 16, 384), BF),
            pltpu.VMEM((1, 3, 4, 16, 384), BF),
            pltpu.VMEM((1, 3, 16, 384), BF),
            pltpu.VMEM((1, 2, 16, 384), F32),
            block(BF),
            block(BF),
            pltpu.VMEM((2, 16, ROWS), F32),
            pltpu.VMEM((2, 16, ROWS), F32),
        ]
        + [block(BF)] * 12
        + [
            pltpu.VMEM((1024, ROWS), BF),
            pltpu.VMEM((1024, ROWS), BF),
            block(F32),
            block(F32, 2),
            pltpu.VMEM((8, ROWS, 128), BF),
            pltpu.VMEM((ROWS, 384), BF),
            pltpu.VMEM((16, ROWS), F32),
            pltpu.VMEM((16, ROWS), F32),
            pltpu.VMEM((5, 16, WIDTH), F32),
            pltpu.VMEM((10, 16, WIDTH), F32),
            pltpu.SemaphoreType.DMA((8,)),
            pltpu.SemaphoreType.DMA((3,)),
            pltpu.SemaphoreType.DMA((4,)),
            pltpu.SemaphoreType.DMA((5,)),
            pltpu.SemaphoreType.DMA((5,)),
            pltpu.SemaphoreType.DMA((len(STEPS),)),
            pltpu.SemaphoreType.DMA((len(STEPS),)),
            pltpu.SemaphoreType.DMA((4,)),
            pltpu.SemaphoreType.DMA((4,)),
        ],
        compiler_params=pltpu.CompilerParams(
            collective_id=0, has_side_effects=True, vmem_limit_bytes=63 * 2**20
        ),
        name="encoder",
    )(
        row_counts,
        image_lengths,
        tokens,
        cotangent,
        input_weight,
        out_weight,
        up_weight,
        down_weight,
        query_bias,
        value_bias,
        out_bias,
        first_gain,
        first_shift,
        second_gain,
        second_shift,
        up_bias,
        down_bias,
    )
    return pl.pallas_call(
        finish,
        out_shape=tuple(jax.ShapeDtypeStruct(value.shape, value.dtype) for value in out),
        in_specs=[hbm] * len(out),
        out_specs=(hbm,) * len(out),
        scratch_shapes=[pltpu.VMEM(value.shape, value.dtype) for value in out]
        + [pltpu.SemaphoreType.DMA((len(out),))] * 2,
        name="finish",
    )(*out)


def solution(mesh):
    rows = P(("seq", "dp"), None)
    split = P("dp", None)
    line = P("dp")
    return jax.shard_map(
        body,
        mesh=mesh,
        in_specs=(rows,) + (P(),) * 13 + (rows, split, split),
        out_specs=(
            rows,
            rows,
            split,
            line,
            line,
            split,
            line,
            line,
            line,
            line,
            line,
            split,
            line,
            split,
            line,
        ),
        check_vma=False,
    )
```

```python
import jax
import jax.numpy as jnp
from jax import lax
from jax.experimental import pallas as pl
from jax.experimental.pallas import tpu as pltpu
from jax.sharding import PartitionSpec as P

F32 = jnp.float32
BF = jnp.bfloat16
EPS = 1e-06
ROWS = 512
WIDTH = 768
TILE = 256
CHUNKS = 11
SLOTS = 7
FEATURES = 37
PARTS = (
    ((2, 0, 768),),
    ((0, 0, 768),),
    ((1, 0, 768),),
    ((0, 0, 768),),
    ((1, 0, 768),),
    ((0, 0, 768),),
    ((1, 0, 768),),
    ((0, 0, 384), (1, 384, 768)),
    ((0, 0, 384), (1, 384, 768)),
    ((0, 0, 384), (1, 384, 768)),
    ((3, 0, 384), (4, 384, 768)),
)
Y_FIRST = (0,)
STEPS = [(c, 0, 0) for c in range(CHUNKS)]
STEPS += [(c, s, p) for c in range(CHUNKS) for p, _, _ in PARTS[c] for s in (1, 2, 3)]
STEPS += [(c, 4, 2) for c in Y_FIRST]
STEPS += [(c, 5, p) for c in range(CHUNKS) for p, _, _ in PARTS[c] if p < 2]
MESH = pl.DeviceIdType.MESH


def dot_nn(left, right):
    return lax.dot_general(left, right, (((1,), (0,)), ((), ())), preferred_element_type=F32)


def dot_nt(left, right):
    return lax.dot_general(left, right, (((1,), (1,)), ((), ())), preferred_element_type=F32)


def dot_tn(left, right):
    return lax.dot_general(left, right, (((0,), (0,)), ((), ())), preferred_element_type=F32)


def norm_parts(block):
    centred = block - jnp.mean(block, axis=-1, keepdims=True)
    spread = jnp.mean(centred * centred, axis=-1, keepdims=True)
    inverse = lax.rsqrt(spread + EPS)
    return centred * inverse, inverse


def kernel(
    counts_ref,
    lengths_ref,
    tokens_hbm,
    cot_hbm,
    wi_hbm,
    wo_hbm,
    wu_hbm,
    wd_hbm,
    qb_ref,
    vb_ref,
    ob_ref,
    fg_ref,
    fs_ref,
    sg_ref,
    ss_ref,
    ub_ref,
    db_ref,
    lo_hbm,
    gt_hbm,
    gi_ref,
    gqb_ref,
    gvb_ref,
    go_ref,
    gob_ref,
    gfg_ref,
    gfs_ref,
    gsg_ref,
    gss_ref,
    gu_ref,
    gub_ref,
    gd_ref,
    gdb_ref,
    W,
    CH,
    R0,
    R1,
    R2,
    R3,
    S1,
    S2,
    S3,
    S4,
    FT,
    FDO,
    STAT,
    FSTAT,
    QO,
    KO,
    VO,
    QF,
    KF,
    VF,
    TOK,
    COT,
    ATT,
    SEC,
    ACT,
    DH,
    XT,
    XN,
    RES,
    ACC,
    MF,
    PB,
    TOP,
    SUM,
    VS,
    VR,
    wsem,
    dsem,
    iosem,
    xsend,
    xrecv,
    rsend,
    rrecv,
    vsend,
    vrecv,
):
    ACC1, ACC2 = ACC.at[0], ACC.at[1]
    part = lax.axis_index("seq")
    dp = lax.axis_index("dp")
    y_lo = dp // 32
    z = (dp // 8) % 4
    x = (dp // 2) % 4
    core = dp % 2
    y = 2 * part + y_lo

    def device(yy, zz, xx, cc):
        return (yy // 2, ((yy % 2) * 4 + zz) * 8 + xx * 2 + cc)

    sibling = device(y, z, x, 1 - core)
    z_of = [(z + k) % 4 for k in range(4)]
    x_of = [(x + k) % 4 for k in range(4)]
    y_of = [(y + k) % 4 for k in range(4)]
    z_a, z_b = z + 1 - 2 * (z % 2), 3 - z
    x_a, x_b = x + 1 - 2 * (x % 2), 3 - x
    near_z = [device(y, v, x, core) for v in (z_a, z_b)]
    near_x = [device(y, z, v, core) for v in (x_a, x_b)]
    z_peer = [device(y, v, x, core) for v in z_of]
    x_peer = [device(y, z, v, core) for v in x_of]
    y_peer = [device(v, z, x, core) for v in y_of]
    partner = y_peer[2]

    def load(src, dst, sem):
        copy = pltpu.make_async_copy(src, dst, sem)
        copy.start()
        return copy

    tok_load = load(tokens_hbm, TOK, iosem.at[0])
    w_load = {}
    for i in range(3):
        w_load[i] = load(wi_hbm.at[:, pl.ds(WIDTH * i, WIDTH)], W.at[i], wsem.at[i])
    cot_load = load(cot_hbm, COT, iosem.at[1])
    w_load[3] = load(wo_hbm, W.at[3], wsem.at[3])

    def load_ffn(f):
        slot = f % 2
        up = load(wu_hbm.at[:, pl.ds(WIDTH * f, WIDTH)], W.at[4 + slot], wsem.at[4 + slot])
        down = load(wd_hbm.at[pl.ds(WIDTH * f, WIDTH)], W.at[6 + slot], wsem.at[6 + slot])
        return up, down

    ffn_load = {0: load_ffn(0), 1: load_ffn(1)}
    down_load = [
        load(wd_hbm.at[pl.ds(2 * WIDTH + ROWS * i, ROWS)], ref, dsem.at[i])
        for i, ref in enumerate((SEC, ACT, DH))
    ]

    barrier = pltpu.get_barrier_semaphore()
    for peer in [sibling] + z_peer[1:] + x_peer[1:] + y_peer[1:]:
        pl.semaphore_signal(barrier, inc=1, device_id=peer, device_id_type=MESH)
    pl.semaphore_wait(barrier, 10)

    def remote(src, dst, send, recv, peer):
        copy = pltpu.make_async_remote_copy(
            src_ref=src,
            dst_ref=dst,
            send_sem=send,
            recv_sem=recv,
            device_id=peer,
            device_id_type=MESH,
        )
        copy.start()
        return copy

    far_tokens = remote(tokens_hbm, FT, xsend.at[0], xrecv.at[0], partner)

    def all_bytes(ref, sem):
        pltpu.make_async_copy(ref, ref, sem).wait()

    landing = {}

    def send_all(key, dst, copies):
        i = STEPS.index(key)
        landing[key] = dst
        for src, into, peer in copies:
            remote(src, into, rsend.at[i], rrecv.at[i], peer)

    def received(key):
        all_bytes(landing[key], rrecv.at[STEPS.index(key)])

    def gone(key):
        all_bytes(landing.pop(key), rsend.at[STEPS.index(key)])

    def rs_core(c):
        src = CH.at[c % SLOTS, :, :, :, 1 - core]
        send_all((c, 0, 0), R0.at[c], [(src, R0.at[c], sibling)])

    def row_of(c):
        return c - sum(first < c for first in Y_FIRST)

    def y_slot(c):
        n = Y_FIRST.index(c)
        return n, 384

    def rs_first(c):
        received((c, 0, 0))

        def add(i, carry):
            yl, zz = i // 4, i % 4
            R0[c, yl, zz] = (
                R0[c, yl, zz].astype(F32) + CH[c % SLOTS, yl, zz, :, core].astype(F32)
            ).astype(BF)
            return carry

        lax.fori_loop(0, 8, add, 0)
        for p, lo, hi in PARTS[c]:
            copies = []
            if p == 2:
                n, width = y_slot(c)
                whole = S1.at[n, :, :, :, :, 0:width]
                for k in (2, 1, 3):
                    start = pl.multiple_of(lo + width * (y_of[k] // 2), 128)
                    src = R0.at[c, y_of[k] % 2, :, :, :, pl.ds(start, width)]
                    copies.append((src, S1.at[n, k - 1, :, :, :, 0:width], y_peer[k]))
            elif p > 2:
                whole = R1.at[row_of(c), :, :, :, :, lo:hi]
                for k in (2, 1, 3):
                    if p == 3:
                        src, peer = R0.at[c, :, z_of[k], :, :, lo:hi], z_peer[k]
                    else:
                        src, peer = R0.at[c, :, :, x_of[k], :, lo:hi], x_peer[k]
                    copies.append((src, R1.at[row_of(c), k - 1, :, :, :, lo:hi], peer))
            else:
                whole = R1.at[row_of(c), 0:2, :, :, :, lo:hi]
                a, b = (z_a, z_b) if p == 0 else (x_a, x_b)
                across = 3 - a
                peers = near_z if p == 0 else near_x
                for half, nearest in ((0, a), (1, b)):
                    for spot, wanted in ((1, across), (0, nearest)):
                        dst = R1.at[row_of(c), half, spot, :, :, lo:hi]
                        copies.append((shares(c, p, half, wanted, lo, hi), dst, peers[half]))
            send_all((c, 1, p), whole, copies)

    def shares(c, p, yl, v, lo, hi):
        if p == 0:
            return R0.at[c, yl, v, :, :, lo:hi]
        return R0.at[c, yl, :, v, :, lo:hi]

    def rs_mid(c):
        for p, lo, hi in PARTS[c]:
            if p > 1:
                continue
            received((c, 1, p))
            v, a, b = (z, z_a, z_b) if p == 0 else (x, x_a, x_b)
            for half, other in ((0, b), (1, a)):
                for spot, kept in ((0, v), (1, other)):
                    at = (row_of(c), half, spot, slice(None), slice(None), slice(lo, hi))
                    own = shares(c, p, half, kept, lo, hi)[...]
                    R1[at] = (own.astype(F32) + R1[at].astype(F32)).astype(BF)
            peers = near_z if p == 0 else near_x
            copies = []
            for half in range(2):
                src = R1.at[row_of(c), half, 1, :, :, lo:hi]
                copies.append((src, R1.at[row_of(c), 2, half, :, :, lo:hi], peers[1 - half]))
            send_all((c, 5, p), R1.at[row_of(c), 2, :, :, :, lo:hi], copies)

    def rs_second(c):
        for p, lo, hi in PARTS[c]:
            received((c, 5 if p < 2 else 1, p))
            copies = []
            if p == 2:
                n, width = y_slot(c)
                start = pl.multiple_of(lo + width * part, 128)
                for zz in range(4):
                    total = R0[c, y_lo, zz, :, :, pl.ds(start, width)].astype(F32)
                    for k in range(3):
                        total = total + S1[n, k, zz, :, :, 0:width].astype(F32)
                    S1[n, 0, zz, :, :, 0:width] = total.astype(BF)
                whole = S2.at[n, :, :, :, 0:width]
            elif p > 2:
                for yl in range(2):
                    if p == 3:
                        total = R0[c, yl, z, :, :, lo:hi].astype(F32)
                    else:
                        total = R0[c, yl, :, x, :, lo:hi].astype(F32)
                    for k in range(3):
                        total = total + R1[row_of(c), k, yl, :, :, lo:hi].astype(F32)
                    R1[row_of(c), 0, yl, :, :, lo:hi] = total.astype(BF)
                whole = R2.at[row_of(c), :, :, :, lo:hi]
            else:
                for half in range(2):
                    at = (row_of(c), half, 0, slice(None), slice(None), slice(lo, hi))
                    total = R1[at].astype(F32) + R1[row_of(c), 2, half, :, :, lo:hi].astype(F32)
                    R1[at] = total.astype(BF)
                whole = R2.at[row_of(c), :, :, :, lo:hi]
            for k in (2, 1, 3):
                if p == 3:
                    src = R1.at[row_of(c), 0, :, x_of[k], :, lo:hi]
                    dst, peer = R2.at[row_of(c), k - 1, :, :, lo:hi], x_peer[k]
                elif p == 4:
                    src = R1.at[row_of(c), 0, :, z_of[k], :, lo:hi]
                    dst, peer = R2.at[row_of(c), k - 1, :, :, lo:hi], z_peer[k]
                elif p == 0:
                    src = R1.at[row_of(c), 0:2, 0, x_of[k], :, lo:hi]
                    dst, peer = R2.at[row_of(c), k - 1, :, :, lo:hi], x_peer[k]
                elif p == 1:
                    src = R1.at[row_of(c), 0:2, 0, z_of[k], :, lo:hi]
                    dst, peer = R2.at[row_of(c), k - 1, :, :, lo:hi], z_peer[k]
                else:
                    src = S1.at[n, 0, z_of[k], :, :, 0:width]
                    dst, peer = S2.at[n, k - 1, :, :, 0:width], z_peer[k]
                copies.append((src, dst, peer))
            send_all((c, 2, p), whole, copies)

    def rs_third(c):
        for p, lo, hi in PARTS[c]:
            received((c, 2, p))
            copies = []
            if p == 2:
                n, width = y_slot(c)
                total = S1[n, 0, z, :, :, 0:width].astype(F32)
                for k in range(3):
                    total = total + S2[n, k, :, :, 0:width].astype(F32)
                S2[n, 0, :, :, 0:width] = total.astype(BF)
                whole = S3.at[n, :, :, 0:width]
            else:
                if p == 3:
                    total = R1[row_of(c), 0, :, x, :, lo:hi].astype(F32)
                elif p == 4:
                    total = R1[row_of(c), 0, :, z, :, lo:hi].astype(F32)
                elif p == 0:
                    total = R1[row_of(c), 0:2, 0, x, :, lo:hi].astype(F32)
                else:
                    total = R1[row_of(c), 0:2, 0, z, :, lo:hi].astype(F32)
                for k in range(3):
                    total = total + R2[row_of(c), k, :, :, lo:hi].astype(F32)
                R2[row_of(c), 0, :, :, lo:hi] = total.astype(BF)
                whole = R3.at[row_of(c), :, :, lo:hi]
            for k in (2, 1, 3):
                if p == 2:
                    src = S2.at[n, 0, x_of[k], :, 0:width]
                    dst, peer = S3.at[n, k - 1, :, 0:width], x_peer[k]
                else:
                    src = R2.at[row_of(c), 0, y_of[k] % 2, :, lo:hi]
                    dst, peer = R3.at[row_of(c), k - 1, :, lo:hi], y_peer[k]
                copies.append((src, dst, peer))
            send_all((c, 3, p), whole, copies)

    def store_share(c, lo, hi, total):
        if c < 4:
            gu_ref[:, WIDTH * c + lo : WIDTH * c + hi] = total[0:12]
        elif c < 7:
            gd_ref[16 * (c - 4) : 16 * (c - 3), lo:hi] = total
        elif c == 7:
            go_ref[:, lo:hi] = total[0:12]
        else:
            for b in range(lo // 384, hi // 384):
                start = 384 * b if c == 8 else WIDTH * (b + 1) + 384 * (c - 9)
                gi_ref[:, start : start + 384] = total[0:12, 384 * b - lo : 384 * (b + 1) - lo]

    def rs_fourth(c):
        for p, lo, hi in PARTS[c]:
            received((c, 3, p))
            if p == 2:
                n, width = y_slot(c)
                total = S2[n, 0, x, :, 0:width].astype(F32)
                for k in range(3):
                    total = total + S3[n, k, :, 0:width].astype(F32)
                S4[n, 0, :, 0:width] = total
                dst = S4.at[n, 1, :, 0:width]
                send_all((c, 4, p), dst, [(S4.at[n, 0, :, 0:width], dst, partner)])
            else:
                total = (R2[row_of(c), 0, y_lo, :, lo:hi].astype(F32) + R3[row_of(c), 1, :, lo:hi].astype(F32)) + (
                    R3[row_of(c), 0, :, lo:hi].astype(F32) + R3[row_of(c), 2, :, lo:hi].astype(F32)
                )
                store_share(c, lo, hi, total)

    def rs_end(c):
        n, width = y_slot(c)
        received((c, 4, 2))
        mine = S4[n, 0, :, 0:width]
        other = S4[n, 1, :, 0:width]
        low = jnp.where(part == 0, mine, other)
        high = jnp.where(part == 0, other, mine)
        lo = PARTS[c][-1][1]
        store_share(c, lo, lo + 2 * width, jnp.concatenate([low, high], axis=1))

    counts0 = counts_ref[0, 0]
    counts1 = counts_ref[0, 1]
    end0 = lengths_ref[0, 0]
    end1 = end0 + lengths_ref[0, 1]
    end2 = end1 + lengths_ref[0, 2]
    end3 = end2 + lengths_ref[0, 3]

    def used_rows(start, size, width):
        place = lax.broadcasted_iota(jnp.int32, (size, width), 0) + start
        return place < counts0 + part * (counts1 - counts0)

    def features(base, which):
        place = lax.broadcasted_iota(jnp.int32, (ROWS, 128), 0)
        shifted = place + which * counts0
        index = jnp.zeros((ROWS, 128), jnp.int32)
        for end in (end0, end1, end2, end3):
            index = index + jnp.where(end <= shifted, 1, 0)
        owned = counts0 + which * (counts1 - counts0)
        ids = jnp.where(place < owned, index, 4 + which * ROWS + place)
        lane = lax.broadcasted_iota(jnp.int32, (ROWS, 128), 1)
        high = lane >= 64
        spot = jnp.where(high, lane - 64, lane)
        digit = jnp.where(
            spot < 16, ids & 15, jnp.where(spot < 32, ((ids >> 4) & 15) + 16, (ids >> 8) + 32)
        )
        hot = jnp.where(digit == spot, 1.0, 0.0)
        query = jnp.where(spot < FEATURES, 1.0 - hot, 0.0)
        key = hot * -1e30
        MF[base] = jnp.where(high, query, 0.0).astype(BF)
        MF[base + 1] = jnp.where(high, 0.0, query).astype(BF)
        MF[base + 2] = jnp.where(high, key, 0.0).astype(BF)
        MF[base + 3] = jnp.where(high, 0.0, key).astype(BF)

    features(0, part)
    features(4, 1 - part)
    lane_row = lax.broadcasted_iota(jnp.int32, (1, 128), 1)
    select = [
        jnp.where(lane_row < 64, 1.0, 0.0).astype(BF),
        jnp.where(lane_row < 64, 0.0, 1.0).astype(BF),
    ]

    rho = lax.broadcasted_iota(jnp.int32, (ROWS, 384), 0)
    feature = lax.broadcasted_iota(jnp.int32, (ROWS, 384), 1)
    within = rho & 15
    PB[...] = jnp.where(
        (within < 12) & (feature == (rho >> 4) * 12 + within), 1.0, 0.0
    ).astype(BF)

    def padded_transpose(source, into):
        for b in range(2):
            into[ROWS * b : ROWS * (b + 1), :] = dot_nt(
                PB[...], source[:, 384 * b : 384 * (b + 1)]
            ).astype(BF)

    def chunk_matmul(c, right):
        left = XT if c < 8 else XN

        def block(m, carry):
            cols = pl.ds(pl.multiple_of(m * TILE, TILE), TILE)
            out = dot_nn(left[...], right[:, cols]).astype(BF)
            CH[c % SLOTS, :, :, :, :, :, cols] = out.reshape(2, 4, 4, 2, 16, TILE)
            return carry

        lax.fori_loop(0, 3, block, 0)

    ones = jnp.ones((16, ROWS), BF)

    def row_sum(block):
        return dot_nn(ones, block)[0:1]

    def tiles(step):
        def run(t, carry):
            step(pl.ds(pl.multiple_of(t * TILE, TILE), TILE), t * TILE)
            return carry

        lax.fori_loop(0, ROWS // TILE, run, 0)

    qb = qb_ref[...].reshape(1, WIDTH)
    vb = vb_ref[...].reshape(1, WIDTH)
    ob = ob_ref[...].reshape(1, WIDTH)
    fg = fg_ref[...].reshape(1, WIDTH)
    fs = fs_ref[...].reshape(1, WIDTH)
    sg = sg_ref[...].reshape(1, WIDTH)
    ss = ss_ref[...].reshape(1, WIDTH)
    db = db_ref[...].reshape(1, WIDTH)

    def projection(source, q_ref, k_ref, v_ref):
        def step(rows, start):
            unit, _ = norm_parts(source[rows, :].astype(F32))
            normed = (unit * fg + fs).astype(BF)
            q = (dot_nn(normed, W[0]) + qb).astype(BF)
            q_ref[rows, :] = q * jnp.asarray(0.125, BF)
            k_ref[rows, :] = dot_nn(normed, W[1]).astype(BF)
            v_ref[rows, :] = (dot_nn(normed, W[2]) + vb).astype(BF)

        return step

    tok_load.wait()
    for i in range(3):
        w_load[i].wait()
    tiles(projection(TOK, QO, KO, VO))

    cot_load.wait()

    def mask_cot(rows, start):
        used = used_rows(start, TILE, WIDTH)
        COT[rows, :] = jnp.where(used, COT[rows, :].astype(F32), 0.0).astype(BF)

    tiles(mask_cot)

    def pair_cols(hp):
        return pl.ds(pl.multiple_of(hp * 128, 128), 128)

    def mix_at(hp, h):
        start = pl.multiple_of(128 * (hp % 4) + 64 * h, 64)
        return hp // 4, pl.ds(start, 64), slice(0, ROWS)

    def attend_own(hp, carry):
        cols = pair_cols(hp)
        q = QO[:, cols]
        keys = KO[:, cols]
        values = VO[:, cols].T
        for h in range(2):
            row = pl.ds(2 * hp + h, 1)
            scores = dot_nt(keys * select[h] + MF[2 + h], q * select[h] + MF[h])
            top = jnp.max(scores, axis=0, keepdims=True)
            probs = jnp.exp(scores - top)
            TOP[row, :] = top
            SUM[row, :] = jnp.sum(probs, axis=0, keepdims=True)
            own = slice(64 * h, 64 * h + 64)
            ACC[mix_at(hp, h)] = dot_nn(values[own], probs.astype(BF))
        return carry

    lax.fori_loop(0, 6, attend_own, 0)

    def attend_far(hp, carry):
        cols = pair_cols(hp)
        q = QO[:, cols]
        keys = KF[:, cols]
        values = VF[:, cols].T
        outs = []
        for h in range(2):
            row = pl.ds(2 * hp + h, 1)
            own = slice(64 * h, 64 * h + 64)
            scores = dot_nt(keys * select[h] + MF[6 + h], q * select[h] + MF[h])
            before = TOP[row, :]
            top = jnp.maximum(before, jnp.max(scores, axis=0, keepdims=True))
            shrink = jnp.exp(before - top)
            probs = jnp.exp(scores - top)
            total = SUM[row, :] * shrink + jnp.sum(probs, axis=0, keepdims=True)
            mixed = ACC[mix_at(hp, h)] * shrink + dot_nn(values[own], probs.astype(BF))
            STAT[0, row, :] = top + jnp.log(total)
            outs.append(mixed * (1.0 / total))
        ATT[:, cols] = jnp.concatenate(outs, axis=0).T.astype(BF)
        return carry

    def again(rows, start):
        unit, _ = norm_parts(TOK[rows, :].astype(F32))
        ATT[rows, :] = (unit * fg + fs).astype(BF)

    tiles(again)
    padded_transpose(ATT, XN)

    for copy in down_load:
        copy.wait()
    for f in range(2):
        ffn_load[f][1].wait()

    def early_step(rows, start):
        dout = COT[rows, :]
        block = start // TILE * 2

        def keep(f, lo, value):
            CH[f, 0, pl.ds(block, 2), :, :, :, lo : lo + value.shape[1]] = value.astype(BF).reshape(
                2, 4, 2, 16, value.shape[1]
            )

        for f in range(2):
            keep(f, 0, dot_nt(dout, W[6 + f]))
        keep(2, 0, dot_nt(dout, SEC[...]))
        middle = dot_nt(dout, ACT[...])
        keep(2, 512, middle[:, 0:256])
        keep(3, 0, middle[:, 256:512])
        keep(3, 256, dot_nt(dout, DH[...]))

    tiles(early_step)

    far_tokens.wait_recv()
    tiles(projection(FT, QF, KF, VF))
    lax.fori_loop(0, 6, attend_far, 0)

    w_load[3].wait()

    def out_step(rows, start):
        res = TOK[rows, :].astype(F32) + dot_nn(ATT[rows, :], W[3]) + ob
        RES[rows, :] = res
        unit, _ = norm_parts(res)
        SEC[rows, :] = (unit * sg + ss).astype(BF)
        ACC1[rows, :] = jnp.zeros((TILE, WIDTH), F32)
        ACC2[rows, :] = jnp.zeros((TILE, WIDTH), F32)

    tiles(out_step)
    padded_transpose(SEC, XT)
    VS[0] = jnp.zeros((16, WIDTH), F32)

    for f in range(4):
        slot = f % 2
        ffn_load[f][0].wait()
        if f > 1:
            ffn_load[f][1].wait()
        ub = ub_ref[WIDTH * f : WIDTH * (f + 1)].reshape(1, WIDTH)

        def ffn_step(rows, start, f=f, slot=slot, ub=ub):
            early = CH[f, 0, pl.ds(start // TILE * 2, 2)].reshape(TILE, WIDTH).astype(F32)
            hidden = dot_nn(SEC[rows, :], W[4 + slot]) + ub
            cdf = 0.5 * (1.0 + lax.erf(hidden * 0.7071067811865476))
            density = jnp.exp(-0.5 * hidden * hidden) * 0.3989422804014327
            active = (hidden * cdf).astype(BF)
            ACT[rows, :] = active
            dhidden = (early * (cdf + hidden * density)).astype(BF)
            DH[rows, :] = dhidden
            ACC1[rows, :] += dot_nn(active, W[6 + slot])
            ACC2[rows, :] += dot_nt(dhidden, W[4 + slot])

        tiles(ffn_step)
        if f + 2 < 4:
            ffn_load[f + 2] = load_ffn(f + 2)
        if f >= 1:
            rs_first(f - 1)
        chunk_matmul(f, DH)
        rs_core(f)
        VS[0, 8 + f : 9 + f, :] = row_sum(DH[...])

        def down_step(b, carry, f=f):
            cols = pl.ds(pl.multiple_of(b * 384, 384), 384)
            out = dot_tn(ACT[:, cols], COT[...]).astype(BF).reshape(4, 2, 3, 16, WIDTH)
            for k in range(3):
                CH[4 + k, f // 2, 2 * (f % 2) + b] = out[:, :, k]
            return carry

        lax.fori_loop(0, 2, down_step, 0)
    for k in range(3):
        rs_core(4 + k)

    def second_back(rows, start):
        res = RES[rows, :]
        used = used_rows(start, TILE, WIDTH)
        FT[rows, :] = jnp.where(used, res + ACC1[rows, :] + db, 0.0).astype(BF)
        unit, inverse = norm_parts(res)
        dsecond = ACC2[rows, :]
        VS[0, 5:6, :] += jnp.sum(dsecond * unit, axis=0, keepdims=True)
        VS[0, 6:7, :] += jnp.sum(dsecond, axis=0, keepdims=True)
        g = dsecond * sg
        through = (
            g
            - jnp.mean(g, axis=-1, keepdims=True)
            - unit * jnp.mean(g * unit, axis=-1, keepdims=True)
        ) * inverse
        dres = COT[rows, :].astype(F32) + through
        RES[rows, :] = dres
        SEC[rows, :] = dres.astype(BF)
        DH[rows, :] = dot_nt(dres.astype(BF), W[3]).astype(BF)

    tiles(second_back)
    lo_store = load(FT, lo_hbm, iosem.at[2])
    far_dout = []
    for r in range(2):
        half = pl.ds(384 * r, 384)
        far_dout.append(
            remote(DH.at[:, half], FDO.at[:, half], xsend.at[2 + r], xrecv.at[2 + r], partner)
        )
    rs_first(3)
    VS[0, 7:8, :] = row_sum(COT[...])
    VS[0, 2:3, :] = row_sum(SEC[...])

    head = lax.broadcasted_iota(jnp.int32, (16, WIDTH), 0)
    column = lax.broadcasted_iota(jnp.int32, (16, WIDTH), 1)
    in_head = jnp.where((column >> 6) == head, 1.0, 0.0).astype(BF)
    product = DH[...].astype(F32) * ATT[...].astype(F32)
    rough = product.astype(BF)
    STAT[1] = dot_nt(in_head, rough) + dot_nt(in_head, (product - rough.astype(F32)).astype(BF))
    far_stats = remote(STAT, FSTAT, xsend.at[4], xrecv.at[4], partner)

    padded_transpose(ATT, XT)
    gone((0, 0, 0))
    chunk_matmul(7, SEC)
    rs_core(7)
    rs_first(4)
    rs_first(5)
    rs_mid(1)

    def own_queries(hp, carry):
        cols = pair_cols(hp)
        q = QO[:, cols]
        ko = KO[:, cols]
        kf = KF[:, cols]
        vo = VO[:, cols]
        vf = VF[:, cols]
        do = DH[:, cols]
        ko_t = ko.T
        kf_t = kf.T
        dq = []
        dk = None
        for h in range(2):
            logsum = STAT[0, pl.ds(2 * hp + h, 1), :]
            delta = STAT[1, pl.ds(2 * hp + h, 1), :]
            qm = q * select[h] + MF[h]
            qs = q * select[h]
            dom = do * select[h]
            near = jnp.exp(dot_nt(ko * select[h] + MF[2 + h], qm) - logsum)
            dnear = (near * (dot_nt(vo, dom) - delta)).astype(BF)
            far = jnp.exp(dot_nt(kf * select[h] + MF[6 + h], qm) - logsum)
            dfar = (far * (dot_nt(vf, dom) - delta)).astype(BF)
            dq.append(
                dot_nn(ko_t[64 * h : 64 * h + 64], dnear)
                + dot_nn(kf_t[64 * h : 64 * h + 64], dfar)
            )
            dk_h = dot_nn(dnear, qs)
            dv_h = dot_nn(near.astype(BF), dom)
            dk, dv = (dk_h, dv_h) if dk is None else (dk + dk_h, dv + dv_h)
        ACC1[:, cols] = dk
        ACC2[:, cols] = dv
        QO[:, cols] = (jnp.concatenate(dq, axis=0).T * 0.125).astype(BF)
        return carry

    lax.fori_loop(0, 2, own_queries, 0)
    rs_first(6)
    rs_mid(2)
    rs_second(0)
    lax.fori_loop(2, 4, own_queries, 0)
    rs_first(7)
    rs_mid(3)
    rs_second(1)
    rs_mid(4)
    lax.fori_loop(4, 6, own_queries, 0)
    rs_mid(5)
    rs_second(2)
    rs_third(0)

    def again(rows, start):
        unit, _ = norm_parts(TOK[rows, :].astype(F32))
        ATT[rows, :] = (unit * fg + fs).astype(BF)


    gone((1, 0, 0))
    chunk_matmul(8, QO)
    rs_core(8)
    rs_mid(6)
    rs_second(3)
    rs_third(1)

    far_stats.wait_recv()

    def far_queries(hp, carry):
        cols = pair_cols(hp)
        q = QF[:, cols]
        ko = KO[:, cols]
        vo = VO[:, cols]
        do = FDO[:, cols]
        dk = ACC1[:, cols]
        dv = ACC2[:, cols]
        for h in range(2):
            logsum = FSTAT[0, pl.ds(2 * hp + h, 1), :]
            delta = FSTAT[1, pl.ds(2 * hp + h, 1), :]
            qs = q * select[h]
            dom = do * select[h]
            probs = jnp.exp(dot_nt(ko * select[h] + MF[2 + h], qs + MF[4 + h]) - logsum)
            dscores = (probs * (dot_nt(vo, dom) - delta)).astype(BF)
            dk = dk + dot_nn(dscores, qs)
            dv = dv + dot_nn(probs.astype(BF), dom)
        KO[:, cols] = dk.astype(BF)
        VO[:, cols] = dv.astype(BF)
        return carry

    def chunk_in(c):
        cols = slice(384 * (c - 9), 384 * (c - 8))
        ACT[:, 0:384] = KO[:, cols]
        ACT[:, 384:768] = VO[:, cols]
        gone((c - 7, 0, 0))
        chunk_matmul(c, ACT)
        rs_core(c)

    far_dout[0].wait_recv()
    lax.fori_loop(0, 3, far_queries, 0)
    chunk_in(9)
    rs_first(8)
    rs_mid(7)
    rs_second(4)
    rs_second(5)
    rs_third(2)
    rs_third(3)
    rs_fourth(0)
    far_dout[1].wait_recv()
    lax.fori_loop(3, 4, far_queries, 0)
    rs_first(9)
    lax.fori_loop(4, 6, far_queries, 0)
    chunk_in(10)
    rs_mid(8)
    rs_second(6)
    rs_second(7)
    rs_third(4)
    rs_third(5)
    rs_fourth(1)
    rs_fourth(2)
    rs_fourth(3)

    VS[0, 0:1, :] = row_sum(QO[...])
    VS[0, 1:2, :] = row_sum(VO[...])

    def first_back(rows, start):
        unit, inverse = norm_parts(TOK[rows, :].astype(F32))
        dnormed = (
            dot_nt(QO[rows, :], W[0]) + dot_nt(KO[rows, :], W[1]) + dot_nt(VO[rows, :], W[2])
        )
        VS[0, 3:4, :] += jnp.sum(dnormed * unit, axis=0, keepdims=True)
        VS[0, 4:5, :] += jnp.sum(dnormed, axis=0, keepdims=True)
        g = dnormed * fg
        through = (
            g
            - jnp.mean(g, axis=-1, keepdims=True)
            - unit * jnp.mean(g * unit, axis=-1, keepdims=True)
        ) * inverse
        TOK[rows, :] = (RES[rows, :] + through).astype(BF)

    far_tokens.wait_send()
    tiles(first_back)
    gt_store = load(TOK, gt_hbm, iosem.at[3])

    def vec_send(step, peers):
        base = (0, 1, 4, 7)[step]
        for i, peer in enumerate(peers):
            remote(VS.at[step], VR.at[base + i], vsend.at[step], vrecv.at[step], peer)

    def vec_add(step):
        base = (0, 1, 4, 7)[step]
        if step == 0:
            all_bytes(VR.at[0:1], vrecv.at[0])
            total = VS[0] + VR[0]
        else:
            all_bytes(VR.at[base : base + 3], vrecv.at[step])
            total = (VS[step] + VR[base + 1]) + (VR[base] + VR[base + 2])
        VS[step + 1] = total

    vec_send(0, [sibling])
    rs_first(10)
    rs_mid(9)
    rs_second(8)
    rs_third(6)
    rs_third(7)
    rs_fourth(4)
    rs_fourth(5)
    vec_add(0)
    vec_send(1, z_peer[1:])
    rs_mid(10)
    rs_second(9)
    rs_third(8)
    rs_fourth(6)
    rs_second(10)
    vec_add(1)
    vec_send(2, x_peer[1:])
    rs_third(9)
    rs_fourth(7)
    rs_fourth(8)
    rs_third(10)
    vec_add(2)
    vec_send(3, y_peer[1:])
    rs_end(0)
    rs_fourth(9)
    rs_fourth(10)
    vec_add(3)

    vectors = VS[4]
    small = pltpu.roll(vectors, (WIDTH - 12 * dp) % WIDTH, 1)
    large = pltpu.roll(vectors, (WIDTH - 48 * (dp % 16)) % WIDTH, 1)[:, 0:128]
    row = lax.broadcasted_iota(jnp.int32, (16, 128), 0)
    large = jnp.sum(jnp.where(row == 8 + dp // 16, large, 0.0), axis=0, keepdims=True)
    for i, ref in enumerate(
        (gqb_ref, gvb_ref, gob_ref, gfg_ref, gfs_ref, gsg_ref, gss_ref, gdb_ref)
    ):
        ref[...] = small[i : i + 1, 0:12].reshape(12)
    gub_ref[...] = large[:, 0:48].reshape(48)

    for copy in far_dout:
        copy.wait_send()
    far_stats.wait_send()
    for key in list(landing):
        gone(key)
    all_bytes(VR.at[0:1], vsend.at[0])
    for step in range(1, 4):
        all_bytes(VR.at[3 * step - 2 : 3 * step + 1], vsend.at[step])
    lo_store.wait()
    gt_store.wait()


def finish(*refs):
    count = (len(refs) - 2) // 3
    sems = refs[3 * count :]
    hops = []
    for i in range(count):
        src, dst, held = refs[i], refs[count + i], refs[2 * count + i]
        hops.append(
            (
                pltpu.make_async_copy(src, held, sems[0].at[i]),
                pltpu.make_async_copy(held, dst, sems[1].at[i]),
            )
        )
    for first, _ in hops:
        first.start()
    for first, second in hops:
        first.wait()
        second.start()
    for _, second in hops:
        second.wait()


def body(
    tokens,
    input_weight,
    query_bias,
    value_bias,
    out_weight,
    out_bias,
    first_gain,
    first_shift,
    second_gain,
    second_shift,
    up_weight,
    up_bias,
    down_weight,
    down_bias,
    cotangent,
    row_counts,
    image_lengths,
):
    hbm = pl.BlockSpec(memory_space=pl.ANY)
    vmem = pl.BlockSpec(memory_space=pltpu.VMEM)
    smem = pl.BlockSpec(memory_space=pltpu.SMEM)
    rows = jax.ShapeDtypeStruct((ROWS, WIDTH), BF)

    def f32(*shape):
        return jax.ShapeDtypeStruct(shape, F32)

    def block(kind, *lead):
        return pltpu.VMEM((*lead, ROWS, WIDTH), kind)

    out = pl.pallas_call(
        kernel,
        out_shape=(
            rows,
            rows,
            f32(12, 3 * WIDTH),
            f32(12),
            f32(12),
            f32(12, WIDTH),
            f32(12),
            f32(12),
            f32(12),
            f32(12),
            f32(12),
            f32(12, 4 * WIDTH),
            f32(48),
            f32(48, WIDTH),
            f32(12),
        ),
        in_specs=[smem, smem] + [hbm] * 6 + [vmem] * 9,
        out_specs=(hbm, hbm) + (vmem,) * 13,
        scratch_shapes=[
            pltpu.VMEM((8, WIDTH, WIDTH), BF),
            pltpu.VMEM((SLOTS, 2, 4, 4, 2, 16, WIDTH), BF),
            pltpu.VMEM((CHUNKS, 2, 4, 4, 16, WIDTH), BF),
            pltpu.VMEM((CHUNKS - len(Y_FIRST), 3, 2, 4, 16, WIDTH), BF),
            pltpu.VMEM((CHUNKS - len(Y_FIRST), 3, 2, 16, WIDTH), BF),
            pltpu.VMEM((CHUNKS - len(Y_FIRST), 3, 16, WIDTH), BF),
            pltpu.VMEM((1, 3, 4, 4, 16, 384), BF),
            pltpu.VMEM((1, 3, 4, 16, 384), BF),
            pltpu.VMEM((1, 3, 16, 384), BF),
            pltpu.VMEM((1, 2, 16, 384), F32),
            block(BF),
            block(BF),
            pltpu.VMEM((2, 16, ROWS), F32),
            pltpu.VMEM((2, 16, ROWS), F32),
        ]
        + [block(BF)] * 12
        + [
            pltpu.VMEM((1024, ROWS), BF),
            pltpu.VMEM((1024, ROWS), BF),
            block(F32),
            block(F32, 2),
            pltpu.VMEM((8, ROWS, 128), BF),
            pltpu.VMEM((ROWS, 384), BF),
            pltpu.VMEM((16, ROWS), F32),
            pltpu.VMEM((16, ROWS), F32),
            pltpu.VMEM((5, 16, WIDTH), F32),
            pltpu.VMEM((10, 16, WIDTH), F32),
            pltpu.SemaphoreType.DMA((8,)),
            pltpu.SemaphoreType.DMA((3,)),
            pltpu.SemaphoreType.DMA((4,)),
            pltpu.SemaphoreType.DMA((5,)),
            pltpu.SemaphoreType.DMA((5,)),
            pltpu.SemaphoreType.DMA((len(STEPS),)),
            pltpu.SemaphoreType.DMA((len(STEPS),)),
            pltpu.SemaphoreType.DMA((4,)),
            pltpu.SemaphoreType.DMA((4,)),
        ],
        compiler_params=pltpu.CompilerParams(
            collective_id=0, has_side_effects=True, vmem_limit_bytes=63 * 2**20
        ),
        name="encoder",
    )(
        row_counts,
        image_lengths,
        tokens,
        cotangent,
        input_weight,
        out_weight,
        up_weight,
        down_weight,
        query_bias,
        value_bias,
        out_bias,
        first_gain,
        first_shift,
        second_gain,
        second_shift,
        up_bias,
        down_bias,
    )
    return pl.pallas_call(
        finish,
        out_shape=tuple(jax.ShapeDtypeStruct(value.shape, value.dtype) for value in out),
        in_specs=[hbm] * len(out),
        out_specs=(hbm,) * len(out),
        scratch_shapes=[pltpu.VMEM(value.shape, value.dtype) for value in out]
        + [pltpu.SemaphoreType.DMA((len(out),))] * 2,
        name="finish",
    )(*out)


def solution(mesh):
    rows = P(("seq", "dp"), None)
    split = P("dp", None)
    line = P("dp")
    return jax.shard_map(
        body,
        mesh=mesh,
        in_specs=(rows,) + (P(),) * 13 + (rows, split, split),
        out_specs=(
            rows,
            rows,
            split,
            line,
            line,
            split,
            line,
            line,
            line,
            line,
            line,
            split,
            line,
            split,
            line,
        ),
        check_vma=False,
    )
```

```python
import jax
import jax.numpy as jnp
from jax import lax
from jax.experimental import pallas as pl
from jax.experimental.pallas import tpu as pltpu
from jax.sharding import PartitionSpec as P

F32 = jnp.float32
BF = jnp.bfloat16
EPS = 1e-06
ROWS = 512
WIDTH = 768
TILE = 256
CHUNKS = 11
SLOTS = 7
FEATURES = 37
PARTS = (
    ((2, 0, 768),),
    ((0, 0, 768),),
    ((1, 0, 768),),
    ((0, 0, 768),),
    ((1, 0, 768),),
    ((0, 0, 768),),
    ((1, 0, 768),),
    ((0, 0, 384), (1, 384, 768)),
    ((0, 0, 384), (1, 384, 768)),
    ((0, 0, 384), (1, 384, 768)),
    ((3, 0, 384), (4, 384, 768)),
)
Y_FIRST = (0,)
STEPS = [(c, 0, 0) for c in range(CHUNKS)]
STEPS += [(c, s, p) for c in range(CHUNKS) for p, _, _ in PARTS[c] for s in (1, 2, 3)]
STEPS += [(c, 4, 2) for c in Y_FIRST]
STEPS += [(c, 5, p) for c in range(CHUNKS) for p, _, _ in PARTS[c] if p < 2]
MESH = pl.DeviceIdType.MESH


def dot_nn(left, right):
    return lax.dot_general(left, right, (((1,), (0,)), ((), ())), preferred_element_type=F32)


def dot_nt(left, right):
    return lax.dot_general(left, right, (((1,), (1,)), ((), ())), preferred_element_type=F32)


def dot_tn(left, right):
    return lax.dot_general(left, right, (((0,), (0,)), ((), ())), preferred_element_type=F32)


def norm_parts(block):
    centred = block - jnp.mean(block, axis=-1, keepdims=True)
    spread = jnp.mean(centred * centred, axis=-1, keepdims=True)
    inverse = lax.rsqrt(spread + EPS)
    return centred * inverse, inverse


def kernel(
    counts_ref,
    lengths_ref,
    tokens_hbm,
    cot_hbm,
    wi_hbm,
    wo_hbm,
    wu_hbm,
    wd_hbm,
    qb_ref,
    vb_ref,
    ob_ref,
    fg_ref,
    fs_ref,
    sg_ref,
    ss_ref,
    ub_ref,
    db_ref,
    lo_hbm,
    gt_hbm,
    gi_ref,
    gqb_ref,
    gvb_ref,
    go_ref,
    gob_ref,
    gfg_ref,
    gfs_ref,
    gsg_ref,
    gss_ref,
    gu_ref,
    gub_ref,
    gd_ref,
    gdb_ref,
    W,
    CH,
    R0,
    R1,
    R2,
    R3,
    S1,
    S2,
    S3,
    S4,
    FT,
    FDO,
    STAT,
    FSTAT,
    QO,
    KO,
    VO,
    QF,
    KF,
    VF,
    TOK,
    COT,
    ATT,
    SEC,
    ACT,
    DH,
    XT,
    XN,
    RES,
    ACC,
    MF,
    PB,
    TOP,
    SUM,
    VS,
    VR,
    wsem,
    dsem,
    iosem,
    xsend,
    xrecv,
    rsend,
    rrecv,
    vsend,
    vrecv,
):
    ACC1, ACC2 = ACC.at[0], ACC.at[1]
    part = lax.axis_index("seq")
    dp = lax.axis_index("dp")
    y_lo = dp // 32
    z = (dp // 8) % 4
    x = (dp // 2) % 4
    core = dp % 2
    y = 2 * part + y_lo

    def device(yy, zz, xx, cc):
        return (yy // 2, ((yy % 2) * 4 + zz) * 8 + xx * 2 + cc)

    sibling = device(y, z, x, 1 - core)
    z_of = [(z + k) % 4 for k in range(4)]
    x_of = [(x + k) % 4 for k in range(4)]
    y_of = [(y + k) % 4 for k in range(4)]
    z_a, z_b = z + 1 - 2 * (z % 2), 3 - z
    x_a, x_b = x + 1 - 2 * (x % 2), 3 - x
    near_z = [device(y, v, x, core) for v in (z_a, z_b)]
    near_x = [device(y, z, v, core) for v in (x_a, x_b)]
    z_peer = [device(y, v, x, core) for v in z_of]
    x_peer = [device(y, z, v, core) for v in x_of]
    y_peer = [device(v, z, x, core) for v in y_of]
    partner = y_peer[2]

    def load(src, dst, sem):
        copy = pltpu.make_async_copy(src, dst, sem)
        copy.start()
        return copy

    tok_load = load(tokens_hbm, TOK, iosem.at[0])
    w_load = {}
    for i in range(3):
        w_load[i] = load(wi_hbm.at[:, pl.ds(WIDTH * i, WIDTH)], W.at[i], wsem.at[i])
    cot_load = load(cot_hbm, COT, iosem.at[1])
    w_load[3] = load(wo_hbm, W.at[3], wsem.at[3])

    def load_ffn(f):
        slot = f % 2
        up = load(wu_hbm.at[:, pl.ds(WIDTH * f, WIDTH)], W.at[4 + slot], wsem.at[4 + slot])
        down = load(wd_hbm.at[pl.ds(WIDTH * f, WIDTH)], W.at[6 + slot], wsem.at[6 + slot])
        return up, down

    ffn_load = {0: load_ffn(0), 1: load_ffn(1)}
    down_load = [
        load(wd_hbm.at[pl.ds(2 * WIDTH + ROWS * i, ROWS)], ref, dsem.at[i])
        for i, ref in enumerate((SEC, ACT, DH))
    ]

    barrier = pltpu.get_barrier_semaphore()
    for peer in [sibling] + z_peer[1:] + x_peer[1:] + y_peer[1:]:
        pl.semaphore_signal(barrier, inc=1, device_id=peer, device_id_type=MESH)
    pl.semaphore_wait(barrier, 10)

    def remote(src, dst, send, recv, peer):
        copy = pltpu.make_async_remote_copy(
            src_ref=src,
            dst_ref=dst,
            send_sem=send,
            recv_sem=recv,
            device_id=peer,
            device_id_type=MESH,
        )
        copy.start()
        return copy

    far_tokens = remote(tokens_hbm, FT, xsend.at[0], xrecv.at[0], partner)

    def all_bytes(ref, sem):
        pltpu.make_async_copy(ref, ref, sem).wait()

    landing = {}

    def send_all(key, dst, copies):
        i = STEPS.index(key)
        landing[key] = dst
        for src, into, peer in copies:
            remote(src, into, rsend.at[i], rrecv.at[i], peer)

    def received(key):
        all_bytes(landing[key], rrecv.at[STEPS.index(key)])

    def gone(key):
        all_bytes(landing.pop(key), rsend.at[STEPS.index(key)])

    def rs_core(c):
        src = CH.at[c % SLOTS, :, :, :, 1 - core]
        send_all((c, 0, 0), R0.at[c], [(src, R0.at[c], sibling)])

    def row_of(c):
        return c - sum(first < c for first in Y_FIRST)

    def y_slot(c):
        n = Y_FIRST.index(c)
        return n, 384

    def rs_first(c):
        received((c, 0, 0))

        def add(i, carry):
            yl, zz = i // 4, i % 4
            R0[c, yl, zz] = (
                R0[c, yl, zz].astype(F32) + CH[c % SLOTS, yl, zz, :, core].astype(F32)
            ).astype(BF)
            return carry

        lax.fori_loop(0, 8, add, 0)
        for p, lo, hi in PARTS[c]:
            copies = []
            if p == 2:
                n, width = y_slot(c)
                whole = S1.at[n, :, :, :, :, 0:width]
                for k in (2, 1, 3):
                    start = pl.multiple_of(lo + width * (y_of[k] // 2), 128)
                    src = R0.at[c, y_of[k] % 2, :, :, :, pl.ds(start, width)]
                    copies.append((src, S1.at[n, k - 1, :, :, :, 0:width], y_peer[k]))
            elif p > 2:
                whole = R1.at[row_of(c), :, :, :, :, lo:hi]
                for k in (2, 1, 3):
                    if p == 3:
                        src, peer = R0.at[c, :, z_of[k], :, :, lo:hi], z_peer[k]
                    else:
                        src, peer = R0.at[c, :, :, x_of[k], :, lo:hi], x_peer[k]
                    copies.append((src, R1.at[row_of(c), k - 1, :, :, :, lo:hi], peer))
            else:
                whole = R1.at[row_of(c), 0:2, :, :, :, lo:hi]
                a, b = (z_a, z_b) if p == 0 else (x_a, x_b)
                across = 3 - a
                peers = near_z if p == 0 else near_x
                for half, nearest in ((0, a), (1, b)):
                    for spot, wanted in ((1, across), (0, nearest)):
                        dst = R1.at[row_of(c), half, spot, :, :, lo:hi]
                        copies.append((shares(c, p, half, wanted, lo, hi), dst, peers[half]))
            send_all((c, 1, p), whole, copies)

    def shares(c, p, yl, v, lo, hi):
        if p == 0:
            return R0.at[c, yl, v, :, :, lo:hi]
        return R0.at[c, yl, :, v, :, lo:hi]

    def rs_mid(c):
        for p, lo, hi in PARTS[c]:
            if p > 1:
                continue
            received((c, 1, p))
            v, a, b = (z, z_a, z_b) if p == 0 else (x, x_a, x_b)
            for half, other in ((0, b), (1, a)):
                for spot, kept in ((0, v), (1, other)):
                    at = (row_of(c), half, spot, slice(None), slice(None), slice(lo, hi))
                    own = shares(c, p, half, kept, lo, hi)[...]
                    R1[at] = (own.astype(F32) + R1[at].astype(F32)).astype(BF)
            peers = near_z if p == 0 else near_x
            copies = []
            for half in range(2):
                src = R1.at[row_of(c), half, 1, :, :, lo:hi]
                copies.append((src, R1.at[row_of(c), 2, half, :, :, lo:hi], peers[1 - half]))
            send_all((c, 5, p), R1.at[row_of(c), 2, :, :, :, lo:hi], copies)

    def rs_second(c):
        for p, lo, hi in PARTS[c]:
            received((c, 5 if p < 2 else 1, p))
            copies = []
            if p == 2:
                n, width = y_slot(c)
                start = pl.multiple_of(lo + width * part, 128)
                for zz in range(4):
                    total = R0[c, y_lo, zz, :, :, pl.ds(start, width)].astype(F32)
                    for k in range(3):
                        total = total + S1[n, k, zz, :, :, 0:width].astype(F32)
                    S1[n, 0, zz, :, :, 0:width] = total.astype(BF)
                whole = S2.at[n, :, :, :, 0:width]
            elif p > 2:
                for yl in range(2):
                    if p == 3:
                        total = R0[c, yl, z, :, :, lo:hi].astype(F32)
                    else:
                        total = R0[c, yl, :, x, :, lo:hi].astype(F32)
                    for k in range(3):
                        total = total + R1[row_of(c), k, yl, :, :, lo:hi].astype(F32)
                    R1[row_of(c), 0, yl, :, :, lo:hi] = total.astype(BF)
                whole = R2.at[row_of(c), :, :, :, lo:hi]
            else:
                for half in range(2):
                    at = (row_of(c), half, 0, slice(None), slice(None), slice(lo, hi))
                    total = R1[at].astype(F32) + R1[row_of(c), 2, half, :, :, lo:hi].astype(F32)
                    R1[at] = total.astype(BF)
                whole = R2.at[row_of(c), :, :, :, lo:hi]
            for k in (2, 1, 3):
                if p == 3:
                    src = R1.at[row_of(c), 0, :, x_of[k], :, lo:hi]
                    dst, peer = R2.at[row_of(c), k - 1, :, :, lo:hi], x_peer[k]
                elif p == 4:
                    src = R1.at[row_of(c), 0, :, z_of[k], :, lo:hi]
                    dst, peer = R2.at[row_of(c), k - 1, :, :, lo:hi], z_peer[k]
                elif p == 0:
                    src = R1.at[row_of(c), 0:2, 0, x_of[k], :, lo:hi]
                    dst, peer = R2.at[row_of(c), k - 1, :, :, lo:hi], x_peer[k]
                elif p == 1:
                    src = R1.at[row_of(c), 0:2, 0, z_of[k], :, lo:hi]
                    dst, peer = R2.at[row_of(c), k - 1, :, :, lo:hi], z_peer[k]
                else:
                    src = S1.at[n, 0, z_of[k], :, :, 0:width]
                    dst, peer = S2.at[n, k - 1, :, :, 0:width], z_peer[k]
                copies.append((src, dst, peer))
            send_all((c, 2, p), whole, copies)

    def rs_third(c):
        for p, lo, hi in PARTS[c]:
            received((c, 2, p))
            copies = []
            if p == 2:
                n, width = y_slot(c)
                total = S1[n, 0, z, :, :, 0:width].astype(F32)
                for k in range(3):
                    total = total + S2[n, k, :, :, 0:width].astype(F32)
                S2[n, 0, :, :, 0:width] = total.astype(BF)
                whole = S3.at[n, :, :, 0:width]
            else:
                if p == 3:
                    total = R1[row_of(c), 0, :, x, :, lo:hi].astype(F32)
                elif p == 4:
                    total = R1[row_of(c), 0, :, z, :, lo:hi].astype(F32)
                elif p == 0:
                    total = R1[row_of(c), 0:2, 0, x, :, lo:hi].astype(F32)
                else:
                    total = R1[row_of(c), 0:2, 0, z, :, lo:hi].astype(F32)
                for k in range(3):
                    total = total + R2[row_of(c), k, :, :, lo:hi].astype(F32)
                R2[row_of(c), 0, :, :, lo:hi] = total.astype(BF)
                whole = R3.at[row_of(c), :, :, lo:hi]
            for k in (2, 1, 3):
                if p == 2:
                    src = S2.at[n, 0, x_of[k], :, 0:width]
                    dst, peer = S3.at[n, k - 1, :, 0:width], x_peer[k]
                else:
                    src = R2.at[row_of(c), 0, y_of[k] % 2, :, lo:hi]
                    dst, peer = R3.at[row_of(c), k - 1, :, lo:hi], y_peer[k]
                copies.append((src, dst, peer))
            send_all((c, 3, p), whole, copies)

    def store_share(c, lo, hi, total):
        if c < 4:
            gu_ref[:, WIDTH * c + lo : WIDTH * c + hi] = total[0:12]
        elif c < 7:
            gd_ref[16 * (c - 4) : 16 * (c - 3), lo:hi] = total
        elif c == 7:
            go_ref[:, lo:hi] = total[0:12]
        else:
            for b in range(lo // 384, hi // 384):
                start = 384 * b if c == 8 else WIDTH * (b + 1) + 384 * (c - 9)
                gi_ref[:, start : start + 384] = total[0:12, 384 * b - lo : 384 * (b + 1) - lo]

    def rs_fourth(c):
        for p, lo, hi in PARTS[c]:
            received((c, 3, p))
            if p == 2:
                n, width = y_slot(c)
                total = S2[n, 0, x, :, 0:width].astype(F32)
                for k in range(3):
                    total = total + S3[n, k, :, 0:width].astype(F32)
                S4[n, 0, :, 0:width] = total
                dst = S4.at[n, 1, :, 0:width]
                send_all((c, 4, p), dst, [(S4.at[n, 0, :, 0:width], dst, partner)])
            else:
                total = (R2[row_of(c), 0, y_lo, :, lo:hi].astype(F32) + R3[row_of(c), 1, :, lo:hi].astype(F32)) + (
                    R3[row_of(c), 0, :, lo:hi].astype(F32) + R3[row_of(c), 2, :, lo:hi].astype(F32)
                )
                store_share(c, lo, hi, total)

    def rs_end(c):
        n, width = y_slot(c)
        received((c, 4, 2))
        mine = S4[n, 0, :, 0:width]
        other = S4[n, 1, :, 0:width]
        low = jnp.where(part == 0, mine, other)
        high = jnp.where(part == 0, other, mine)
        lo = PARTS[c][-1][1]
        store_share(c, lo, lo + 2 * width, jnp.concatenate([low, high], axis=1))

    counts0 = counts_ref[0, 0]
    counts1 = counts_ref[0, 1]
    end0 = lengths_ref[0, 0]
    end1 = end0 + lengths_ref[0, 1]
    end2 = end1 + lengths_ref[0, 2]
    end3 = end2 + lengths_ref[0, 3]

    def used_rows(start, size, width):
        place = lax.broadcasted_iota(jnp.int32, (size, width), 0) + start
        return place < counts0 + part * (counts1 - counts0)

    def features(base, which):
        place = lax.broadcasted_iota(jnp.int32, (ROWS, 128), 0)
        shifted = place + which * counts0
        index = jnp.zeros((ROWS, 128), jnp.int32)
        for end in (end0, end1, end2, end3):
            index = index + jnp.where(end <= shifted, 1, 0)
        owned = counts0 + which * (counts1 - counts0)
        ids = jnp.where(place < owned, index, 4 + which * ROWS + place)
        lane = lax.broadcasted_iota(jnp.int32, (ROWS, 128), 1)
        high = lane >= 64
        spot = jnp.where(high, lane - 64, lane)
        digit = jnp.where(
            spot < 16, ids & 15, jnp.where(spot < 32, ((ids >> 4) & 15) + 16, (ids >> 8) + 32)
        )
        hot = jnp.where(digit == spot, 1.0, 0.0)
        query = jnp.where(spot < FEATURES, 1.0 - hot, 0.0)
        key = hot * -1e30
        MF[base] = jnp.where(high, query, 0.0).astype(BF)
        MF[base + 1] = jnp.where(high, 0.0, query).astype(BF)
        MF[base + 2] = jnp.where(high, key, 0.0).astype(BF)
        MF[base + 3] = jnp.where(high, 0.0, key).astype(BF)

    features(0, part)
    features(4, 1 - part)
    lane_row = lax.broadcasted_iota(jnp.int32, (1, 128), 1)
    select = [
        jnp.where(lane_row < 64, 1.0, 0.0).astype(BF),
        jnp.where(lane_row < 64, 0.0, 1.0).astype(BF),
    ]

    rho = lax.broadcasted_iota(jnp.int32, (ROWS, 384), 0)
    feature = lax.broadcasted_iota(jnp.int32, (ROWS, 384), 1)
    within = rho & 15
    PB[...] = jnp.where(
        (within < 12) & (feature == (rho >> 4) * 12 + within), 1.0, 0.0
    ).astype(BF)

    def padded_transpose(source, into):
        for b in range(2):
            into[ROWS * b : ROWS * (b + 1), :] = dot_nt(
                PB[...], source[:, 384 * b : 384 * (b + 1)]
            ).astype(BF)

    def chunk_matmul(c, right):
        left = XT if c < 8 else XN

        def block(m, carry):
            cols = pl.ds(pl.multiple_of(m * TILE, TILE), TILE)
            out = dot_nn(left[...], right[:, cols]).astype(BF)
            CH[c % SLOTS, :, :, :, :, :, cols] = out.reshape(2, 4, 4, 2, 16, TILE)
            return carry

        lax.fori_loop(0, 3, block, 0)

    ones = jnp.ones((16, ROWS), BF)

    def row_sum(block):
        return dot_nn(ones, block)[0:1]

    def tiles(step):
        def run(t, carry):
            step(pl.ds(pl.multiple_of(t * TILE, TILE), TILE), t * TILE)
            return carry

        lax.fori_loop(0, ROWS // TILE, run, 0)

    qb = qb_ref[...].reshape(1, WIDTH)
    vb = vb_ref[...].reshape(1, WIDTH)
    ob = ob_ref[...].reshape(1, WIDTH)
    fg = fg_ref[...].reshape(1, WIDTH)
    fs = fs_ref[...].reshape(1, WIDTH)
    sg = sg_ref[...].reshape(1, WIDTH)
    ss = ss_ref[...].reshape(1, WIDTH)
    db = db_ref[...].reshape(1, WIDTH)

    def projection(source, q_ref, k_ref, v_ref):
        def step(rows, start):
            unit, _ = norm_parts(source[rows, :].astype(F32))
            normed = (unit * fg + fs).astype(BF)
            q = (dot_nn(normed, W[0]) + qb).astype(BF)
            q_ref[rows, :] = q * jnp.asarray(0.125, BF)
            k_ref[rows, :] = dot_nn(normed, W[1]).astype(BF)
            v_ref[rows, :] = (dot_nn(normed, W[2]) + vb).astype(BF)

        return step

    tok_load.wait()
    for i in range(3):
        w_load[i].wait()
    tiles(projection(TOK, QO, KO, VO))

    cot_load.wait()

    def mask_cot(rows, start):
        used = used_rows(start, TILE, WIDTH)
        COT[rows, :] = jnp.where(used, COT[rows, :].astype(F32), 0.0).astype(BF)

    tiles(mask_cot)

    def pair_cols(hp):
        return pl.ds(pl.multiple_of(hp * 128, 128), 128)

    def mix_at(hp, h):
        start = pl.multiple_of(128 * (hp % 4) + 64 * h, 64)
        return hp // 4, pl.ds(start, 64), slice(0, ROWS)

    def attend_own(hp, carry):
        cols = pair_cols(hp)
        q = QO[:, cols]
        keys = KO[:, cols]
        values = VO[:, cols].T
        for h in range(2):
            row = pl.ds(2 * hp + h, 1)
            scores = dot_nt(keys * select[h] + MF[2 + h], q * select[h] + MF[h])
            top = jnp.max(scores, axis=0, keepdims=True)
            probs = jnp.exp(scores - top)
            TOP[row, :] = top
            SUM[row, :] = jnp.sum(probs, axis=0, keepdims=True)
            own = slice(64 * h, 64 * h + 64)
            ACC[mix_at(hp, h)] = dot_nn(values[own], probs.astype(BF))
        return carry

    lax.fori_loop(0, 6, attend_own, 0)

    def attend_far(hp, carry):
        cols = pair_cols(hp)
        q = QO[:, cols]
        keys = KF[:, cols]
        values = VF[:, cols].T
        outs = []
        for h in range(2):
            row = pl.ds(2 * hp + h, 1)
            own = slice(64 * h, 64 * h + 64)
            scores = dot_nt(keys * select[h] + MF[6 + h], q * select[h] + MF[h])
            before = TOP[row, :]
            top = jnp.maximum(before, jnp.max(scores, axis=0, keepdims=True))
            shrink = jnp.exp(before - top)
            probs = jnp.exp(scores - top)
            total = SUM[row, :] * shrink + jnp.sum(probs, axis=0, keepdims=True)
            mixed = ACC[mix_at(hp, h)] * shrink + dot_nn(values[own], probs.astype(BF))
            STAT[0, row, :] = top + jnp.log(total)
            outs.append(mixed * (1.0 / total))
        ATT[:, cols] = jnp.concatenate(outs, axis=0).T.astype(BF)
        return carry

    def again(rows, start):
        unit, _ = norm_parts(TOK[rows, :].astype(F32))
        ATT[rows, :] = (unit * fg + fs).astype(BF)

    tiles(again)
    padded_transpose(ATT, XN)

    for copy in down_load:
        copy.wait()
    for f in range(2):
        ffn_load[f][1].wait()

    def early_step(rows, start):
        dout = COT[rows, :]
        block = start // TILE * 2

        def keep(f, lo, value):
            CH[f, 0, pl.ds(block, 2), :, :, :, lo : lo + value.shape[1]] = value.astype(BF).reshape(
                2, 4, 2, 16, value.shape[1]
            )

        for f in range(2):
            keep(f, 0, dot_nt(dout, W[6 + f]))
        keep(2, 0, dot_nt(dout, SEC[...]))
        middle = dot_nt(dout, ACT[...])
        keep(2, 512, middle[:, 0:256])
        keep(3, 0, middle[:, 256:512])
        keep(3, 256, dot_nt(dout, DH[...]))

    tiles(early_step)

    far_tokens.wait_recv()
    tiles(projection(FT, QF, KF, VF))
    lax.fori_loop(0, 6, attend_far, 0)

    w_load[3].wait()

    def out_step(rows, start):
        res = TOK[rows, :].astype(F32) + dot_nn(ATT[rows, :], W[3]) + ob
        RES[rows, :] = res
        unit, _ = norm_parts(res)
        SEC[rows, :] = (unit * sg + ss).astype(BF)
        ACC1[rows, :] = jnp.zeros((TILE, WIDTH), F32)
        ACC2[rows, :] = jnp.zeros((TILE, WIDTH), F32)

    tiles(out_step)
    padded_transpose(SEC, XT)
    VS[0] = jnp.zeros((16, WIDTH), F32)

    for f in range(4):
        slot = f % 2
        ffn_load[f][0].wait()
        if f > 1:
            ffn_load[f][1].wait()
        ub = ub_ref[WIDTH * f : WIDTH * (f + 1)].reshape(1, WIDTH)

        def ffn_step(rows, start, f=f, slot=slot, ub=ub):
            early = CH[f, 0, pl.ds(start // TILE * 2, 2)].reshape(TILE, WIDTH).astype(F32)
            hidden = dot_nn(SEC[rows, :], W[4 + slot]) + ub
            cdf = 0.5 * (1.0 + lax.erf(hidden * 0.7071067811865476))
            density = jnp.exp(-0.5 * hidden * hidden) * 0.3989422804014327
            active = (hidden * cdf).astype(BF)
            ACT[rows, :] = active
            dhidden = (early * (cdf + hidden * density)).astype(BF)
            DH[rows, :] = dhidden
            ACC1[rows, :] += dot_nn(active, W[6 + slot])
            ACC2[rows, :] += dot_nt(dhidden, W[4 + slot])

        tiles(ffn_step)
        if f + 2 < 4:
            ffn_load[f + 2] = load_ffn(f + 2)
        if f >= 1:
            rs_first(f - 1)
        chunk_matmul(f, DH)
        rs_core(f)
        VS[0, 8 + f : 9 + f, :] = row_sum(DH[...])

        def down_step(b, carry, f=f):
            cols = pl.ds(pl.multiple_of(b * 384, 384), 384)
            out = dot_tn(ACT[:, cols], COT[...]).astype(BF).reshape(4, 2, 3, 16, WIDTH)
            for k in range(3):
                CH[4 + k, f // 2, 2 * (f % 2) + b] = out[:, :, k]
            return carry

        lax.fori_loop(0, 2, down_step, 0)
    for k in range(3):
        rs_core(4 + k)

    def second_back(rows, start):
        res = RES[rows, :]
        used = used_rows(start, TILE, WIDTH)
        FT[rows, :] = jnp.where(used, res + ACC1[rows, :] + db, 0.0).astype(BF)
        unit, inverse = norm_parts(res)
        dsecond = ACC2[rows, :]
        VS[0, 5:6, :] += jnp.sum(dsecond * unit, axis=0, keepdims=True)
        VS[0, 6:7, :] += jnp.sum(dsecond, axis=0, keepdims=True)
        g = dsecond * sg
        through = (
            g
            - jnp.mean(g, axis=-1, keepdims=True)
            - unit * jnp.mean(g * unit, axis=-1, keepdims=True)
        ) * inverse
        dres = COT[rows, :].astype(F32) + through
        RES[rows, :] = dres
        SEC[rows, :] = dres.astype(BF)
        DH[rows, :] = dot_nt(dres.astype(BF), W[3]).astype(BF)

    tiles(second_back)
    lo_store = load(FT, lo_hbm, iosem.at[2])
    far_dout = []
    for r in range(2):
        half = pl.ds(384 * r, 384)
        far_dout.append(
            remote(DH.at[:, half], FDO.at[:, half], xsend.at[2 + r], xrecv.at[2 + r], partner)
        )
    rs_first(3)
    VS[0, 7:8, :] = row_sum(COT[...])
    VS[0, 2:3, :] = row_sum(SEC[...])

    head = lax.broadcasted_iota(jnp.int32, (16, WIDTH), 0)
    column = lax.broadcasted_iota(jnp.int32, (16, WIDTH), 1)
    in_head = jnp.where((column >> 6) == head, 1.0, 0.0).astype(BF)
    product = DH[...].astype(F32) * ATT[...].astype(F32)
    rough = product.astype(BF)
    STAT[1] = dot_nt(in_head, rough) + dot_nt(in_head, (product - rough.astype(F32)).astype(BF))
    far_stats = remote(STAT, FSTAT, xsend.at[4], xrecv.at[4], partner)

    padded_transpose(ATT, XT)
    gone((0, 0, 0))
    chunk_matmul(7, SEC)
    rs_core(7)
    rs_first(4)
    rs_first(5)
    rs_mid(1)

    def own_queries(hp, carry):
        cols = pair_cols(hp)
        q = QO[:, cols]
        ko = KO[:, cols]
        kf = KF[:, cols]
        vo = VO[:, cols]
        vf = VF[:, cols]
        do = DH[:, cols]
        ko_t = ko.T
        kf_t = kf.T
        dq = []
        dk = None
        for h in range(2):
            logsum = STAT[0, pl.ds(2 * hp + h, 1), :]
            delta = STAT[1, pl.ds(2 * hp + h, 1), :]
            qm = q * select[h] + MF[h]
            qs = q * select[h]
            dom = do * select[h]
            near = jnp.exp(dot_nt(ko * select[h] + MF[2 + h], qm) - logsum)
            dnear = (near * (dot_nt(vo, dom) - delta)).astype(BF)
            far = jnp.exp(dot_nt(kf * select[h] + MF[6 + h], qm) - logsum)
            dfar = (far * (dot_nt(vf, dom) - delta)).astype(BF)
            dq.append(
                dot_nn(ko_t[64 * h : 64 * h + 64], dnear)
                + dot_nn(kf_t[64 * h : 64 * h + 64], dfar)
            )
            dk_h = dot_nn(dnear, qs)
            dv_h = dot_nn(near.astype(BF), dom)
            dk, dv = (dk_h, dv_h) if dk is None else (dk + dk_h, dv + dv_h)
        ACC1[:, cols] = dk
        ACC2[:, cols] = dv
        QO[:, cols] = (jnp.concatenate(dq, axis=0).T * 0.125).astype(BF)
        return carry

    lax.fori_loop(0, 2, own_queries, 0)
    rs_first(6)
    rs_mid(2)
    rs_second(0)
    lax.fori_loop(2, 4, own_queries, 0)
    rs_first(7)
    rs_mid(3)
    rs_second(1)
    rs_mid(4)
    lax.fori_loop(4, 6, own_queries, 0)
    rs_mid(5)
    rs_second(2)
    rs_third(0)

    def again(rows, start):
        unit, _ = norm_parts(TOK[rows, :].astype(F32))
        ATT[rows, :] = (unit * fg + fs).astype(BF)


    gone((1, 0, 0))
    chunk_matmul(8, QO)
    rs_core(8)
    rs_mid(6)
    rs_second(3)
    rs_third(1)

    far_stats.wait_recv()

    def far_queries(hp, carry):
        cols = pair_cols(hp)
        q = QF[:, cols]
        ko = KO[:, cols]
        vo = VO[:, cols]
        do = FDO[:, cols]
        dk = ACC1[:, cols]
        dv = ACC2[:, cols]
        for h in range(2):
            logsum = FSTAT[0, pl.ds(2 * hp + h, 1), :]
            delta = FSTAT[1, pl.ds(2 * hp + h, 1), :]
            qs = q * select[h]
            dom = do * select[h]
            probs = jnp.exp(dot_nt(ko * select[h] + MF[2 + h], qs + MF[4 + h]) - logsum)
            dscores = (probs * (dot_nt(vo, dom) - delta)).astype(BF)
            dk = dk + dot_nn(dscores, qs)
            dv = dv + dot_nn(probs.astype(BF), dom)
        KO[:, cols] = dk.astype(BF)
        VO[:, cols] = dv.astype(BF)
        return carry

    def chunk_in(c):
        cols = slice(384 * (c - 9), 384 * (c - 8))
        ACT[:, 0:384] = KO[:, cols]
        ACT[:, 384:768] = VO[:, cols]
        gone((c - 7, 0, 0))
        chunk_matmul(c, ACT)
        rs_core(c)

    far_dout[0].wait_recv()
    lax.fori_loop(0, 3, far_queries, 0)
    chunk_in(9)
    rs_first(8)
    rs_mid(7)
    rs_second(4)
    rs_second(5)
    rs_third(2)
    rs_third(3)
    rs_fourth(0)
    far_dout[1].wait_recv()
    lax.fori_loop(3, 4, far_queries, 0)
    rs_first(9)
    lax.fori_loop(4, 6, far_queries, 0)
    chunk_in(10)
    rs_mid(8)
    rs_second(6)
    rs_second(7)
    rs_third(4)
    rs_third(5)
    rs_fourth(1)
    rs_fourth(2)
    rs_fourth(3)
    rs_mid(9)

    VS[0, 0:1, :] = row_sum(QO[...])
    VS[0, 1:2, :] = row_sum(VO[...])

    def first_back(rows, start):
        unit, inverse = norm_parts(TOK[rows, :].astype(F32))
        dnormed = (
            dot_nt(QO[rows, :], W[0]) + dot_nt(KO[rows, :], W[1]) + dot_nt(VO[rows, :], W[2])
        )
        VS[0, 3:4, :] += jnp.sum(dnormed * unit, axis=0, keepdims=True)
        VS[0, 4:5, :] += jnp.sum(dnormed, axis=0, keepdims=True)
        g = dnormed * fg
        through = (
            g
            - jnp.mean(g, axis=-1, keepdims=True)
            - unit * jnp.mean(g * unit, axis=-1, keepdims=True)
        ) * inverse
        TOK[rows, :] = (RES[rows, :] + through).astype(BF)

    far_tokens.wait_send()
    tiles(first_back)
    gt_store = load(TOK, gt_hbm, iosem.at[3])

    def vec_send(step, peers):
        base = (0, 1, 4, 7)[step]
        for i, peer in enumerate(peers):
            remote(VS.at[step], VR.at[base + i], vsend.at[step], vrecv.at[step], peer)

    def vec_add(step):
        base = (0, 1, 4, 7)[step]
        if step == 0:
            all_bytes(VR.at[0:1], vrecv.at[0])
            total = VS[0] + VR[0]
        else:
            all_bytes(VR.at[base : base + 3], vrecv.at[step])
            total = (VS[step] + VR[base + 1]) + (VR[base] + VR[base + 2])
        VS[step + 1] = total

    vec_send(0, [sibling])
    rs_first(10)
    rs_second(8)
    rs_third(6)
    rs_third(7)
    rs_fourth(4)
    rs_fourth(5)
    vec_add(0)
    vec_send(1, z_peer[1:])
    rs_mid(10)
    rs_second(9)
    rs_third(8)
    rs_fourth(6)
    rs_second(10)
    vec_add(1)
    vec_send(2, x_peer[1:])
    rs_third(9)
    rs_fourth(7)
    rs_fourth(8)
    rs_third(10)
    vec_add(2)
    vec_send(3, y_peer[1:])
    rs_end(0)
    rs_fourth(9)
    rs_fourth(10)
    vec_add(3)

    vectors = VS[4]
    small = pltpu.roll(vectors, (WIDTH - 12 * dp) % WIDTH, 1)
    large = pltpu.roll(vectors, (WIDTH - 48 * (dp % 16)) % WIDTH, 1)[:, 0:128]
    row = lax.broadcasted_iota(jnp.int32, (16, 128), 0)
    large = jnp.sum(jnp.where(row == 8 + dp // 16, large, 0.0), axis=0, keepdims=True)
    for i, ref in enumerate(
        (gqb_ref, gvb_ref, gob_ref, gfg_ref, gfs_ref, gsg_ref, gss_ref, gdb_ref)
    ):
        ref[...] = small[i : i + 1, 0:12].reshape(12)
    gub_ref[...] = large[:, 0:48].reshape(48)

    for copy in far_dout:
        copy.wait_send()
    far_stats.wait_send()
    for key in list(landing):
        gone(key)
    all_bytes(VR.at[0:1], vsend.at[0])
    for step in range(1, 4):
        all_bytes(VR.at[3 * step - 2 : 3 * step + 1], vsend.at[step])
    lo_store.wait()
    gt_store.wait()


def finish(*refs):
    count = (len(refs) - 2) // 3
    sems = refs[3 * count :]
    hops = []
    for i in range(count):
        src, dst, held = refs[i], refs[count + i], refs[2 * count + i]
        hops.append(
            (
                pltpu.make_async_copy(src, held, sems[0].at[i]),
                pltpu.make_async_copy(held, dst, sems[1].at[i]),
            )
        )
    for first, _ in hops:
        first.start()
    for first, second in hops:
        first.wait()
        second.start()
    for _, second in hops:
        second.wait()


def body(
    tokens,
    input_weight,
    query_bias,
    value_bias,
    out_weight,
    out_bias,
    first_gain,
    first_shift,
    second_gain,
    second_shift,
    up_weight,
    up_bias,
    down_weight,
    down_bias,
    cotangent,
    row_counts,
    image_lengths,
):
    hbm = pl.BlockSpec(memory_space=pl.ANY)
    vmem = pl.BlockSpec(memory_space=pltpu.VMEM)
    smem = pl.BlockSpec(memory_space=pltpu.SMEM)
    rows = jax.ShapeDtypeStruct((ROWS, WIDTH), BF)

    def f32(*shape):
        return jax.ShapeDtypeStruct(shape, F32)

    def block(kind, *lead):
        return pltpu.VMEM((*lead, ROWS, WIDTH), kind)

    out = pl.pallas_call(
        kernel,
        out_shape=(
            rows,
            rows,
            f32(12, 3 * WIDTH),
            f32(12),
            f32(12),
            f32(12, WIDTH),
            f32(12),
            f32(12),
            f32(12),
            f32(12),
            f32(12),
            f32(12, 4 * WIDTH),
            f32(48),
            f32(48, WIDTH),
            f32(12),
        ),
        in_specs=[smem, smem] + [hbm] * 6 + [vmem] * 9,
        out_specs=(hbm, hbm) + (vmem,) * 13,
        scratch_shapes=[
            pltpu.VMEM((8, WIDTH, WIDTH), BF),
            pltpu.VMEM((SLOTS, 2, 4, 4, 2, 16, WIDTH), BF),
            pltpu.VMEM((CHUNKS, 2, 4, 4, 16, WIDTH), BF),
            pltpu.VMEM((CHUNKS - len(Y_FIRST), 3, 2, 4, 16, WIDTH), BF),
            pltpu.VMEM((CHUNKS - len(Y_FIRST), 3, 2, 16, WIDTH), BF),
            pltpu.VMEM((CHUNKS - len(Y_FIRST), 3, 16, WIDTH), BF),
            pltpu.VMEM((1, 3, 4, 4, 16, 384), BF),
            pltpu.VMEM((1, 3, 4, 16, 384), BF),
            pltpu.VMEM((1, 3, 16, 384), BF),
            pltpu.VMEM((1, 2, 16, 384), F32),
            block(BF),
            block(BF),
            pltpu.VMEM((2, 16, ROWS), F32),
            pltpu.VMEM((2, 16, ROWS), F32),
        ]
        + [block(BF)] * 12
        + [
            pltpu.VMEM((1024, ROWS), BF),
            pltpu.VMEM((1024, ROWS), BF),
            block(F32),
            block(F32, 2),
            pltpu.VMEM((8, ROWS, 128), BF),
            pltpu.VMEM((ROWS, 384), BF),
            pltpu.VMEM((16, ROWS), F32),
            pltpu.VMEM((16, ROWS), F32),
            pltpu.VMEM((5, 16, WIDTH), F32),
            pltpu.VMEM((10, 16, WIDTH), F32),
            pltpu.SemaphoreType.DMA((8,)),
            pltpu.SemaphoreType.DMA((3,)),
            pltpu.SemaphoreType.DMA((4,)),
            pltpu.SemaphoreType.DMA((5,)),
            pltpu.SemaphoreType.DMA((5,)),
            pltpu.SemaphoreType.DMA((len(STEPS),)),
            pltpu.SemaphoreType.DMA((len(STEPS),)),
            pltpu.SemaphoreType.DMA((4,)),
            pltpu.SemaphoreType.DMA((4,)),
        ],
        compiler_params=pltpu.CompilerParams(
            collective_id=0, has_side_effects=True, vmem_limit_bytes=63 * 2**20
        ),
        name="encoder",
    )(
        row_counts,
        image_lengths,
        tokens,
        cotangent,
        input_weight,
        out_weight,
        up_weight,
        down_weight,
        query_bias,
        value_bias,
        out_bias,
        first_gain,
        first_shift,
        second_gain,
        second_shift,
        up_bias,
        down_bias,
    )
    return pl.pallas_call(
        finish,
        out_shape=tuple(jax.ShapeDtypeStruct(value.shape, value.dtype) for value in out),
        in_specs=[hbm] * len(out),
        out_specs=(hbm,) * len(out),
        scratch_shapes=[pltpu.VMEM(value.shape, value.dtype) for value in out]
        + [pltpu.SemaphoreType.DMA((len(out),))] * 2,
        name="finish",
    )(*out)


def solution(mesh):
    rows = P(("seq", "dp"), None)
    split = P("dp", None)
    line = P("dp")
    return jax.shard_map(
        body,
        mesh=mesh,
        in_specs=(rows,) + (P(),) * 13 + (rows, split, split),
        out_specs=(
            rows,
            rows,
            split,
            line,
            line,
            split,
            line,
            line,
            line,
            line,
            line,
            split,
            line,
            split,
            line,
        ),
        check_vma=False,
    )
```
